32 devices in a mesh: dp: 2 (over x), seq: 8 (over z, y), mp: 2 (over core).
Axes of the slice: x: 2, y: 2, z: 4, core: 2. Of those that a mesh axis runs over, the one named last changes fastest.
Arguments:
- tokens: bfloat16 [4, 2048, 512], P('dp', ('seq', 'mp')), may hold values from -6 to 6
- segments: int32 [4, 2048], P('dp', ('seq', 'mp')), may hold values from 0 to 16, as said below
- timesteps: int32 [4], P('dp'), may hold values from 0 to 999
- step_table: bfloat16 [1000, 512], replicated, may hold values from -3 to 3
- first_gain: float32 [512], replicated, may hold values from 0.5 to 1.5
- first_shift: float32 [512], replicated, may hold values from -3 to 3
- query_weight: bfloat16 [512, 512], P(None, 'mp'), may hold values from -0.25 to 0.25
- query_bias: bfloat16 [512], P('mp'), may hold values from -3 to 3
- key_weight: bfloat16 [512, 512], P(None, 'mp'), may hold values from -0.25 to 0.25
- value_weight: bfloat16 [512, 512], P(None, 'mp'), may hold values from -0.25 to 0.25
- value_bias: bfloat16 [512], P('mp'), may hold values from -3 to 3
- out_weight: bfloat16 [512, 512], P('mp'), may hold values from -2 to 2
- out_bias: bfloat16 [512], replicated, may hold values from -3 to 3
- second_gain: float32 [512], replicated, may hold values from 0.5 to 1.5
- second_shift: float32 [512], replicated, may hold values from -3 to 3
- up_weight: bfloat16 [512, 2048], P(None, 'mp'), may hold values from -0.25 to 0.25
- up_bias: bfloat16 [2048], P('mp'), may hold values from -3 to 3
- down_weight: bfloat16 [2048, 512], P('mp'), may hold values from -0.25 to 0.25
- down_bias: bfloat16 [512], replicated, may hold values from -3 to 3
- cotangent: bfloat16 [4, 2048, 512], P('dp', ('seq', 'mp')), may hold values from -6 to 6
Outputs:
- result: bfloat16 [4, 2048, 512], P('dp', ('seq', 'mp'))
- token_grad: float32 [4, 2048, 512], P('dp', ('seq', 'mp'))
- table_grad: float32 [1000, 512], replicated
- first_gain_grad: float32 [512], replicated
- first_shift_grad: float32 [512], replicated
- query_weight_grad: float32 [512, 512], P(None, 'mp')
- query_bias_grad: float32 [512], P('mp')
- key_weight_grad: float32 [512, 512], P(None, 'mp')
- value_weight_grad: float32 [512, 512], P(None, 'mp')
- value_bias_grad: float32 [512], P('mp')
- out_weight_grad: float32 [512, 512], P('mp')
- out_bias_grad: float32 [512], replicated
- second_gain_grad: float32 [512], replicated
- second_shift_grad: float32 [512], replicated
- up_weight_grad: float32 [512, 2048], P(None, 'mp')
- up_bias_grad: float32 [2048], P('mp')
- down_weight_grad: float32 [2048, 512], P('mp')
- down_bias_grad: float32 [512], replicated
The draws below stay inside these ranges and needn't reach their ends.
Inputs may be any that keep to these rules, and one draw needn't show every extreme that they name: `segments`: along each row the ids never fall before the padding; 0 marks padding, which fills the last 32 to 128 characters of every row and nothing else.
All inputs are finite; a program needn't handle non-finite values.
Results may differ from the reference program's by a relative error of at most 0.03.
Values may be sent and summed in bfloat16 or wider, within the bound.
A program may use at most 128 MiB of HBM per device.

```python
import math
import jax
import jax.numpy as jnp
from jax import lax

D = 512
HEADS = 8
HEAD_DIM = 64
FF = 2048
TSTEPS = 1000
ROWS_DEV = 2
BOUNDS = 15
ROWS = 4
LENGTH = 2048
N_DP = 2
N_SEQ = 8


def draw_segments(key, part):
    key = jax.random.fold_in(key, 11)
    first, second, third, fourth = jax.random.split(key, 4)
    padding = jax.random.randint(first, (ROWS,), LENGTH // 64, LENGTH // 16 + 1)
    filled = LENGTH - padding
    spread_cuts = jax.random.randint(second, (ROWS, BOUNDS), 1, LENGTH * 7 // 8)
    early_cuts = jax.random.randint(third, (ROWS, BOUNDS), 1, LENGTH // (2 * N_SEQ))
    picked = jax.random.randint(fourth, (N_DP,), 0, ROWS_DEV)
    row_ids = jnp.arange(ROWS, dtype=jnp.int32)
    chosen = row_ids % ROWS_DEV == picked[row_ids // ROWS_DEV]
    cuts = jnp.where(chosen[:, None], early_cuts, spread_cuts)
    places = jnp.arange(LENGTH, dtype=jnp.int32)
    span_ids = 1 + jnp.sum((cuts[:, None, :] <= places[None, :, None]).astype(jnp.int32), axis=2)
    return jnp.where(places[None, :] < filled[:, None], span_ids, 0).astype(jnp.int32)


def plant(drawn, rng, low, largest):
    index_at = [jax.random.randint(jax.random.fold_in(rng, axis), (), 0, length) for axis, length in enumerate(drawn.shape)]
    longest = drawn.shape.index(max(drawn.shape))
    beside = index_at[:longest] + [(index_at[longest] + 1) % drawn.shape[longest]] + index_at[longest + 1:]
    return drawn.at[tuple(index_at)].set(low).at[tuple(beside)].set(largest)


def shard_levels(own_key, dims, shards, least, largest):
    def one(dim, blocks):
        heights = jax.random.uniform(jax.random.fold_in(jax.random.fold_in(own_key, 6), dim), (blocks,), jnp.float32, least / len(shards), largest / len(shards))
        return jnp.repeat(jnp.exp(heights), dims[dim] // blocks).reshape((-1,) + (1,) * (len(dims) - dim - 1))

    level = one(*shards[0])
    for cut in shards[1:]:
        level = level * one(*cut)
    return level


def scatter_about(key, shape, width, bound, shards=(), kind=jnp.bfloat16):
    values = jax.random.normal(key, shape, jnp.float32) * width
    if len(shards) > 0:
        values = shard_levels(key, shape, shards, -0.22, 0.18) * values
    return jnp.clip(values, min=-bound, max=bound).astype(kind)


def setup_inputs(seed: int = 0) -> dict:
    seeds = jax.random.split(jax.random.key(seed), 21)
    tokens = scatter_about(seeds[0], (ROWS, LENGTH, D), 1.0, 6.0, ((0, 2), (1, 16)))
    segments = draw_segments(jax.random.fold_in(seeds[20], 71), 0)
    timesteps = plant(jax.random.randint(seeds[2], (ROWS,), 0, TSTEPS), jax.random.fold_in(seeds[2], 1), 0, TSTEPS - 1).astype(jnp.int32)
    step_table = scatter_about(seeds[3], (TSTEPS, D), 0.5, 3.0)
    first_gain = jnp.clip(1.0 + 0.1 * jax.random.normal(seeds[4], (D,), jnp.float32), 0.5, 1.5)
    first_shift = scatter_about(seeds[5], (D,), 0.3, 3.0, (), jnp.float32)
    query_weight = scatter_about(seeds[6], (D, D), D ** -0.5, 0.25, ((1, 2),))
    query_bias = scatter_about(seeds[7], (D,), 0.3, 3.0, ((0, 2),))
    key_weight = scatter_about(seeds[8], (D, D), D ** -0.5, 0.25, ((1, 2),))
    value_weight = scatter_about(seeds[9], (D, D), D ** -0.5, 0.25, ((1, 2),))
    value_bias = scatter_about(seeds[10], (D,), 0.3, 3.0, ((0, 2),))
    out_weight = scatter_about(seeds[11], (D, D), (D // 64) ** -0.5, 2.0, ((0, 2),))
    out_bias = scatter_about(seeds[12], (D,), 0.3, 3.0)
    second_gain = jnp.clip(1.0 + 0.1 * jax.random.normal(seeds[13], (D,), jnp.float32), 0.5, 1.5)
    second_shift = scatter_about(seeds[14], (D,), 0.3, 3.0, (), jnp.float32)
    up_weight = scatter_about(seeds[15], (D, FF), D ** -0.5, 0.25, ((1, 2),))
    up_bias = scatter_about(seeds[16], (FF,), 0.3, 3.0, ((0, 2),))
    down_weight = scatter_about(seeds[17], (FF, D), (FF // 4) ** -0.5, 0.25, ((0, 2),))
    down_bias = scatter_about(seeds[18], (D,), 0.3, 3.0)
    cotangent = scatter_about(seeds[19], (ROWS, LENGTH, D), 1.0, 6.0, ((0, 2), (1, 16)))
    return dict(tokens=tokens, segments=segments, timesteps=timesteps, step_table=step_table, first_gain=first_gain, first_shift=first_shift, query_weight=query_weight, query_bias=query_bias, key_weight=key_weight, value_weight=value_weight, value_bias=value_bias, out_weight=out_weight, out_bias=out_bias, second_gain=second_gain, second_shift=second_shift, up_weight=up_weight, up_bias=up_bias, down_weight=down_weight, down_bias=down_bias, cotangent=cotangent)


highest = lax.Precision.HIGHEST
masked = -1e+30

@jax.custom_vjp
def low(v):
    return lax.optimization_barrier(v.astype(jnp.bfloat16)).astype(jnp.float32)

@jax.custom_vjp
def low_back(v):
    return v

def low_keep(v):
    return (low(v), None)

def low_pass(kept, grad):
    return (grad,)

def back_keep(v):
    return (v, None)

def back_low(kept, grad):
    return (low(grad),)
low.defvjp(low_keep, low_pass)
low_back.defvjp(back_keep, back_low)

def layer_norm(value, gain, shift):
    average = lax.optimization_barrier(jnp.mean(value, axis=-1, keepdims=True))
    centred = value - average
    spread = lax.optimization_barrier(jnp.mean(centred * centred, axis=-1, keepdims=True))
    return centred * lax.rsqrt(spread + 1e-05) * gain + shift

def matmul(left, right):
    return jnp.dot(left, right, precision=highest)

def attend_row(query, keys, values, seg_row):
    length = query.shape[0]
    block = math.gcd(length, 1024)
    scale = 1.0 / math.sqrt(HEAD_DIM)
    query_blocks = query.reshape(length // block, block, HEADS, HEAD_DIM)
    seg_blocks = seg_row.reshape(length // block, block)

    def one_block(inputs):
        query_part, seg_part = inputs
        scores = low_back(jnp.einsum('qhe,khe->hqk', query_part, keys, precision=highest) * scale)
        allowed = (seg_part[:, None] == seg_row[None, :])[None]
        scores = jnp.where(allowed, scores, masked)
        top = lax.optimization_barrier(jnp.max(scores, axis=-1, keepdims=True))
        weights = jnp.where(allowed, jnp.exp(scores - top), 0.0)
        probs = low(weights / lax.optimization_barrier(jnp.sum(weights, axis=-1, keepdims=True)))
        return jnp.einsum('hqk,khe->qhe', probs, values, precision=highest)
    outputs = lax.map(jax.checkpoint(one_block), (query_blocks, seg_blocks))
    return outputs.reshape(length, HEADS * HEAD_DIM)

def row_forward(token_row, seg_row, embed_row, weights):
    first_gain, first_shift, query_weight, query_bias, key_weight, value_weight, value_bias, out_weight, out_bias, second_gain, second_shift, up_weight, up_bias, down_weight, down_bias = weights
    length = token_row.shape[0]
    hidden = token_row + embed_row[None, :]
    normed = low(layer_norm(hidden, first_gain, first_shift))
    query = low_back(low(matmul(normed, query_weight) + query_bias))
    keys = low_back(low(matmul(normed, key_weight)))
    values = low_back(low(matmul(normed, value_weight) + value_bias))
    attended = attend_row(query.reshape(length, HEADS, HEAD_DIM), keys.reshape(length, HEADS, HEAD_DIM), values.reshape(length, HEADS, HEAD_DIM), seg_row)
    live = (seg_row > 0).astype(jnp.float32)
    mixed = low_back(low(attended * live[:, None]))
    residual = hidden + low_back(matmul(mixed, out_weight)) + out_bias
    normed_second = low(layer_norm(residual, second_gain, second_shift))
    inner = low_back(matmul(normed_second, up_weight) + up_bias)
    activated = low(jax.nn.gelu(inner, approximate=True))
    return residual + matmul(activated, down_weight) + down_bias

def reference(tokens, segments, timesteps, step_table, first_gain, first_shift, query_weight, query_bias, key_weight, value_weight, value_bias, out_weight, out_bias, second_gain, second_shift, up_weight, up_bias, down_weight, down_bias, cotangent):
    params = tuple((item.astype(jnp.float32) for item in (first_gain, first_shift, query_weight, query_bias, key_weight, value_weight, value_bias, out_weight, out_bias, second_gain, second_shift, up_weight, up_bias, down_weight, down_bias)))

    def forward(token_values, table_values, *weights):
        embeds = jnp.take(table_values, timesteps, axis=0)

        def one_row(inputs):
            return row_forward(inputs[0], inputs[1], inputs[2], weights)
        return lax.map(jax.checkpoint(one_row), (token_values, segments, embeds))
    output, pullback = jax.vjp(forward, tokens.astype(jnp.float32), step_table.astype(jnp.float32), *params)
    grads = pullback(cotangent.astype(jnp.float32))
    return (output.astype(jnp.bfloat16), grads[0], grads[1], grads[2], grads[3], grads[4], grads[5], grads[6], grads[7], grads[8], grads[9], grads[10], grads[11], grads[12], grads[13], grads[14], grads[15], grads[16])
```

```python
import functools
import math

import jax
import jax.numpy as jnp
from jax import lax
from jax.experimental import pallas as pl
from jax.experimental.pallas import tpu as pltpu
from jax.sharding import PartitionSpec as P

MESH = pl.DeviceIdType.MESH
BF, F32 = jnp.bfloat16, jnp.float32
NN = (((1,), (0,)), ((), ()))
NT = (((1,), (1,)), ((), ()))
TN = (((0,), (0,)), ((), ()))
HEAD_DIM = 64
BLOCK = 128
PAIR = 2 * HEAD_DIM
MASKED = -1e30
GELU_A = 0.044715
GELU_C = math.sqrt(2.0 / math.pi)
UP_AT, DOWN_AT, OUT_AT, Q_AT, K_AT, V_AT, WG_ROWS = 0, 2048, 4096, 4608, 5120, 5632, 6144
SV_TABLE = 16


def dot(a, b, dims):
    return lax.dot_general(a, b, dims, preferred_element_type=F32)


def bit(v, n):
    return lax.rem(lax.div(v, n), 2)


def flip(v, n):
    return v + n - 2 * n * bit(v, n)


def here():
    return lax.axis_index("dp"), lax.axis_index("seq"), lax.axis_index("mp")


def neighbour(name):
    dp, seq, mp = here()
    if name == "core":
        return (dp, seq, 1 - mp)
    if name == "x":
        return (1 - dp, seq, mp)
    if name == "y":
        return (dp, flip(seq, 1), mp)
    if name == "zl":
        return (dp, flip(seq, 2), mp)
    if name == "diag":
        return (dp, flip(flip(seq, 1), 2), mp)
    return (dp, flip(seq, 4), mp)


def side(name):
    dp, seq, mp = here()
    return {"x": dp, "y": bit(seq, 1), "zl": bit(seq, 2), "zh": bit(seq, 4), "core": mp}[name]


def greet(names):
    barrier = pltpu.get_barrier_semaphore()
    for name in names:
        pl.semaphore_signal(barrier, inc=1, device_id=neighbour(name), device_id_type=MESH)
    pl.semaphore_wait(barrier, len(names))


class Wire:
    def __init__(self, send_sem, recv_sem):
        self.send_sem, self.recv_sem = send_sem, recv_sem
        self.sent = []

    def send(self, src, dst, name):
        n = len(self.sent)
        copy = pltpu.make_async_remote_copy(
            src_ref=src,
            dst_ref=dst,
            send_sem=self.send_sem.at[n],
            recv_sem=self.recv_sem.at[n],
            device_id=neighbour(name),
            device_id_type=MESH,
        )
        copy.start()
        self.sent.append(copy)
        return copy

    def finish(self):
        for copy in self.sent:
            copy.wait_send()


PEERS = ("y", "zl", "diag")
GATHER_COPIES = 48


def gather_kernel(
    tokens, cot, segs, wq, wk, wv, wo, up, down, bias,
    xrow, seg_all, cot2, wq_f, wk_f, wv_f, wo_f, up_f, down_f, bias_f,
    send_sem, recv_sem, local_sem,
):
    dp, seq, mp = here()
    g = lax.div(seq, 4)
    own = 2 * seq + mp
    par = 2 * flip(seq, 4) + mp
    greet(("core", "zh") + PEERS)
    wire = Wire(send_sem, recv_sem)
    locals_ = []

    def keep(src, dst):
        copy = pltpu.make_async_copy(src, dst, local_sem.at[len(locals_)])
        copy.start()
        locals_.append(copy)

    def columns(ref):
        w = ref.shape[1] // 2
        return ref.at[:, pl.ds(pl.multiple_of(mp * w, w), w)]

    def rows(ref):
        w = ref.shape[0] // 2
        return ref.at[pl.ds(pl.multiple_of(mp * w, w), w)]

    crossing = [
        wire.send(tokens.at[1 - g], xrow.at[own], "zh"),
        wire.send(segs.at[1 - g], seg_all.at[own], "zh"),
    ]
    cot_copy = wire.send(cot.at[1 - g], cot2.at[1], "zh")
    first = []
    for name in PEERS:
        first.append(wire.send(tokens.at[g], xrow.at[own], name))
        first.append(wire.send(segs.at[g], seg_all.at[own], name))
    last = [
        wire.send(tokens.at[g], xrow.at[own], "core"),
        wire.send(segs.at[g], seg_all.at[own], "core"),
    ]
    for src, dst in (
        (wk, columns(wk_f)), (wv, columns(wv_f)), (wq, columns(wq_f)), (bias, bias_f.at[mp]),
        (wo, rows(wo_f)), (up, columns(up_f)), (down, rows(down_f)),
    ):
        last.append(wire.send(src, dst, "core"))
        keep(src, dst)
    keep(tokens.at[g], xrow.at[own])
    keep(segs.at[g], seg_all.at[own])
    keep(cot.at[g], cot2.at[0])
    for copy in crossing:
        copy.wait_recv()
    second = []
    for name in PEERS:
        second.append(wire.send(xrow.at[par], xrow.at[par], name))
        second.append(wire.send(seg_all.at[par], seg_all.at[par], name))
    last.append(wire.send(xrow.at[par], xrow.at[par], "core"))
    last.append(wire.send(seg_all.at[par], seg_all.at[par], "core"))
    for copies, base in ((first, seq), (second, flip(seq, 4))):
        for i, name in enumerate(PEERS):
            copies[2 * i].wait_recv()
            copies[2 * i + 1].wait_recv()
            there = {"y": flip(base, 1), "zl": flip(base, 2), "diag": flip(flip(base, 1), 2)}[name]
            block = 2 * there + mp
            last.append(wire.send(xrow.at[block], xrow.at[block], "core"))
            last.append(wire.send(seg_all.at[block], seg_all.at[block], "core"))
    for copy in locals_:
        copy.wait()
    cot_copy.wait_recv()
    for copy in last:
        copy.wait_recv()
    wire.finish()


def any_spec(n):
    return [pl.BlockSpec(memory_space=pl.ANY)] * n


def vmem_spec(n):
    return [pl.BlockSpec(memory_space=pltpu.VMEM)] * n


def gather(tokens, cot, segs, wq, wk, wv, wo, up, down, bias):
    shape = jax.ShapeDtypeStruct
    d = tokens.shape[2]
    blocks = 2 * lax.axis_size("seq")
    return pl.pallas_call(
        gather_kernel,
        out_shape=(
            shape((blocks, BLOCK, d), BF),
            shape((blocks, 8, BLOCK), F32),
            shape(cot.shape, BF),
            shape((d, 2 * wq.shape[1]), BF),
            shape((d, 2 * wk.shape[1]), BF),
            shape((d, 2 * wv.shape[1]), BF),
            shape((2 * wo.shape[0], d), BF),
            shape((d, 2 * up.shape[1]), BF),
            shape((2 * down.shape[0], d), BF),
            shape((2,) + bias.shape, F32),
        ),
        in_specs=any_spec(10),
        out_specs=tuple(any_spec(10)),
        scratch_shapes=[
            pltpu.SemaphoreType.DMA((GATHER_COPIES,)),
            pltpu.SemaphoreType.DMA((GATHER_COPIES,)),
            pltpu.SemaphoreType.DMA((10,)),
        ],
        compiler_params=pltpu.CompilerParams(collective_id=0, has_side_effects=True),
        name="gather",
    )(tokens, cot, segs, wq, wk, wv, wo, up, down, bias)


def normalise(value):
    centred = value - jnp.mean(value, axis=-1, keepdims=True)
    rstd = lax.rsqrt(jnp.mean(centred * centred, axis=-1, keepdims=True) + 1e-5)
    return centred * rstd, rstd


def normalise_back(grad_hat, hat, rstd):
    return rstd * (
        grad_hat
        - jnp.mean(grad_hat, axis=-1, keepdims=True)
        - hat * jnp.mean(grad_hat * hat, axis=-1, keepdims=True)
    )


def column_sum(value):
    return jnp.sum(value, axis=0, keepdims=True)


def layer_kernel(
    xrow, seg_all, cot2, embed, vecs, wq, wk, wv, wo, up, down, bias, ids,
    result2, wg, sv, t_out,
    normed, k_ref, v_ref, hot, s_buf, att, att_t, lse, q_ref, dk_ref, dv_ref, dq_ref, t_buf, dwk, dwv,
):
    dp, seq, mp = here()
    own = 2 * seq + mp
    par = 2 * flip(seq, 4) + mp
    d = normed.shape[1]
    length = normed.shape[0]
    pairs = d // PAIR
    step = 512
    steps = length // step
    nb = step // BLOCK
    ff = up.shape[1]
    row_embed = embed[...]
    gain, shift = vecs[0:1, :], vecs[1:2, :]

    def bias_row(r, n):
        return jnp.concatenate([bias[m, r + i : r + i + 1, :] for m in range(2) for i in range(n)], axis=1)

    value_bias = bias_row(1, 1)

    def hidden_of(block):
        return block.astype(F32) + row_embed

    def seg_column(block):
        return jnp.transpose(block)[:, 0:1]

    def project(c, carry):
        at = pl.ds(pl.multiple_of(c * step, step), step)
        hat, _ = normalise(hidden_of(xrow[pl.ds(c * nb, nb)].reshape(step, d)))
        low = (hat * gain + shift).astype(BF)
        normed[at, :] = low
        k_ref[at, :] = dot(low, wk[...], NN).astype(BF)
        v_ref[at, :] = (dot(low, wv[...], NN) + value_bias).astype(BF)
        spans = jnp.concatenate([seg_column(seg_all[c * nb + i]) for i in range(nb)], axis=0)
        lanes = lax.broadcasted_iota(jnp.int32, (step, BLOCK), 1).astype(F32)
        hot[at, :] = jnp.where(spans == lanes, 1.0, 0.0).astype(BF)
        return carry

    lax.fori_loop(0, steps, project, 0)

    def query_rows(ref):
        return jnp.concatenate(
            [ref[pl.ds(pl.multiple_of(b * BLOCK, BLOCK), BLOCK), :] for b in (own, par)], axis=0
        )

    normed_q = query_rows(normed)
    q_ref[...] = ((dot(normed_q, wq[...], NN) + bias_row(0, 1)).astype(BF).astype(F32) * (1.0 / math.sqrt(HEAD_DIM))).astype(BF)
    spans_q = jnp.concatenate([seg_column(seg_all[own]), seg_column(seg_all[par])], axis=0)
    nq = 2 * BLOCK
    lanes_q = lax.broadcasted_iota(jnp.int32, (nq, BLOCK), 1).astype(F32)
    other = jnp.where(spans_q == lanes_q, 0.0, MASKED).astype(BF)
    live = jnp.where(spans_q > 0.0, 1.0, 0.0)
    other2 = jnp.concatenate([other, other], axis=0)
    first_head = lax.broadcasted_iota(jnp.int32, (nq, PAIR), 1) < HEAD_DIM
    first_head_t = lax.broadcasted_iota(jnp.int32, (PAIR, nq), 0) < HEAD_DIM

    def split_heads(value):
        wide = value.astype(F32)
        return jnp.concatenate(
            [jnp.where(first_head, wide, 0.0), jnp.where(first_head, 0.0, wide)], axis=0
        ).astype(BF)

    def join_heads_t(value):
        return jnp.where(first_head_t, value[:, :nq], value[:, nq:])

    def lanes_of(p):
        return pl.ds(pl.multiple_of(p * PAIR, PAIR), PAIR)

    def chunk(c):
        return pl.ds(c * step, step)

    def attend(p, carry):
        at = lanes_of(p)
        query = jnp.concatenate([split_heads(q_ref[:, at]), other2], axis=1)
        top = jnp.full((8, 2 * nq), -3e38, F32)
        for c in range(steps):
            keys = jnp.concatenate([k_ref[chunk(c), at], hot[chunk(c), :]], axis=1)
            scores = dot(keys, query, NT)
            s_buf[chunk(c), :] = scores
            top = jnp.maximum(top, jnp.max(scores.reshape(step // 8, 8, 2 * nq), axis=0))
        top = jnp.max(top, axis=0, keepdims=True)
        total = jnp.zeros((8, 2 * nq), F32)
        summed = jnp.zeros((PAIR, 2 * nq), F32)
        for c in range(steps):
            weights = jnp.exp(s_buf[chunk(c), :] - top)
            total = total + jnp.sum(weights.reshape(step // 8, 8, 2 * nq), axis=0)
            summed = summed + dot(v_ref[chunk(c), at], weights.astype(BF), TN)
        total = jnp.sum(total, axis=0, keepdims=True)
        joined = join_heads_t(summed / total)
        att_t[p] = joined
        att[:, at] = jnp.transpose(joined)
        lse[p] = jnp.broadcast_to(top + jnp.log(total), (8, 2 * nq))
        return carry

    lax.fori_loop(0, pairs, attend, 0)

    mixed = (att[...] * live).astype(BF)
    hidden_q = hidden_of(jnp.concatenate([xrow[own], xrow[par]], axis=0))
    residual = hidden_q + dot(mixed, wo[...], NN) + vecs[4:5, :]
    gain2, shift2 = vecs[2:3, :], vecs[3:4, :]
    hat2, rstd2 = normalise(residual)
    normed2 = (hat2 * gain2 + shift2).astype(BF)
    cotangent = jnp.concatenate([cot2[0], cot2[1]], axis=0)
    half = ff // 2
    unit_result = residual + vecs[5:6, :]
    grad_normed2 = jnp.zeros((nq, d), F32)
    for j in range(ff // step):
        units = pl.ds(j * step, step)
        up_bias = jnp.concatenate([bias[(j * step) // half, 2 + (j * step) % half // 256 + i : 3 + (j * step) % half // 256 + i, :] for i in range(step // 256)], axis=1)
        inner = dot(normed2, up[:, units], NN) + up_bias
        square = inner * inner
        bent = jnp.tanh(GELU_C * inner * (1.0 + GELU_A * square))
        activated = (0.5 * inner * (1.0 + bent)).astype(BF)
        unit_result = unit_result + dot(activated, down[units, :], NN)
        slope = 0.5 * (1.0 + bent) + 0.5 * inner * (1.0 - bent * bent) * (
            GELU_C * (1.0 + 3.0 * GELU_A * square)
        )
        grad_inner = (dot(cotangent, down[units, :], NT) * slope).astype(BF)
        grad_normed2 = grad_normed2 + dot(grad_inner, up[:, units], NT)
        down_grad = dot(activated, cotangent, TN).astype(BF)
        up_grad = dot(normed2, grad_inner, TN).astype(BF)
        m, r = (j * step) // half, (j * step) % half
        for b in range(2):
            wg[m, pl.ds(UP_AT + 2 * r + b * d, d), :] = up_grad[:, b * 256 : (b + 1) * 256]
            wg[m, pl.ds(DOWN_AT + b * half + r, step), :] = down_grad[:, b * 256 : (b + 1) * 256]
        sv[6 + j : 7 + j, :] = column_sum(grad_inner.astype(F32))
    out = unit_result.astype(BF)
    result2[0] = out[:BLOCK]
    result2[1] = out[BLOCK:]
    cot_f = cotangent.astype(F32)
    grad_residual = cot_f + normalise_back(grad_normed2 * gain2, hat2, rstd2)
    sv[2:3, :] = column_sum(grad_normed2 * hat2)
    sv[3:4, :] = column_sum(grad_normed2)
    sv[4:5, :] = column_sum(grad_residual)
    sv[5:6, :] = column_sum(cot_f)
    branch_grad = grad_residual.astype(BF)
    out_grad = dot(mixed, branch_grad, TN).astype(BF)
    for m in range(2):
        for b in range(2):
            wg[m, pl.ds(OUT_AT + b * 256, 256), :] = out_grad[m * 256 : (m + 1) * 256, b * 256 : (b + 1) * 256]
    grad_mixed = dot(branch_grad, wo[...], NT).astype(BF).astype(F32) * live
    att[...] = grad_mixed

    def back(p, carry):
        at = lanes_of(p)
        query = split_heads(q_ref[:, at])
        query_wide = jnp.concatenate([query, other2], axis=1)
        heads = att[:, at]
        grads = split_heads(heads)
        product = jnp.transpose(heads) * att_t[p]
        delta = jnp.concatenate([column_sum(product[:HEAD_DIM]), column_sum(product[HEAD_DIM:])], axis=1)
        log_total = lse[p][0:1, :]
        query_grad = jnp.zeros((PAIR, 2 * nq), F32)
        for c in range(steps):
            keys = k_ref[chunk(c), at]
            scores = dot(jnp.concatenate([keys, hot[chunk(c), :]], axis=1), query_wide, NT)
            probs = jnp.exp(scores - log_total)
            grad_probs = dot(v_ref[chunk(c), at], grads, NT)
            grad_scores = (probs * (grad_probs - delta)).astype(BF)
            dk_ref[chunk(c), at] = dot(grad_scores, query, NN).astype(BF)
            dv_ref[chunk(c), at] = dot(probs.astype(BF), grads, NN).astype(BF)
            query_grad = query_grad + dot(keys, grad_scores, TN)
        joined = join_heads_t(query_grad) * (1.0 / math.sqrt(HEAD_DIM))
        dq_ref[:, at] = jnp.transpose(joined).astype(BF)
        return carry

    lax.fori_loop(0, pairs, back, 0)

    dwk[...] = jnp.zeros_like(dwk)
    dwv[...] = jnp.zeros_like(dwv)

    def tokens_back(grad_normed, block):
        hat, rstd = normalise(hidden_of(block))
        return (
            normalise_back(grad_normed * gain, hat, rstd),
            column_sum(grad_normed * hat),
            column_sum(grad_normed),
        )

    def project_back(c, carry):
        gain_sum, shift_sum, token_sum, value_sum = carry
        at = pl.ds(pl.multiple_of(c * step, step), step)
        low, key_grad, value_grad = normed[at, :], dk_ref[at, :], dv_ref[at, :]
        dwk[...] += dot(low, key_grad, TN)
        dwv[...] += dot(low, value_grad, TN)
        grad_normed = dot(key_grad, wk[...], NT) + dot(value_grad, wv[...], NT)
        token_grad, a, b = tokens_back(grad_normed, xrow[pl.ds(c * nb, nb)].reshape(step, d))
        t_buf[pl.ds(c * nb, nb)] = token_grad.reshape(nb, BLOCK, d)
        return (
            gain_sum + a,
            shift_sum + b,
            token_sum + column_sum(token_grad),
            value_sum + column_sum(value_grad.astype(F32)),
        )

    zero = jnp.zeros((1, d), F32)
    gain_sum, shift_sum, token_sum, value_sum = lax.fori_loop(0, steps, project_back, (zero,) * 4)
    query_grad = dq_ref[...]
    token_grad, a, b = tokens_back(
        dot(query_grad, wq[...], NT), jnp.concatenate([xrow[own], xrow[par]], axis=0)
    )
    token_grad = token_grad + grad_residual
    t_buf[own] += token_grad[:BLOCK]
    t_buf[par] += token_grad[BLOCK:]
    for i in range(t_out.shape[0]):
        t_out[i] = t_buf[i].astype(BF)
    sv[0:1, :] = gain_sum + a
    sv[1:2, :] = shift_sum + b
    sv[10:11, :] = column_sum(query_grad.astype(F32))
    sv[11:12, :] = value_sum
    sv[12:16, :] = jnp.zeros((4, d), F32)
    sv[12:13, :] = ids[...]
    sv[SV_TABLE:, :] = jnp.zeros((sv.shape[0] - SV_TABLE, d), F32)
    slot = lax.broadcasted_iota(jnp.int32, (sv.shape[0] - SV_TABLE, d), 0) == 2 * dp + lax.div(seq, 4)
    sv[SV_TABLE:, :] = jnp.where(slot, token_sum + column_sum(token_grad), 0.0)
    query_weight_grad = dot(query_rows(normed), query_grad, TN).astype(BF)
    for m in range(2):
        at = slice(m * 256, (m + 1) * 256)
        wg[m, pl.ds(Q_AT, d), :] = query_weight_grad[:, at]
        wg[m, pl.ds(K_AT, d), :] = dwk[:, at].astype(BF)
        wg[m, pl.ds(V_AT, d), :] = dwv[:, at].astype(BF)


def layer(xrow, seg_all, cot2, embed, vecs, wq, wk, wv, wo, up, down, bias, ids, sv_rows):
    shape = jax.ShapeDtypeStruct
    blocks, _, d = xrow.shape
    length = blocks * BLOCK
    nq = 2 * BLOCK
    pairs = d // PAIR
    return pl.pallas_call(
        layer_kernel,
        out_shape=(
            shape(cot2.shape, BF),
            shape((2, WG_ROWS, 256), BF),
            shape((sv_rows, d), F32),
            shape((blocks, BLOCK, d), BF),
        ),
        in_specs=vmem_spec(13),
        out_specs=tuple(vmem_spec(4)),
        scratch_shapes=[
            pltpu.VMEM((length, d), BF),
            pltpu.VMEM((length, d), BF),
            pltpu.VMEM((length, d), BF),
            pltpu.VMEM((length, BLOCK), BF),
            pltpu.VMEM((length, 2 * nq), F32),
            pltpu.VMEM((nq, d), F32),
            pltpu.VMEM((pairs, PAIR, nq), F32),
            pltpu.VMEM((pairs, 8, 2 * nq), F32),
            pltpu.VMEM((nq, d), BF),
            pltpu.VMEM((length, d), BF),
            pltpu.VMEM((length, d), BF),
            pltpu.VMEM((nq, d), BF),
            pltpu.VMEM((blocks, BLOCK, d), F32),
            pltpu.VMEM((d, d), F32),
            pltpu.VMEM((d, d), F32),
        ],
        compiler_params=pltpu.CompilerParams(vmem_limit_bytes=60 << 20),
        name="layer",
    )(xrow, seg_all, cot2, embed, vecs, wq, wk, wv, wo, up, down, bias, ids)


def reduce_kernel(
    orders, wg, sv, t_in, result2,
    wg_out, sv_out, tg_out, res_out,
    acc, core_buf, step_buf, t_core, t_acc, t_step, sv_buf, sv_acc, send_sem, recv_sem,
):
    dp, seq, mp = here()
    g = lax.div(seq, 4)
    y, zl = bit(seq, 1), bit(seq, 2)
    dims = orders[0]
    greet(("core",) + tuple(sorted(dims)))
    wire = Wire(send_sem, recv_sem)
    part = WG_ROWS // len(orders)
    piece = 256

    def add_rows(out, out_at, a, a_at, b, b_at, n):
        size = min(piece, n)

        def one(i, carry):
            def at(base):
                return pl.ds(pl.multiple_of(base + i * size, size), size)

            out[at(out_at), :] = a[at(a_at), :] + b[at(b_at), :]
            return carry

        lax.fori_loop(0, n // size, one, 0)

    def weights_chain(n):
        low, size = n * part, part
        at = pl.ds(low, size)
        copy = wire.send(wg.at[1 - mp, at], core_buf.at[at], "core")
        yield
        copy.wait_recv()
        add_rows(acc, low, wg.at[mp], low, core_buf, low, size)
        used = n * part
        for i, dim in enumerate(orders[n]):
            half = size // 2
            b = side(dim)
            spot = pl.ds(used, half)
            there = pl.ds(pl.multiple_of(low + (1 - b) * half, half), half)
            copy = wire.send(acc.at[there], step_buf.at[spot], dim)
            yield
            copy.wait_recv()
            low = low + b * half
            size = half
            last = i == len(orders[n]) - 1
            add_rows(wg_out if last else acc, low, acc, low, step_buf, used, size)
            used += half
        for dim in reversed(orders[n]):
            at = pl.ds(pl.multiple_of(low, size), size)
            copy = wire.send(wg_out.at[at], wg_out.at[at], dim)
            yield
            copy.wait_recv()
            low = low - side(dim) * size
            size = 2 * size

    def vectors_chain():
        sv_acc[0] = sv[...]
        for i, dim in enumerate(("core",) + tuple(dims)):
            copy = wire.send(sv_acc.at[i], sv_buf.at[i], dim)
            yield
            copy.wait_recv()
            sv_acc[i + 1] = sv_acc[i] + sv_buf[i]
        sv_out[...] = sv_acc[len(dims) + 1]

    def tokens_chain():
        copy = wire.send(t_in.at[:, :, :, 1 - mp], t_core, "core")
        back = wire.send(result2.at[1], res_out.at[g], "zh")
        res_out[g] = result2[0]
        yield
        copy.wait_recv()
        for a in range(2):
            for b in range(2):
                for c in range(2):
                    t_acc[a, b, c] = t_in[a, b, c, mp] + t_core[a, b, c]
        one = wire.send(t_acc.at[0, :, 1 - y], t_step.at[0], "y")
        two = wire.send(t_acc.at[1, 1 - zl], t_step.at[1], "zl")
        yield
        one.wait_recv()
        for i in range(2):
            t_acc[0, i, y] += t_step[0, i]
        one = wire.send(t_acc.at[0, 1 - zl, y], t_step.at[2, 0], "zl")
        two.wait_recv()
        for i in range(2):
            t_acc[1, zl, i] += t_step[1, i]
        two = wire.send(t_acc.at[1, zl, 1 - y], t_step.at[2, 1], "y")
        yield
        one.wait_recv()
        two.wait_recv()
        t_acc[0, zl, y] += t_step[2, 0]
        t_acc[1, zl, y] += t_step[2, 1]
        copy = wire.send(t_acc.at[1 - g, zl, y], tg_out.at[g], "zh")
        tg_out[g] = t_acc[g, zl, y]
        yield
        copy.wait_recv()
        back.wait_recv()

    chains = [weights_chain(n) for n in range(len(orders))] + [tokens_chain(), vectors_chain()]
    while chains:
        running = []
        for chain in chains:
            try:
                next(chain)
                running.append(chain)
            except StopIteration:
                pass
        chains = running
    wire.finish()


def reduce(wg, sv, t_in, result2, orders):
    shape = jax.ShapeDtypeStruct
    block = t_in.shape[-2:]
    dims = len(orders[0])
    copies = len(orders) * (2 * dims + 1) + 7 + dims + 1
    return pl.pallas_call(
        functools.partial(reduce_kernel, orders),
        out_shape=(
            shape((WG_ROWS, 256), BF),
            shape(sv.shape, F32),
            shape(result2.shape, BF),
            shape(result2.shape, BF),
        ),
        in_specs=vmem_spec(4),
        out_specs=tuple(vmem_spec(4)),
        scratch_shapes=[
            pltpu.VMEM((WG_ROWS, 256), BF),
            pltpu.VMEM((WG_ROWS, 256), BF),
            pltpu.VMEM((WG_ROWS, 256), BF),
            pltpu.VMEM((2, 2, 2) + block, BF),
            pltpu.VMEM((2, 2, 2) + block, BF),
            pltpu.VMEM((3, 2) + block, BF),
            pltpu.VMEM((dims + 1,) + sv.shape, F32),
            pltpu.VMEM((dims + 2,) + sv.shape, F32),
            pltpu.SemaphoreType.DMA((copies,)),
            pltpu.SemaphoreType.DMA((copies,)),
        ],
        compiler_params=pltpu.CompilerParams(
            collective_id=1, has_side_effects=True, vmem_limit_bytes=60 << 20
        ),
        name="reduce",
    )(wg, sv, t_in, result2)


def local(
    n_dp, tokens, segments, timesteps, step_table, first_gain, first_shift, query_weight, query_bias,
    key_weight, value_weight, value_bias, out_weight, out_bias, second_gain, second_shift,
    up_weight, up_bias, down_weight, down_bias, cotangent,
):
    dp, seq, mp = here()
    g = lax.div(seq, 4)
    d = tokens.shape[2]
    table_rows = tokens.shape[0] * n_dp
    segs = jnp.broadcast_to(segments.astype(F32)[:, None, :], (segments.shape[0], 8, segments.shape[1]))
    bias = jnp.concatenate([query_bias, value_bias, up_bias, jnp.zeros((512,), BF)]).astype(F32).reshape(8, 256)
    step = lax.dynamic_index_in_dim(timesteps, g, 0, keepdims=False)
    embed = lax.dynamic_slice_in_dim(step_table, step, 1, 0).astype(F32)
    vecs = jnp.stack(
        [first_gain, first_shift, second_gain, second_shift, out_bias.astype(F32), down_bias.astype(F32)]
        + [jnp.zeros_like(first_gain)] * 2
    )
    speaks = (lax.rem(seq, 4) == 0) & (mp == 0)
    ids = jnp.where((jnp.arange(d) == 2 * dp + g) & speaks, step, 0).astype(F32)[None, :]
    xrow, seg_all, cot2, wq, wk, wv, wo, up, down, bias_all = gather(
        tokens, cotangent, segs, query_weight, key_weight, value_weight, out_weight, up_weight, down_weight, bias
    )
    sv_rows = SV_TABLE + -(-table_rows // 8) * 8
    result2, wg, sv, t_out = layer(
        xrow, seg_all, cot2, embed, vecs, wq, wk, wv, wo, up, down, bias_all, ids, sv_rows
    )
    orders = [["x", "y", "zl", "zh"], ["y", "zl", "zh", "x"], ["zl", "x", "y", "zh"]]
    if n_dp != 2:
        orders = [[dim for dim in order if dim != "x"] for order in orders]
    wg, sv, token_grad, result = reduce(wg, sv, t_out.reshape((2, 2, 2, 2) + t_out.shape[1:]), result2, orders)
    if n_dp != 2:
        wg, sv = lax.psum((wg.astype(F32), sv), "dp")
    wide = wg.astype(F32)

    def blocks(at, rows, n):
        return jnp.concatenate([wide[at + i * rows : at + (i + 1) * rows] for i in range(n)], axis=1)

    ids = sv[12, :table_rows].astype(jnp.int32)
    picks = (jnp.arange(step_table.shape[0], dtype=jnp.int32)[:, None] == ids[None, :]).astype(F32)
    table_grad = jnp.dot(picks, sv[SV_TABLE : SV_TABLE + table_rows], precision=lax.Precision.HIGHEST)
    half, units = query_weight.shape[1], up_weight.shape[1]

    def mine(row, width):
        return lax.dynamic_slice_in_dim(row, mp * width, width, 0)

    return (
        result,
        token_grad.astype(F32),
        table_grad,
        sv[0],
        sv[1],
        wide[Q_AT:K_AT],
        mine(sv[10], half),
        wide[K_AT:V_AT],
        wide[V_AT:],
        mine(sv[11], half),
        blocks(OUT_AT, out_weight.shape[0], 2),
        sv[4],
        sv[2],
        sv[3],
        blocks(UP_AT, d, 4),
        mine(sv[6:10].reshape(-1), units),
        blocks(DOWN_AT, units, 2),
        sv[5],
    )


def solution(mesh):
    rows, chars, whole = P("dp", ("seq", "mp"), None), P("dp", ("seq", "mp")), P()
    columns, split, tall = P(None, "mp"), P("mp"), P("mp", None)
    in_specs = (
        rows, chars, P("dp"), whole, whole, whole, columns, split, columns, columns, split, tall,
        whole, whole, whole, columns, split, tall, whole, rows,
    )
    out_specs = (
        rows, rows, whole, whole, whole, columns, split, columns, columns, split, tall,
        whole, whole, whole, columns, split, tall, whole,
    )
    return jax.shard_map(
        functools.partial(local, mesh.shape["dp"]),
        mesh=mesh,
        in_specs=in_specs,
        out_specs=out_specs,
        check_vma=False,
    )
```

```python
import functools
import math

import jax
import jax.numpy as jnp
from jax import lax
from jax.experimental import pallas as pl
from jax.experimental.pallas import tpu as pltpu
from jax.sharding import PartitionSpec as P

MESH = pl.DeviceIdType.MESH
BF, F32 = jnp.bfloat16, jnp.float32
NN = (((1,), (0,)), ((), ()))
NT = (((1,), (1,)), ((), ()))
TN = (((0,), (0,)), ((), ()))
HEAD_DIM = 64
BLOCK = 128
PAIR = 2 * HEAD_DIM
MASKED = -1e30
GELU_A = 0.044715
GELU_C = math.sqrt(2.0 / math.pi)
OUT_AT, Q_AT, K_AT, V_AT, WG_ROWS = 4096, 4608, 5120, 5632, 6144
SV_TABLE = 16
COPIES = 160
PEERS = ("y", "zl", "diag")
ORDERS = (("x", "y", "zl", "zh"), ("y", "x", "zl", "zh"), ("zl", "x", "y", "zh"))
WAVE_ONE = ((0, 768, 0), (768, 768, 1), (1536, 512, 2))
WAVE_TWO = ((2048, 1024, 0), (3072, 1024, 1), (4096, 512, 2))
WAVE_LAST = ((4608, 512, 0), (5120, 512, 1), (5632, 512, 2))


def dot(a, b, dims):
    return lax.dot_general(a, b, dims, preferred_element_type=F32)


def bit(v, n):
    return lax.rem(lax.div(v, n), 2)


def flip(v, n):
    return v + n - 2 * n * bit(v, n)


def here():
    return lax.axis_index("dp"), lax.axis_index("seq"), lax.axis_index("mp")


def neighbour(name):
    dp, seq, mp = here()
    if name == "core":
        return (dp, seq, 1 - mp)
    if name == "x":
        return (1 - dp, seq, mp)
    if name == "y":
        return (dp, flip(seq, 1), mp)
    if name == "zl":
        return (dp, flip(seq, 2), mp)
    if name == "diag":
        return (dp, flip(flip(seq, 1), 2), mp)
    return (dp, flip(seq, 4), mp)


def side(name):
    dp, seq, mp = here()
    return {"x": dp, "y": bit(seq, 1), "zl": bit(seq, 2), "zh": bit(seq, 4), "core": mp}[name]


def greet(names):
    barrier = pltpu.get_barrier_semaphore()
    for name in names:
        pl.semaphore_signal(barrier, inc=1, device_id=neighbour(name), device_id_type=MESH)
    pl.semaphore_wait(barrier, len(names))


class Wire:
    def __init__(self, send_sem, recv_sem):
        self.send_sem, self.recv_sem = send_sem, recv_sem
        self.sent = []

    def send(self, src, dst, name):
        n = len(self.sent)
        copy = pltpu.make_async_remote_copy(
            src_ref=src,
            dst_ref=dst,
            send_sem=self.send_sem.at[n],
            recv_sem=self.recv_sem.at[n],
            device_id=neighbour(name),
            device_id_type=MESH,
        )
        copy.start()
        self.sent.append(copy)
        return copy

    def finish(self):
        for copy in self.sent:
            copy.wait_send()


def any_spec(n):
    return [pl.BlockSpec(memory_space=pl.ANY)] * n


def vmem_spec(n):
    return [pl.BlockSpec(memory_space=pltpu.VMEM)] * n


def normalise(value):
    centred = value - jnp.mean(value, axis=-1, keepdims=True)
    rstd = lax.rsqrt(jnp.mean(centred * centred, axis=-1, keepdims=True) + 1e-5)
    return centred * rstd, rstd


def normalise_back(grad_hat, hat, rstd):
    return rstd * (
        grad_hat
        - jnp.mean(grad_hat, axis=-1, keepdims=True)
        - hat * jnp.mean(grad_hat * hat, axis=-1, keepdims=True)
    )


def column_sum(value):
    return jnp.sum(value, axis=0, keepdims=True)


class Chains:
    def __init__(self):
        self.queue = []

    def add(self, *chains):
        for chain in chains:
            next(chain)
            self.queue.append(chain)

    def tick(self, n=1):
        for _ in range(min(n, len(self.queue))):
            chain = self.queue.pop(0)
            try:
                next(chain)
                self.queue.append(chain)
            except StopIteration:
                pass

    def drain(self):
        while self.queue:
            self.tick()


def layer_kernel(
    orders,
    tokens, cot, wq_h, wk_h, wv_h, wo_h, up_h, down_h, segments, timesteps, table, vecs,
    wg_out, sv_out, tg_out, res_out,
    xrow, seg_mine, seg_all, cot2, wq, wk, wv, wo, up, down, bias,
    normed, k_ref, v_ref, hot, s_buf, att, att_t, lse, q_ref, dk_ref, dv_ref, dq_ref, t_buf, dwk, dwv,
    wg, acc, core_buf, step_buf, t_out, t_core, t_acc, t_step, result2, sv_buf, sv_acc,
    send_sem, recv_sem, local_sem,
):
    dp, seq, mp = here()
    g = lax.div(seq, 4)
    pseq = flip(seq, 4)
    own, par = 2 * seq + mp, 2 * pseq + mp
    y, zl = bit(seq, 1), bit(seq, 2)
    d = normed.shape[1]
    length = normed.shape[0]
    pairs = d // PAIR
    step = 512
    steps = length // step
    nb = step // BLOCK
    ff = up.shape[1]
    half = ff // 2
    nq = 2 * BLOCK

    seg_mine[...] = jnp.broadcast_to(segments[...].astype(F32)[:, None, :], seg_mine.shape)
    greet(("core",) + PEERS + tuple(sorted(set(orders[0]) - set(PEERS))))
    wire = Wire(send_sem, recv_sem)
    chains = Chains()
    kept = []

    def keep(src, dst):
        copy = pltpu.make_async_copy(src, dst, local_sem.at[len(kept)])
        copy.start()
        kept.append(copy)
        return copy

    def columns(ref):
        w = ref.shape[1] // 2
        return ref.at[:, pl.ds(pl.multiple_of(mp * w, w), w)]

    def rows(ref):
        w = ref.shape[0] // 2
        return ref.at[pl.ds(pl.multiple_of(mp * w, w), w)]

    def pass_on(block, name):
        return [
            wire.send(xrow.at[block], xrow.at[block], name),
            wire.send(seg_all.at[block], seg_all.at[block], name),
        ]

    def arrive(copies):
        for copy in copies:
            copy.wait_recv()

    def share(name):
        return [wire.send(tokens.at[g], xrow.at[own], name), wire.send(seg_mine.at[g], seg_all.at[own], name)]

    crossing = [
        wire.send(tokens.at[1 - g], xrow.at[own], "zh"),
        wire.send(seg_mine.at[1 - g], seg_all.at[own], "zh"),
    ]
    first = {name: share(name) for name in PEERS}
    own_kept = [keep(tokens.at[g], xrow.at[own]), keep(seg_mine.at[g], seg_all.at[own])]
    own_mate = share("core")
    early, late, early_kept, late_kept = [], [], [], []
    for src, dst in ((wk_h, columns(wk)), (wv_h, columns(wv)), (vecs.at[pl.ds(8, 8)], bias.at[mp])):
        early.append(wire.send(src, dst, "core"))
        early_kept.append(keep(src, dst))
    for src, dst in ((wq_h, columns(wq)), (wo_h, rows(wo)), (up_h, columns(up)), (down_h, rows(down))):
        late.append(wire.send(src, dst, "core"))
        late_kept.append(keep(src, dst))
    late.append(wire.send(cot.at[1 - g], cot2.at[1], "zh"))
    late_kept.append(keep(cot.at[g], cot2.at[0]))

    lane = lax.broadcasted_iota(jnp.int32, timesteps.shape, 1)
    moment = jnp.sum(jnp.where(lane == g, timesteps[...], 0).astype(F32), axis=1, keepdims=True)
    ids = lax.broadcasted_iota(jnp.int32, (8, table.shape[0]), 1).astype(F32)
    row_embed = dot(jnp.where(ids == moment, 1.0, 0.0).astype(BF), table[...], NN)[0:1, :]
    gain, shift = vecs[0:1, :], vecs[1:2, :]

    def hidden_of(block):
        return block.astype(F32) + row_embed

    def seg_column(block):
        return jnp.transpose(block)[:, 0:1]

    for copy in early_kept + own_kept:
        copy.wait()
    arrive(early)
    query_bias = jnp.concatenate([bias[0, 0:1, :256], bias[1, 0:1, :256]], axis=1)
    value_bias = jnp.concatenate([bias[0, 0:1, 256:], bias[1, 0:1, 256:]], axis=1)

    def project(s):
        n = 2 * BLOCK
        at = pl.ds(pl.multiple_of(s * n, n), n)
        hat, _ = normalise(hidden_of(xrow[pl.ds(2 * s, 2)].reshape(n, d)))
        low = (hat * gain + shift).astype(BF)
        normed[at, :] = low
        k_ref[at, :] = dot(low, wk[...], NN).astype(BF)
        v_ref[at, :] = (dot(low, wv[...], NN) + value_bias).astype(BF)
        spans = jnp.concatenate([seg_column(seg_all[2 * s + i]) for i in range(2)], axis=0)
        lanes = lax.broadcasted_iota(jnp.int32, (n, BLOCK), 1).astype(F32)
        hot[at, :] = jnp.where(spans == lanes, 1.0, 0.0).astype(BF)

    def beyond(base, name):
        return {"y": flip(base, 1), "zl": flip(base, 2), "diag": flip(flip(base, 1), 2)}[name]

    arrive(own_mate)
    project(seq)
    mates = {}
    for name in PEERS:
        arrive(first[name])
        mates[name] = pass_on(2 * beyond(seq, name) + mp, "core")
    arrive(crossing)
    second = {name: pass_on(par, name) for name in PEERS}
    par_mate = pass_on(par, "core")
    for name in PEERS:
        arrive(mates[name])
        project(beyond(seq, name))
    arrive(par_mate)
    project(pseq)
    for name in PEERS:
        arrive(second[name])
        mates[name] = pass_on(2 * beyond(pseq, name) + mp, "core")
    for copy in late_kept:
        copy.wait()
    arrive(late)

    def query_rows(ref):
        return jnp.concatenate(
            [ref[pl.ds(pl.multiple_of(b * BLOCK, BLOCK), BLOCK), :] for b in (own, par)], axis=0
        )

    scale = 1.0 / math.sqrt(HEAD_DIM)
    query_low = (dot(query_rows(normed), wq[...], NN) + query_bias).astype(BF)
    q_ref[...] = (query_low.astype(F32) * scale).astype(BF)
    for name in PEERS:
        arrive(mates[name])
        project(beyond(pseq, name))

    spans_q = jnp.concatenate([seg_column(seg_all[own]), seg_column(seg_all[par])], axis=0)
    lanes_q = lax.broadcasted_iota(jnp.int32, (nq, BLOCK), 1).astype(F32)
    other = jnp.where(spans_q == lanes_q, 0.0, MASKED).astype(BF)
    live = jnp.where(spans_q > 0.0, 1.0, 0.0)
    other2 = jnp.concatenate([other, other], axis=0)
    first_head = lax.broadcasted_iota(jnp.int32, (nq, PAIR), 1) < HEAD_DIM
    first_head_t = lax.broadcasted_iota(jnp.int32, (PAIR, nq), 0) < HEAD_DIM

    def split_heads(value):
        wide = value.astype(F32)
        return jnp.concatenate(
            [jnp.where(first_head, wide, 0.0), jnp.where(first_head, 0.0, wide)], axis=0
        ).astype(BF)

    def join_heads_t(value):
        return jnp.where(first_head_t, value[:, :nq], value[:, nq:])

    def lanes_of(p):
        return pl.ds(p * PAIR, PAIR)

    def chunk(c):
        return pl.ds(c * step, step)

    def attend(p):
        at = lanes_of(p)
        query = jnp.concatenate([split_heads(q_ref[:, at]), other2], axis=1)
        top = jnp.full((8, 2 * nq), -3e38, F32)
        for c in range(steps):
            keys = jnp.concatenate([k_ref[chunk(c), at], hot[chunk(c), :]], axis=1)
            scores = dot(keys, query, NT)
            s_buf[chunk(c), :] = scores
            top = jnp.maximum(top, jnp.max(scores.reshape(step // 8, 8, 2 * nq), axis=0))
        top = jnp.max(top, axis=0, keepdims=True)
        total = jnp.zeros((8, 2 * nq), F32)
        summed = jnp.zeros((PAIR, 2 * nq), F32)
        for c in range(steps):
            weights = jnp.exp(s_buf[chunk(c), :] - top)
            total = total + jnp.sum(weights.reshape(step // 8, 8, 2 * nq), axis=0)
            summed = summed + dot(v_ref[chunk(c), at], weights.astype(BF), TN)
        total = jnp.sum(total, axis=0, keepdims=True)
        joined = join_heads_t(summed / total)
        att_t[p] = joined
        att[:, at] = jnp.transpose(joined)
        lse[p] = jnp.broadcast_to(top + jnp.log(total), (8, 2 * nq))

    for p in range(pairs):
        attend(p)

    def add_rows(out, out_at, a, a_at, b, b_at, n):
        size = next(s for s in (256, 192, 128, 96, 64, 48, 32, 16) if n % s == 0)

        def one(i, carry):
            def at(base):
                return pl.ds(pl.multiple_of(base + i * size, size), size)

            out[at(out_at), :] = a[at(a_at), :] + b[at(b_at), :]
            return carry

        lax.fori_loop(0, n // size, one, 0)

    def weights_chain(low, size, order):
        at = pl.ds(low, size)
        used = low
        copy = wire.send(wg.at[1 - mp, at], core_buf.at[at], "core")
        yield
        copy.wait_recv()
        add_rows(acc, low, wg.at[mp], low, core_buf, low, size)
        for i, dim in enumerate(order):
            size = size // 2
            b = side(dim)
            spot = pl.ds(used, size)
            there = pl.ds(pl.multiple_of(low + (1 - b) * size, size), size)
            copy = wire.send(acc.at[there], step_buf.at[spot], dim)
            yield
            copy.wait_recv()
            low = low + b * size
            add_rows(wg_out if i == len(order) - 1 else acc, low, acc, low, step_buf, used, size)
            used += size
        for dim in reversed(order):
            at = pl.ds(pl.multiple_of(low, size), size)
            copy = wire.send(wg_out.at[at], wg_out.at[at], dim)
            yield
            copy.wait_recv()
            low = low - side(dim) * size
            size = 2 * size

    def start_weights(wave):
        chains.add(*[weights_chain(low, size, orders[n]) for low, size, n in wave])

    mixed = (att[...] * live).astype(BF)
    hidden_q = hidden_of(jnp.concatenate([xrow[own], xrow[par]], axis=0))
    residual = hidden_q + dot(mixed, wo[...], NN) + vecs[4:5, :]
    gain2, shift2 = vecs[2:3, :], vecs[3:4, :]
    hat2, rstd2 = normalise(residual)
    normed2 = (hat2 * gain2 + shift2).astype(BF)
    cotangent = jnp.concatenate([cot2[0], cot2[1]], axis=0)
    unit_result = residual + vecs[5:6, :]
    grad_normed2 = jnp.zeros((nq, d), F32)
    sv = sv_acc.at[0]
    for r in range(half // step):
        for m in range(2):
            j = (m * half + r * step) // step
            units = pl.ds(j * step, step)
            inner = dot(normed2, up[:, units], NN) + bias[m, 1 + r : 2 + r, :]
            square = inner * inner
            bent = jnp.tanh(GELU_C * inner * (1.0 + GELU_A * square))
            activated = (0.5 * inner * (1.0 + bent)).astype(BF)
            unit_result = unit_result + dot(activated, down[units, :], NN)
            slope = 0.5 * (1.0 + bent) + 0.5 * inner * (1.0 - bent * bent) * (
                GELU_C * (1.0 + 3.0 * GELU_A * square)
            )
            grad_inner = (dot(cotangent, down[units, :], NT) * slope).astype(BF)
            grad_normed2 = grad_normed2 + dot(grad_inner, up[:, units], NT)
            down_grad = dot(activated, cotangent, TN).astype(BF)
            up_grad = dot(normed2, grad_inner, TN).astype(BF)
            for b in range(2):
                at = slice(b * 256, (b + 1) * 256)
                wg[m, pl.ds(2048 * r + b * 512, 512), :] = up_grad[:, at]
                wg[m, pl.ds(2048 * r + 1024 + b * 512, 512), :] = down_grad[:, at]
            sv[6 + j : 7 + j, :] = column_sum(grad_inner.astype(F32))
        if r == 0:
            start_weights(WAVE_ONE)
    out = unit_result.astype(BF)
    result2[0] = out[:BLOCK]
    result2[1] = out[BLOCK:]
    result_back = wire.send(result2.at[1], res_out.at[g], "zh")
    res_out[g] = out[:BLOCK]
    cot_f = cotangent.astype(F32)
    grad_residual = cot_f + normalise_back(grad_normed2 * gain2, hat2, rstd2)
    sv[2:3, :] = column_sum(grad_normed2 * hat2)
    sv[3:4, :] = column_sum(grad_normed2)
    sv[4:5, :] = column_sum(grad_residual)
    sv[5:6, :] = column_sum(cot_f)
    branch_grad = grad_residual.astype(BF)
    out_grad = dot(mixed, branch_grad, TN).astype(BF)
    for m in range(2):
        for b in range(2):
            wg[m, pl.ds(OUT_AT + b * 256, 256), :] = out_grad[m * 256 : (m + 1) * 256, b * 256 : (b + 1) * 256]
    start_weights(WAVE_TWO)
    att[...] = dot(branch_grad, wo[...], NT).astype(BF).astype(F32) * live

    def back(p):
        at = lanes_of(p)
        query = split_heads(q_ref[:, at])
        query_wide = jnp.concatenate([query, other2], axis=1)
        heads = att[:, at]
        grads = split_heads(heads)
        product = jnp.transpose(heads) * att_t[p]
        delta = jnp.concatenate([column_sum(product[:HEAD_DIM]), column_sum(product[HEAD_DIM:])], axis=1)
        log_total = lse[p][0:1, :]
        query_grad = jnp.zeros((PAIR, 2 * nq), F32)
        for c in range(steps):
            keys = k_ref[chunk(c), at]
            scores = dot(jnp.concatenate([keys, hot[chunk(c), :]], axis=1), query_wide, NT)
            probs = jnp.exp(scores - log_total)
            grad_probs = dot(v_ref[chunk(c), at], grads, NT)
            grad_scores = (probs * (grad_probs - delta)).astype(BF)
            dk_ref[chunk(c), at] = dot(grad_scores, query, NN).astype(BF)
            dv_ref[chunk(c), at] = dot(probs.astype(BF), grads, NN).astype(BF)
            query_grad = query_grad + dot(keys, grad_scores, TN)
            chains.tick()
        joined = join_heads_t(query_grad) * scale
        dq_ref[:, at] = jnp.transpose(joined).astype(BF)

    for p in range(pairs):
        back(p)

    def tokens_back(grad_normed, block):
        hat, rstd = normalise(hidden_of(block))
        return (
            normalise_back(grad_normed * gain, hat, rstd),
            column_sum(grad_normed * hat),
            column_sum(grad_normed),
        )

    gain_sum = shift_sum = token_sum = value_sum = jnp.zeros((1, d), F32)
    for c in range(steps):
        at = chunk(c)
        low, key_grad, value_grad = normed[at, :], dk_ref[at, :], dv_ref[at, :]
        grad_normed = dot(key_grad, wk[...], NT) + dot(value_grad, wv[...], NT)
        token_grad, a, b = tokens_back(grad_normed, xrow[pl.ds(c * nb, nb)].reshape(step, d))
        t_buf[pl.ds(c * nb, nb)] = token_grad.reshape(nb, BLOCK, d)
        gain_sum, shift_sum, token_sum = gain_sum + a, shift_sum + b, token_sum + column_sum(token_grad)
        value_sum = value_sum + column_sum(value_grad.astype(F32))
        chains.tick()
    query_grad = dq_ref[...]
    token_grad, a, b = tokens_back(
        dot(query_grad, wq[...], NT), jnp.concatenate([xrow[own], xrow[par]], axis=0)
    )
    token_grad = token_grad + grad_residual
    t_buf[own] += token_grad[:BLOCK]
    t_buf[par] += token_grad[BLOCK:]
    for i in range(t_buf.shape[0]):
        t_out[i // 8, i // 4 % 2, i // 2 % 2, i % 2] = t_buf[i].astype(BF)

    def tokens_chain():
        copy = wire.send(t_out.at[:, :, :, 1 - mp], t_core, "core")
        yield
        copy.wait_recv()
        for a in range(2):
            for b in range(2):
                for c in range(2):
                    t_acc[a, b, c] = t_out[a, b, c, mp] + t_core[a, b, c]
        one = wire.send(t_acc.at[0, :, 1 - y], t_step.at[0], "y")
        two = wire.send(t_acc.at[1, 1 - zl], t_step.at[1], "zl")
        yield
        one.wait_recv()
        for i in range(2):
            t_acc[0, i, y] += t_step[0, i]
        one = wire.send(t_acc.at[0, 1 - zl, y], t_step.at[2, 0], "zl")
        two.wait_recv()
        for i in range(2):
            t_acc[1, zl, i] += t_step[1, i]
        two = wire.send(t_acc.at[1, zl, 1 - y], t_step.at[2, 1], "y")
        yield
        one.wait_recv()
        two.wait_recv()
        t_acc[0, zl, y] += t_step[2, 0]
        t_acc[1, zl, y] += t_step[2, 1]
        copy = wire.send(t_acc.at[1 - g, zl, y], tg_out.at[g], "zh")
        tg_out[g] = t_acc[g, zl, y]
        yield
        copy.wait_recv()
        result_back.wait_recv()

    chains.add(tokens_chain())
    chains.tick(2)
    for c in range(steps):
        at = chunk(c)
        key_part, value_part = dot(normed[at, :], dk_ref[at, :], TN), dot(normed[at, :], dv_ref[at, :], TN)
        dwk[...] = key_part if c == 0 else dwk[...] + key_part
        dwv[...] = value_part if c == 0 else dwv[...] + value_part
        chains.tick()
    query_weight_grad = dot(query_rows(normed), query_grad, TN).astype(BF)
    for m in range(2):
        at = slice(m * 256, (m + 1) * 256)
        wg[m, pl.ds(Q_AT, d), :] = query_weight_grad[:, at]
        wg[m, pl.ds(K_AT, d), :] = dwk[:, at].astype(BF)
        wg[m, pl.ds(V_AT, d), :] = dwv[:, at].astype(BF)
    start_weights(WAVE_LAST)

    sv[0:1, :] = gain_sum + a
    sv[1:2, :] = shift_sum + b
    sv[10:11, :] = column_sum(query_grad.astype(F32))
    sv[11:12, :] = value_sum
    sv[12:16, :] = jnp.zeros((4, d), F32)
    slot_lane = lax.broadcasted_iota(jnp.int32, (1, d), 1)
    speaks = jnp.logical_and(lax.rem(seq, 4) == 0, mp == 0)
    my_slot = 2 * dp + g
    sv[12:13, :] = jnp.where(slot_lane == jnp.where(speaks, my_slot, -1), moment, 0.0)
    slot = lax.broadcasted_iota(jnp.int32, (sv.shape[0] - SV_TABLE, d), 0) == my_slot
    sv[SV_TABLE:, :] = jnp.where(slot, token_sum + column_sum(token_grad), 0.0)

    def vectors_chain():
        dims = ("core",) + tuple(orders[0])
        for i, dim in enumerate(dims):
            copy = wire.send(sv_acc.at[i], sv_buf.at[i], dim)
            yield
            copy.wait_recv()
            sv_acc[i + 1] = sv_acc[i] + sv_buf[i]
        sv_out[...] = sv_acc[len(dims)]

    chains.add(vectors_chain())
    chains.drain()
    wire.finish()


def layer(tokens, cot, wq, wk, wv, wo, up, down, segments, timesteps, table, vecs, orders, sv_rows):
    shape = jax.ShapeDtypeStruct
    d = tokens.shape[2]
    blocks = 2 * lax.axis_size("seq")
    length = blocks * BLOCK
    nq = 2 * BLOCK
    pairs = d // PAIR
    ff = 2 * up.shape[1]
    dims = len(orders[0])
    block = (BLOCK, d)
    vmem = pltpu.VMEM
    return pl.pallas_call(
        functools.partial(layer_kernel, orders),
        out_shape=(
            shape((WG_ROWS, 256), BF),
            shape((sv_rows, d), F32),
            shape(tokens.shape, BF),
            shape(tokens.shape, BF),
        ),
        in_specs=any_spec(8) + vmem_spec(4),
        out_specs=tuple(vmem_spec(4)),
        scratch_shapes=[
            vmem((blocks,) + block, BF),
            vmem((2, 8, BLOCK), F32),
            vmem((blocks, 8, BLOCK), F32),
            vmem((2,) + block, BF),
            vmem((d, d), BF),
            vmem((d, d), BF),
            vmem((d, d), BF),
            vmem((d, d), BF),
            vmem((d, ff), BF),
            vmem((ff, d), BF),
            vmem((2, 8, d), F32),
            vmem((length, d), BF),
            vmem((length, d), BF),
            vmem((length, d), BF),
            vmem((length, BLOCK), BF),
            vmem((length, 2 * nq), F32),
            vmem((nq, d), F32),
            vmem((pairs, PAIR, nq), F32),
            vmem((pairs, 8, 2 * nq), F32),
            vmem((nq, d), BF),
            vmem((length, d), BF),
            vmem((length, d), BF),
            vmem((nq, d), BF),
            vmem((blocks,) + block, F32),
            vmem((d, d), F32),
            vmem((d, d), F32),
            vmem((2, WG_ROWS, 256), BF),
            vmem((WG_ROWS, 256), BF),
            vmem((WG_ROWS, 256), BF),
            vmem((WG_ROWS, 256), BF),
            vmem((2, 2, 2, 2) + block, BF),
            vmem((2, 2, 2) + block, BF),
            vmem((2, 2, 2) + block, BF),
            vmem((3, 2) + block, BF),
            vmem((2,) + block, BF),
            vmem((dims + 1, sv_rows, d), F32),
            vmem((dims + 2, sv_rows, d), F32),
            pltpu.SemaphoreType.DMA((COPIES,)),
            pltpu.SemaphoreType.DMA((COPIES,)),
            pltpu.SemaphoreType.DMA((16,)),
        ],
        compiler_params=pltpu.CompilerParams(
            collective_id=0, has_side_effects=True, vmem_limit_bytes=62 << 20
        ),
        name="layer",
    )(tokens, cot, wq, wk, wv, wo, up, down, segments, timesteps, table, vecs)


def local(
    n_dp, tokens, segments, timesteps, step_table, first_gain, first_shift, query_weight, query_bias,
    key_weight, value_weight, value_bias, out_weight, out_bias, second_gain, second_shift,
    up_weight, up_bias, down_weight, down_bias, cotangent,
):
    mp = lax.axis_index("mp")
    d = tokens.shape[2]
    table_rows = tokens.shape[0] * n_dp
    vecs = jnp.concatenate(
        [first_gain, first_shift, second_gain, second_shift]
        + [v.astype(F32) for v in (out_bias, down_bias)]
        + [jnp.zeros((2 * d,), F32)]
        + [v.astype(F32) for v in (query_bias, value_bias, up_bias)]
        + [jnp.zeros((5 * d,), F32)]
    ).reshape(16, d)
    sv_rows = SV_TABLE + -(-table_rows // 8) * 8
    orders = [tuple(dim for dim in order if dim != "x" or n_dp == 2) for order in ORDERS]
    wg, sv, token_grad, result = layer(
        tokens, cotangent, query_weight, key_weight, value_weight, out_weight, up_weight, down_weight,
        segments, timesteps[None, :], step_table, vecs, orders, sv_rows,
    )
    if n_dp != 2:
        wg, sv = lax.psum((wg.astype(F32), sv), "dp")
    wide = wg.astype(F32)

    def beside(at, rows, n):
        return jnp.concatenate([wide[at + i * rows : at + (i + 1) * rows] for i in range(n)], axis=1)

    ids = sv[12, :table_rows].astype(jnp.int32)
    picks = (jnp.arange(step_table.shape[0], dtype=jnp.int32)[:, None] == ids[None, :]).astype(F32)
    table_grad = jnp.dot(picks, sv[SV_TABLE : SV_TABLE + table_rows], precision=lax.Precision.HIGHEST)
    half, units = query_weight.shape[1], up_weight.shape[1]

    def mine(row, width):
        return lax.dynamic_slice_in_dim(row, mp * width, width, 0)

    return (
        result,
        token_grad.astype(F32),
        table_grad,
        sv[0],
        sv[1],
        wide[Q_AT:K_AT],
        mine(sv[10], half),
        wide[K_AT:V_AT],
        wide[V_AT:],
        mine(sv[11], half),
        beside(OUT_AT, out_weight.shape[0], 2),
        sv[4],
        sv[2],
        sv[3],
        jnp.concatenate([beside(0, d, 2), beside(2048, d, 2)], axis=1),
        mine(sv[6:10].reshape(-1), units),
        jnp.concatenate([beside(1024, 512, 2), beside(3072, 512, 2)], axis=0),
        sv[5],
    )


def solution(mesh):
    rows, chars, whole = P("dp", ("seq", "mp"), None), P("dp", ("seq", "mp")), P()
    columns, split, tall = P(None, "mp"), P("mp"), P("mp", None)
    in_specs = (
        rows, chars, P("dp"), whole, whole, whole, columns, split, columns, columns, split, tall,
        whole, whole, whole, columns, split, tall, whole, rows,
    )
    out_specs = (
        rows, rows, whole, whole, whole, columns, split, columns, columns, split, tall,
        whole, whole, whole, columns, split, tall, whole,
    )
    return jax.shard_map(
        functools.partial(local, mesh.shape["dp"]),
        mesh=mesh,
        in_specs=in_specs,
        out_specs=out_specs,
        check_vma=False,
    )
```

```python
import functools
import math

import jax
import jax.numpy as jnp
from jax import lax
from jax.experimental import pallas as pl
from jax.experimental.pallas import tpu as pltpu
from jax.sharding import PartitionSpec as P

MESH = pl.DeviceIdType.MESH
BF, F32 = jnp.bfloat16, jnp.float32
NN = (((1,), (0,)), ((), ()))
NT = (((1,), (1,)), ((), ()))
TN = (((0,), (0,)), ((), ()))
HEAD_DIM = 64
BLOCK = 128
PAIR = 2 * HEAD_DIM
MASKED = -1e30
GELU_A = 0.044715
GELU_C = math.sqrt(2.0 / math.pi)
OUT_AT, PAIR_AT, PAIR_ROWS, WG_ROWS = 4096, (4608, 5376), 768, 6144
SV_TABLE = 16
RECEIVES, SENDS, KEEPS = 184, 48, 28
SPANS_AT, ROWS_AT = 128, 144
PEERS = ("y", "zl", "diag")
ORDER_A = (("x",), ("y",), ("zl", "zh"))
ORDER_B = (("y",), ("x",), ("zl", "zh"))
ORDER_C = (("zl",), ("x",), ("y",), ("zh",))
WAVE_ONE = ((0, 512, ORDER_A), (512, 512, ORDER_B), (1024, 512, ORDER_C))
WAVE_TWO = ((1536, 512, ORDER_A), (2048, 512, ORDER_B), (2560, 512, ORDER_C))
WAVE_THREE = ((3072, 512, ORDER_A), (3584, 512, ORDER_B), (4096, 512, ORDER_C))
WAVE_PAIR = (((4608, 512, ORDER_A), (5120, 256, ORDER_B)), ((5376, 512, ORDER_A), (5888, 256, ORDER_B)))


def dot(a, b, dims):
    return lax.dot_general(a, b, dims, preferred_element_type=F32)


def bit(v, n):
    return lax.rem(lax.div(v, n), 2)


def flip(v, n):
    return v + n - 2 * n * bit(v, n)


def here():
    return lax.axis_index("dp"), lax.axis_index("seq"), lax.axis_index("mp")


def neighbour(name):
    dp, seq, mp = here()
    dims = {"diag": ("y", "zl")}.get(name, name if isinstance(name, tuple) else (name,))
    for dim in dims:
        if dim == "core":
            mp = 1 - mp
        elif dim == "x":
            dp = 1 - dp
        else:
            seq = flip(seq, {"y": 1, "zl": 2, "zh": 4}[dim])
    return (dp, seq, mp)


def side(name):
    dp, seq, mp = here()
    return {"x": dp, "y": bit(seq, 1), "zl": bit(seq, 2), "zh": bit(seq, 4), "core": mp}[name]


def relations(stage):
    return [tuple(dim for i, dim in enumerate(stage) if k >> i & 1) for k in range(1, 1 << len(stage))]


def rank(stage, differs=()):
    place = 0
    for dim in stage:
        b = side(dim)
        place = 2 * place + (1 - b if dim in differs else b)
    return place


def greet(names):
    barrier = pltpu.get_barrier_semaphore()
    for name in names:
        pl.semaphore_signal(barrier, inc=1, device_id=neighbour(name), device_id_type=MESH)
    pl.semaphore_wait(barrier, len(names))


class Wire:
    def __init__(self, send_sem, recv_sem):
        self.send_sem, self.recv_sem = send_sem, recv_sem
        self.count, self.slots = 0, 0
        self.leaving = {}

    def slot(self):
        self.slots += 1
        return self.slots - 1

    def send(self, src, dst, name, slot=None):
        if slot is None:
            slot = self.slot()
        if slot in self.leaving:
            self.leaving.pop(slot).wait_send()
        copy = pltpu.make_async_remote_copy(
            src_ref=src,
            dst_ref=dst,
            send_sem=self.send_sem.at[slot],
            recv_sem=self.recv_sem.at[self.count],
            device_id=neighbour(name),
            device_id_type=MESH,
        )
        copy.start()
        self.count += 1
        assert self.count <= RECEIVES and slot < SENDS
        self.leaving[slot] = copy
        return copy

    def finish(self):
        for copy in self.leaving.values():
            copy.wait_send()
        self.leaving = {}
        self.slots = 0


def any_spec(n):
    return [pl.BlockSpec(memory_space=pl.ANY)] * n


def vmem_spec(n):
    return [pl.BlockSpec(memory_space=pltpu.VMEM)] * n


def normalise(value):
    centred = value - jnp.mean(value, axis=-1, keepdims=True)
    rstd = lax.rsqrt(jnp.mean(centred * centred, axis=-1, keepdims=True) + 1e-5)
    return centred * rstd, rstd


def normalise_back(grad_hat, hat, rstd):
    return rstd * (
        grad_hat
        - jnp.mean(grad_hat, axis=-1, keepdims=True)
        - hat * jnp.mean(grad_hat * hat, axis=-1, keepdims=True)
    )


def column_sum(value):
    return jnp.sum(value, axis=0, keepdims=True)


class Chains:
    def __init__(self):
        self.queue = []

    def add(self, *chains):
        for chain in chains:
            next(chain)
            self.queue.append(chain)

    def tick(self, n=1):
        for _ in range(min(n, len(self.queue))):
            chain = self.queue.pop(0)
            try:
                next(chain)
                self.queue.append(chain)
            except StopIteration:
                pass

    def drain(self):
        while self.queue:
            self.tick()


def layer_kernel(
    has_x,
    tokens, cot, wq_h, wk_h, wv_h, wo_h, up_h, down_h, table_h,
    segments, timesteps, gain_1, shift_1, gain_2, shift_2, out_bias_1, down_bias_1, query_bias_1, value_bias_1, up_bias_1,
    wg_h, sv_out, tg_out, res_out,
    xrow, xcross, table, cot2, wq, wk, wv, wo, up, down, bias,
    normed, normed_t, k_ref, v_ref, hot, s_buf, att, att_t, lse, q_ref, dkv, dq_ref, t_buf, part_top, part_sum,
    wg, acc, core_buf, step_buf, wg_out, t_out, t_core, t_acc, t_step, result2, sv_buf, sv_acc,
    send_sem, recv_sem, local_sem,
):
    dp, seq, mp = here()
    g = lax.div(seq, 4)
    pseq = flip(seq, 4)
    own, par = 2 * seq + mp, 2 * pseq + mp
    y, zl = bit(seq, 1), bit(seq, 2)
    d = normed.shape[1]
    length = normed.shape[0]
    pairs = d // PAIR
    step = 512
    steps = length // step
    nb = step // BLOCK
    ff = up.shape[1]
    half = ff // 2
    nq = 2 * BLOCK
    wire = Wire(send_sem, recv_sem)
    chains = Chains()
    kept = []

    def keep(src, dst):
        copy = pltpu.make_async_copy(src, dst, local_sem.at[len(kept)])
        copy.start()
        kept.append(copy)
        return copy

    def columns(ref):
        w = ref.shape[1] // 2
        return ref.at[:, pl.ds(pl.multiple_of(mp * w, w), w)]

    def rows(ref):
        w = ref.shape[0] // 2
        return ref.at[pl.ds(pl.multiple_of(mp * w, w), w)]

    def arrive(copies):
        for copy in copies:
            copy.wait_recv()

    chars = pl.ds(0, BLOCK)
    cross_kept = keep(tokens.at[1 - g], xcross.at[chars])
    own_kept = keep(tokens.at[g], xrow.at[own, chars])
    early_kept = [keep(table_h, table), keep(wk_h, columns(wk)), keep(wv_h, columns(wv)), keep(wq_h, columns(wq))]
    spans = segments[...].astype(F32)
    first_row = jnp.where(g == 0, spans[0:1, :], spans[1:2, :])
    second_row = jnp.where(g == 0, spans[1:2, :], spans[0:1, :])
    blank = jnp.zeros((ROWS_AT - SPANS_AT, d - BLOCK), F32)

    def span_rows(row):
        return jnp.concatenate([jnp.broadcast_to(row, (ROWS_AT - SPANS_AT, BLOCK)), blank], axis=1).astype(BF)

    xcross[SPANS_AT:, :] = span_rows(second_row)
    xrow[own, SPANS_AT:, :] = span_rows(first_row)

    def line(ref):
        return ref[...].astype(F32).reshape(1, ref.shape[0])

    bias[mp] = jnp.concatenate(
        [jnp.concatenate([line(query_bias_1), line(value_bias_1)], axis=1)]
        + [line(up_bias_1)[:, i * d : (i + 1) * d] for i in range(half // d)]
        + [jnp.zeros((8 - 1 - half // d, d), F32)],
        axis=0,
    )
    greet(("core", "y", "zl", "diag", "zh", ("zl", "zh")) + (("x", ("x", "y")) if has_x else ()))

    upper, lower = pl.ds(0, BLOCK // 2), pl.ds(BLOCK // 2, ROWS_AT - BLOCK // 2)
    cross_kept.wait()
    crossing = [wire.send(xcross.at[part], xrow.at[own, part], "zh") for part in (upper, lower)]
    own_kept.wait()
    first = {"y": wire.send(xrow.at[own], xrow.at[own], "y")}
    own_mate = wire.send(xrow.at[own], xrow.at[own], "core")
    early = [
        wire.send(wk_h, columns(wk), "core"),
        wire.send(wv_h, columns(wv), "core"),
        wire.send(wq_h, columns(wq), "core"),
        wire.send(bias.at[mp], bias.at[mp], "core"),
    ]
    late_kept = [
        keep(src, dst)
        for src, dst in ((wo_h, rows(wo)), (up_h, columns(up)), (down_h, rows(down)), (cot.at[g], cot2.at[0]))
    ]
    for copy in early_kept:
        copy.wait()

    t_buf[...] = jnp.zeros_like(t_buf)

    lane = lax.broadcasted_iota(jnp.int32, timesteps.shape, 1)
    moment = jnp.sum(jnp.where(lane == g, timesteps[...], 0).astype(F32), axis=1, keepdims=True)
    ids = lax.broadcasted_iota(jnp.int32, (8, table.shape[0]), 1).astype(F32)
    row_embed = dot(jnp.where(ids == moment, 1.0, 0.0).astype(BF), table[...], NN)[0:1, :]
    gain, shift = line(gain_1), line(shift_1)

    def hidden_of(block):
        return block.astype(F32) + row_embed

    def seg_column(b):
        return jnp.transpose(xrow[b, SPANS_AT:, 0:BLOCK].astype(F32))[:, 0:1]

    arrive(early)
    query_bias = jnp.concatenate([bias[0, 0:1, :256], bias[1, 0:1, :256]], axis=1)
    value_bias = jnp.concatenate([bias[0, 0:1, 256:], bias[1, 0:1, 256:]], axis=1)

    def project(s):
        n = 2 * BLOCK
        at = pl.ds(pl.multiple_of(s * n, n), n)
        hat, _ = normalise(hidden_of(xrow[pl.ds(2 * s, 2), 0:BLOCK, :].reshape(n, d)))
        low = (hat * gain + shift).astype(BF)
        normed[at, :] = low
        normed_t[:, at] = jnp.transpose(low)
        k_ref[at, :] = dot(low, wk[...], NN).astype(BF)
        v_ref[at, :] = (dot(low, wv[...], NN) + value_bias).astype(BF)
        spans = jnp.concatenate([seg_column(2 * s + i) for i in range(2)], axis=0)
        lanes = lax.broadcasted_iota(jnp.int32, (n, BLOCK), 1).astype(F32)
        hot[at, :] = jnp.where(spans == lanes, 1.0, 0.0).astype(BF)

    def beyond(base, name):
        return {"y": flip(base, 1), "zl": flip(base, 2), "diag": flip(flip(base, 1), 2)}[name]

    def to_mate(s):
        block = xrow.at[2 * s + mp]
        return wire.send(block, block, "core")

    own_mate.wait_recv()
    project(seq)
    for name in ("zl", "diag"):
        first[name] = wire.send(xrow.at[own], xrow.at[own], name)
    first["y"].wait_recv()
    mates = {"y": to_mate(beyond(seq, "y"))}
    second = {name: [] for name in PEERS}
    for copy, part in zip(crossing, (upper, lower)):
        copy.wait_recv()
        for name in PEERS:
            second[name].append(wire.send(xrow.at[par, part], xrow.at[par, part], name))
    par_mate = to_mate(pseq)
    mates["y"].wait_recv()
    project(beyond(seq, "y"))
    for name in ("zl", "diag"):
        first[name].wait_recv()
        mates[name] = to_mate(beyond(seq, name))
    late = [
        wire.send(src, dst, "core")
        for src, dst in ((wo_h, rows(wo)), (up_h, columns(up)), (down_h, rows(down)))
    ]
    late.append(wire.send(cot.at[1 - g], cot2.at[1], "zh"))
    par_mate.wait_recv()
    project(pseq)

    def query_rows(ref):
        return jnp.concatenate(
            [ref[pl.ds(pl.multiple_of(b * BLOCK, BLOCK), BLOCK), :] for b in (own, par)], axis=0
        )

    scale = 1.0 / math.sqrt(HEAD_DIM)
    query_low = (dot(query_rows(normed), wq[...], NN) + query_bias).astype(BF)
    q_ref[...] = (query_low.astype(F32) * scale).astype(BF)
    for name in ("zl", "diag"):
        mates[name].wait_recv()
        project(beyond(seq, name))

    spans_q = jnp.concatenate([seg_column(own), seg_column(par)], axis=0)
    lanes_q = lax.broadcasted_iota(jnp.int32, (nq, BLOCK), 1).astype(F32)
    other = jnp.where(spans_q == lanes_q, 0.0, MASKED).astype(BF)
    live = jnp.where(spans_q > 0.0, 1.0, 0.0)
    other2 = jnp.concatenate([other, other], axis=0)
    first_head = lax.broadcasted_iota(jnp.int32, (nq, PAIR), 1) < HEAD_DIM
    first_head_t = lax.broadcasted_iota(jnp.int32, (PAIR, nq), 0) < HEAD_DIM

    def split_heads(value):
        wide = value.astype(F32)
        return jnp.concatenate(
            [jnp.where(first_head, wide, 0.0), jnp.where(first_head, 0.0, wide)], axis=0
        ).astype(BF)

    def join_heads_t(value):
        return jnp.where(first_head_t, value[:, :nq], value[:, nq:])

    def lanes_of(p):
        return pl.ds(p * PAIR if isinstance(p, int) else pl.multiple_of(p * PAIR, PAIR), PAIR)

    def chunk(c):
        return pl.ds(c * step, step)

    def attend(p, places):
        at = lanes_of(p)
        query = jnp.concatenate([split_heads(q_ref[:, at]), other2], axis=1)
        top = jnp.full((8, 2 * nq), -3e38, F32)
        keys_at = [pl.ds(pl.multiple_of(s * nq, nq), nq) for s in places]
        for i, here_at in enumerate(keys_at):
            keys = jnp.concatenate([k_ref[here_at, at], hot[here_at, :]], axis=1)
            scores = dot(keys, query, NT)
            s_buf[pl.ds(i * nq, nq), :] = scores
            top = jnp.maximum(top, jnp.max(scores.reshape(nq // 8, 8, 2 * nq), axis=0))
        top = jnp.max(top, axis=0, keepdims=True)
        total = jnp.zeros((8, 2 * nq), F32)
        summed = jnp.zeros((PAIR, 2 * nq), F32)
        for i, here_at in enumerate(keys_at):
            weights = jnp.exp(s_buf[pl.ds(i * nq, nq), :] - top)
            total = total + jnp.sum(weights.reshape(nq // 8, 8, 2 * nq), axis=0)
            summed = summed + dot(v_ref[here_at, at], weights.astype(BF), TN)
        return top, jnp.sum(total, axis=0, keepdims=True), summed

    near = [seq] + [beyond(seq, name) for name in PEERS] + [pseq]
    def near_pair(p, carry):
        top, total, summed = attend(p, near)
        part_top[p, 0:1, :] = top
        part_top[p, 8:9, :] = total
        part_sum[p] = summed
        return carry

    lax.fori_loop(0, pairs, near_pair, 0)
    for name in PEERS:
        arrive(second[name])
        mates[name] = to_mate(beyond(pseq, name))
    for name in PEERS:
        mates[name].wait_recv()
        project(beyond(pseq, name))
    far = [beyond(pseq, name) for name in PEERS]
    def far_pair(p, carry):
        top, total, summed = attend(p, far)
        top_near = part_top[p, 0:1, :]
        top_all = jnp.maximum(top, top_near)
        weight, weight_near = jnp.exp(top - top_all), jnp.exp(top_near - top_all)
        total = total * weight + part_top[p, 8:9, :] * weight_near
        summed = summed * weight + part_sum[p] * weight_near
        joined = join_heads_t(summed / total)
        att_t[p] = joined
        att[:, lanes_of(p)] = jnp.transpose(joined)
        lse[p] = jnp.broadcast_to(top_all + jnp.log(total), (8, 2 * nq))
        return carry

    lax.fori_loop(0, pairs, far_pair, 0)

    for copy in late_kept:
        copy.wait()
    arrive(late)
    wire.finish()

    def stages_of(order):
        stages = [tuple(dim for dim in stage if has_x or dim != "x") for stage in order]
        return [stage for stage in stages if stage]

    def add_rows(out, out_at, terms, n):
        size = next(s for s in (256, 192, 128, 96, 64, 48, 32, 16) if n % s == 0)

        def one(i, carry):
            def at(base):
                return pl.ds(pl.multiple_of(base + i * size, size), size)

            values = [ref[at(base), :] for ref, base in terms]
            if len(values) == 2:
                out[at(out_at), :] = values[0] + values[1]
            else:
                out[at(out_at), :] = sum(value.astype(F32) for value in values).astype(BF)
            return carry

        lax.fori_loop(0, n // size, one, 0)

    def weights_chain(low, size, order):
        stages = stages_of(order)
        whole = pl.ds(low, size)
        used = low
        slots = [wire.slot() for _ in range(max(len(relations(stage)) for stage in stages))]
        copy = wire.send(wg.at[1 - mp, whole], core_buf.at[whole], "core", slots[0])
        yield
        copy.wait_recv()
        add_rows(acc, low, [(wg.at[mp], low), (core_buf, low)], size)
        for i, stage in enumerate(stages):
            size = size >> len(stage)
            terms, copies = [], []
            for slot, differs in zip(slots, relations(stage)):
                there = pl.ds(pl.multiple_of(low + rank(stage, differs) * size, size), size)
                copies.append(wire.send(acc.at[there], step_buf.at[pl.ds(used, size)], differs, slot))
                terms.append((step_buf, used))
                used += size
            yield
            arrive(copies)
            low = low + rank(stage) * size
            add_rows(wg_out if i == len(stages) - 1 else acc, low, [(acc, low)] + terms, size)
        for stage in reversed(stages):
            at = pl.ds(pl.multiple_of(low, size), size)
            copies = [wire.send(wg_out.at[at], wg_out.at[at], differs, slot) for slot, differs in zip(slots, relations(stage))]
            yield
            arrive(copies)
            low = low - rank(stage) * size
            size = size << len(stage)
        keep(wg_out.at[whole], wg_h.at[whole])

    def start_weights(wave):
        chains.add(*[weights_chain(low, size, order) for low, size, order in wave])

    finished = len(kept)
    mixed = (att[...] * live).astype(BF)
    hidden_q = hidden_of(jnp.concatenate([xrow[own, 0:BLOCK, :], xrow[par, 0:BLOCK, :]], axis=0))
    residual = hidden_q + dot(mixed, wo[...], NN) + line(out_bias_1)
    gain2, shift2 = line(gain_2), line(shift_2)
    hat2, rstd2 = normalise(residual)
    normed2 = (hat2 * gain2 + shift2).astype(BF)
    cotangent = jnp.concatenate([cot2[0], cot2[1]], axis=0)
    unit_result = residual + line(down_bias_1)
    grad_normed2 = jnp.zeros((nq, d), F32)
    sv = sv_acc.at[0]
    for r in range(half // step):
        for m in range(2):
            j = (m * half + r * step) // step
            units = pl.ds(j * step, step)
            inner = dot(normed2, up[:, units], NN) + bias[m, 1 + r : 2 + r, :]
            square = inner * inner
            bent = jnp.tanh(GELU_C * inner * (1.0 + GELU_A * square))
            activated = (0.5 * inner * (1.0 + bent)).astype(BF)
            unit_result = unit_result + dot(activated, down[units, :], NN)
            slope = 0.5 * (1.0 + bent) + 0.5 * inner * (1.0 - bent * bent) * (
                GELU_C * (1.0 + 3.0 * GELU_A * square)
            )
            grad_inner = (dot(cotangent, down[units, :], NT) * slope).astype(BF)
            grad_normed2 = grad_normed2 + dot(grad_inner, up[:, units], NT)
            down_grad = dot(activated, cotangent, TN).astype(BF)
            up_grad = dot(normed2, grad_inner, TN).astype(BF)
            for b in range(2):
                at = slice(b * 256, (b + 1) * 256)
                wg[m, pl.ds(2048 * r + b * 512, 512), :] = up_grad[:, at]
                wg[m, pl.ds(2048 * r + 1024 + b * 512, 512), :] = down_grad[:, at]
            sv[6 + j : 7 + j, :] = column_sum(grad_inner.astype(F32))
        start_weights((WAVE_ONE, WAVE_TWO)[r])
        chains.tick(3 * r)
    out = unit_result.astype(BF)
    result2[0] = out[:BLOCK]
    result2[1] = out[BLOCK:]
    result_back = wire.send(result2.at[1], res_out.at[g], "zh")
    res_out[g] = out[:BLOCK]
    cot_f = cotangent.astype(F32)
    grad_residual = cot_f + normalise_back(grad_normed2 * gain2, hat2, rstd2)
    sv[2:3, :] = column_sum(grad_normed2 * hat2)
    sv[3:4, :] = column_sum(grad_normed2)
    sv[4:5, :] = column_sum(grad_residual)
    sv[5:6, :] = column_sum(cot_f)
    branch_grad = grad_residual.astype(BF)
    out_grad = dot(mixed, branch_grad, TN).astype(BF)
    for m in range(2):
        for b in range(2):
            wg[m, pl.ds(OUT_AT + b * 256, 256), :] = out_grad[m * 256 : (m + 1) * 256, b * 256 : (b + 1) * 256]
    start_weights(WAVE_THREE)
    att[...] = dot(branch_grad, wo[...], NT).astype(BF).astype(F32) * live

    def back(p):
        at = lanes_of(p)
        query = split_heads(q_ref[:, at])
        query_wide = jnp.concatenate([query, other2], axis=1)
        heads = att[:, at]
        grads = split_heads(heads)
        product = jnp.transpose(heads) * att_t[p]
        delta = jnp.concatenate([column_sum(product[:HEAD_DIM]), column_sum(product[HEAD_DIM:])], axis=1)
        log_total = lse[p][0:1, :]
        query_grad = jnp.zeros((PAIR, 2 * nq), F32)
        for c in range(steps):
            keys = k_ref[chunk(c), at]
            scores = dot(jnp.concatenate([keys, hot[chunk(c), :]], axis=1), query_wide, NT)
            probs = jnp.exp(scores - log_total)
            grad_probs = dot(v_ref[chunk(c), at], grads, NT)
            grad_scores = (probs * (grad_probs - delta)).astype(BF)
            dkv[p, chunk(c), 0:PAIR] = dot(grad_scores, query, NN).astype(BF)
            dkv[p, chunk(c), PAIR:] = dot(probs.astype(BF), grads, NN).astype(BF)
            query_grad = query_grad + dot(keys, grad_scores, TN)
            chains.tick(2)
        joined = join_heads_t(query_grad) * scale
        dq_ref[:, at] = jnp.transpose(joined).astype(BF)

    normed_q = query_rows(normed)
    for n in range(2):
        for m in range(2):
            back(2 * m + n)
        for m in range(2):
            p = 2 * m + n
            pair_grad = dot(normed_t[...], dkv[p], NN)
            wg[m, pl.ds(PAIR_AT[n], d), :] = pair_grad.astype(BF)
            pair_grad = dot(normed_q, dq_ref[:, lanes_of(p)], TN).astype(BF)
            wg[m, pl.ds(PAIR_AT[n] + d, d // 2), 0:PAIR] = pair_grad[: d // 2]
            wg[m, pl.ds(PAIR_AT[n] + d, d // 2), PAIR:] = pair_grad[d // 2 :]
        start_weights(WAVE_PAIR[n])

    def tokens_back(grad_normed, block):
        hat, rstd = normalise(hidden_of(block))
        return (
            normalise_back(grad_normed * gain, hat, rstd),
            column_sum(grad_normed * hat),
            column_sum(grad_normed),
        )

    query_grad = dq_ref[...]
    token_grad, gain_sum, shift_sum = tokens_back(
        dot(query_grad, wq[...], NT), jnp.concatenate([xrow[own, 0:BLOCK, :], xrow[par, 0:BLOCK, :]], axis=0)
    )
    token_grad = token_grad + grad_residual
    t_buf[own] = token_grad[:BLOCK]
    t_buf[par] = token_grad[BLOCK:]
    token_sum = column_sum(token_grad)
    value_sums = [jnp.zeros((1, PAIR), F32) for _ in range(pairs)]

    def tokens_chain(hi, dims):
        slot = wire.slot()
        one, two = dims
        copy = wire.send(t_out.at[hi, :, :, 1 - mp], t_core.at[hi], "core", slot)
        yield
        copy.wait_recv()
        for b in range(2):
            for c in range(2):
                t_acc[hi, b, c] = t_out[hi, b, c, mp] + t_core[hi, b, c]
        if one == "y":
            copy = wire.send(t_acc.at[hi, :, 1 - y], t_step.at[hi, 0:2], "y", slot)
        else:
            copy = wire.send(t_acc.at[hi, 1 - zl], t_step.at[hi, 0:2], "zl", slot)
        yield
        copy.wait_recv()
        if one == "y":
            for i in range(2):
                t_acc[hi, i, y] += t_step[hi, i]
            copy = wire.send(t_acc.at[hi, 1 - zl, y], t_step.at[hi, 2], "zl", slot)
        else:
            for i in range(2):
                t_acc[hi, zl, i] += t_step[hi, i]
            copy = wire.send(t_acc.at[hi, zl, 1 - y], t_step.at[hi, 2], "y", slot)
        yield
        copy.wait_recv()
        t_acc[hi, zl, y] += t_step[hi, 2]
        if two == "zl":
            copy = wire.send(t_acc.at[hi, zl, y], tg_out.at[g], "zh", slot)
            yield
            copy.wait_recv()
        else:
            tg_out[g] = t_acc[hi, zl, y]

    for hi, dims in ((1 - g, ("y", "zl")), (g, ("zl", "y"))):
        for c in range(2):
            place = 2 * hi + c
            at = pl.ds(pl.multiple_of(place * step, step), step)
            grad_normed = jnp.zeros((step, d), F32)
            for p in range(pairs):
                pair_grad = dkv[p, at, :]
                both = jnp.concatenate([wk[:, lanes_of(p)], wv[:, lanes_of(p)]], axis=1)
                grad_normed = grad_normed + dot(pair_grad, both, NT)
                value_sums[p] = value_sums[p] + column_sum(pair_grad[:, PAIR:].astype(F32))
            blocks_at = pl.ds(place * nb, nb)
            token_grad, a, b = tokens_back(grad_normed, xrow[blocks_at, 0:BLOCK, :].reshape(step, d))
            gain_sum, shift_sum, token_sum = gain_sum + a, shift_sum + b, token_sum + column_sum(token_grad)
            token_grad = t_buf[blocks_at] + token_grad.reshape(nb, BLOCK, d)
            for i in range(nb):
                t_out[hi, c, i // 2, i % 2] = token_grad[i].astype(BF)
            chains.tick()
        chains.add(tokens_chain(hi, dims))
    value_sum = jnp.concatenate(value_sums, axis=1)

    sv[0:1, :] = gain_sum
    sv[1:2, :] = shift_sum
    sv[10:11, :] = column_sum(query_grad.astype(F32))
    sv[11:12, :] = value_sum
    sv[12:16, :] = jnp.zeros((4, d), F32)
    slot_lane = lax.broadcasted_iota(jnp.int32, (1, d), 1)
    speaks = jnp.logical_and(lax.rem(seq, 4) == 0, mp == 0)
    my_slot = 2 * dp + g
    sv[12:13, :] = jnp.where(slot_lane == jnp.where(speaks, my_slot, -1), moment, 0.0)
    slot = lax.broadcasted_iota(jnp.int32, (sv.shape[0] - SV_TABLE, d), 0) == my_slot
    sv[SV_TABLE:, :] = jnp.where(slot, token_sum, 0.0)

    def vectors_chain():
        slots = [wire.slot() for _ in range(3)]
        stages = [("core",)] + stages_of((("x", "y"), ("zl", "zh")))
        for i, stage in enumerate(stages):
            copies = [
                wire.send(sv_acc.at[i], sv_buf.at[i, k], differs, slots[k])
                for k, differs in enumerate(relations(stage))
            ]
            yield
            arrive(copies)
            total = sv_acc[i] + sv_buf[i, 0]
            if len(copies) == 3:
                total = total + (sv_buf[i, 1] + sv_buf[i, 2])
            sv_acc[i + 1] = total
        sv_out[...] = sv_acc[len(stages)]
        result_back.wait_recv()

    chains.add(vectors_chain())
    chains.drain()
    wire.finish()
    for copy in kept[finished:]:
        copy.wait()


def layer(big, small, has_x, sv_rows):
    shape = jax.ShapeDtypeStruct
    tokens, up, table = big[0], big[6], big[8]
    d = tokens.shape[2]
    blocks = 2 * lax.axis_size("seq")
    length = blocks * BLOCK
    nq = 2 * BLOCK
    pairs = d // PAIR
    ff = 2 * up.shape[1]
    block = (BLOCK, d)
    vmem = pltpu.VMEM
    return pl.pallas_call(
        functools.partial(layer_kernel, has_x),
        out_shape=(
            shape((WG_ROWS, 256), BF),
            shape((sv_rows, d), F32),
            shape(tokens.shape, BF),
            shape(tokens.shape, BF),
        ),
        in_specs=any_spec(len(big)) + vmem_spec(len(small)),
        out_specs=tuple(any_spec(1) + vmem_spec(3)),
        scratch_shapes=[
            vmem((blocks, ROWS_AT, d), BF),
            vmem((ROWS_AT, d), BF),
            vmem(table.shape, BF),
            vmem((2,) + block, BF),
            vmem((d, d), BF),
            vmem((d, d), BF),
            vmem((d, d), BF),
            vmem((d, d), BF),
            vmem((d, ff), BF),
            vmem((ff, d), BF),
            vmem((2, 8, d), F32),
            vmem((length, d), BF),
            vmem((d, length), BF),
            vmem((length, d), BF),
            vmem((length, d), BF),
            vmem((length, BLOCK), BF),
            vmem((5 * nq, 2 * nq), F32),
            vmem((nq, d), F32),
            vmem((pairs, PAIR, nq), F32),
            vmem((pairs, 8, 2 * nq), F32),
            vmem((nq, d), BF),
            vmem((pairs, length, 2 * PAIR), BF),
            vmem((nq, d), BF),
            vmem((blocks,) + block, F32),
            vmem((pairs, 16, 2 * nq), F32),
            vmem((pairs, PAIR, 2 * nq), F32),
            vmem((2, WG_ROWS, 256), BF),
            vmem((WG_ROWS, 256), BF),
            vmem((WG_ROWS, 256), BF),
            vmem((WG_ROWS, 256), BF),
            vmem((WG_ROWS, 256), BF),
            vmem((2, 2, 2, 2) + block, BF),
            vmem((2, 2, 2) + block, BF),
            vmem((2, 2, 2) + block, BF),
            vmem((2, 3) + block, BF),
            vmem((2,) + block, BF),
            vmem((3, 3, sv_rows, d), F32),
            vmem((4, sv_rows, d), F32),
            pltpu.SemaphoreType.DMA((SENDS,)),
            pltpu.SemaphoreType.DMA((RECEIVES,)),
            pltpu.SemaphoreType.DMA((KEEPS,)),
        ],
        compiler_params=pltpu.CompilerParams(
            collective_id=0, has_side_effects=True, vmem_limit_bytes=62 << 20
        ),
        name="layer",
    )(*big, *small)


def finish_kernel(
    table_rows, wg, tg, res, sv,
    res_o, tg_o, table_o, wq_o, wk_o, wv_o, wo_o, up_o, down_o,
    gain_1, shift_1, query_bias, value_bias, out_bias, gain_2, shift_2, up_bias, down_bias,
    wg_v, tg_v, res_v, tg_f, table_v, wq_v, wk_v, wv_v, wo_v, up_v, down_v,
    in_sem, out_sem,
):
    mp = lax.axis_index("mp")
    leaving = []
    rows = 1024
    parts = WG_ROWS // rows

    def fetch(src, dst, n):
        copy = pltpu.make_async_copy(src, dst, in_sem.at[n])
        copy.start()
        return copy

    def leave(src, dst):
        copy = pltpu.make_async_copy(src, dst, out_sem.at[len(leaving)])
        copy.start()
        leaving.append(copy)

    coming = [fetch(wg.at[pl.ds(i * rows, rows)], wg_v.at[pl.ds(i * rows, rows)], i) for i in range(parts)]
    coming_tg, coming_res = fetch(tg, tg_v, parts), fetch(res, res_v, parts + 1)
    ids = sv[12:13, 0:128]
    spread = jnp.where(lax.broadcasted_iota(jnp.int32, (table_v.shape[0], 128), 0).astype(F32) == ids, 1.0, 0.0)
    sums = jnp.concatenate([sv[SV_TABLE:, :], jnp.zeros((128 - (sv.shape[0] - SV_TABLE), sv.shape[1]), F32)], axis=0)
    table_v[...] = lax.dot_general(spread, sums, NN, precision=lax.Precision.HIGHEST, preferred_element_type=F32)
    leave(table_v, table_o)

    def flat(ref, value):
        ref[...] = value.reshape(ref.shape)

    for ref, r in ((gain_1, 0), (shift_1, 1), (gain_2, 2), (shift_2, 3), (out_bias, 4), (down_bias, 5)):
        flat(ref, sv[r : r + 1, :])
    for ref, r in ((query_bias, 10), (value_bias, 11)):
        flat(ref, jnp.where(mp == 0, sv[r : r + 1, 0:256], sv[r : r + 1, 256:512]))
    flat(up_bias, jnp.where(mp == 0, jnp.concatenate([sv[6:7, :], sv[7:8, :]], axis=1), jnp.concatenate([sv[8:9, :], sv[9:10, :]], axis=1)))

    def take(at, n):
        return wg_v[at : at + n, :].astype(F32)

    for i in range(parts):
        coming[i].wait()
        if i in (0, 2):
            for b in range(2):
                up_v[:, i * 256 + b * 256 : i * 256 + (b + 1) * 256] = take(i * rows + b * 512, 512)
            leave(up_v.at[:, pl.ds(i * 256, 512)], up_o.at[:, pl.ds(i * 256, 512)])
        elif i in (1, 3):
            at = pl.ds(i // 2 * 512, 512)
            for b in range(2):
                down_v[at, b * 256 : (b + 1) * 256] = take(i * rows + b * 512, 512)
            leave(down_v.at[at], down_o.at[at])
        elif i == 4:
            for b in range(2):
                wo_v[:, b * 256 : (b + 1) * 256] = take(OUT_AT + b * 256, 256)
            leave(wo_v, wo_o)
        else:
            for n, at in enumerate(PAIR_AT):
                lanes = slice(n * PAIR, (n + 1) * PAIR)
                both, query = take(at, 512), take(at + 512, 256)
                wk_v[:, lanes] = both[:, :PAIR]
                wv_v[:, lanes] = both[:, PAIR:]
                wq_v[0:256, lanes] = query[:, :PAIR]
                wq_v[256:512, lanes] = query[:, PAIR:]
            leave(wk_v, wk_o)
            leave(wv_v, wv_o)
            leave(wq_v, wq_o)
    coming_res.wait()
    leave(res_v, res_o)
    coming_tg.wait()
    tg_f[...] = tg_v[...].astype(F32)
    leave(tg_f, tg_o)
    for copy in leaving:
        copy.wait()


def finish(wg, tg, res, sv, table_rows, steps, units):
    shape = jax.ShapeDtypeStruct
    d = sv.shape[1]
    big = [
        shape(res.shape, BF), shape(tg.shape, F32), shape((steps, d), F32),
        shape((d, d // 2), F32), shape((d, d // 2), F32), shape((d, d // 2), F32), shape((d // 2, d), F32),
        shape((d, units), F32), shape((units, d), F32),
    ]
    small = [shape((n,), F32) for n in (d, d, d // 2, d // 2, d, d, d, units, d)]
    vmem = pltpu.VMEM
    return pl.pallas_call(
        functools.partial(finish_kernel, table_rows),
        out_shape=tuple(big + small),
        in_specs=any_spec(3) + vmem_spec(1),
        out_specs=tuple(any_spec(len(big)) + vmem_spec(len(small))),
        scratch_shapes=[vmem(wg.shape, BF), vmem(tg.shape, BF), vmem(res.shape, BF), vmem(tg.shape, F32)]
        + [vmem(item.shape, F32) for item in big[2:]]
        + [pltpu.SemaphoreType.DMA((8,)), pltpu.SemaphoreType.DMA((12,))],
        compiler_params=pltpu.CompilerParams(vmem_limit_bytes=62 << 20),
        name="finish",
    )(wg, tg, res, sv)


def local(
    n_dp, tokens, segments, timesteps, step_table, first_gain, first_shift, query_weight, query_bias,
    key_weight, value_weight, value_bias, out_weight, out_bias, second_gain, second_shift,
    up_weight, up_bias, down_weight, down_bias, cotangent,
):
    table_rows = tokens.shape[0] * n_dp
    sv_rows = SV_TABLE + -(-table_rows // 8) * 8
    wg, sv, token_grad, result = layer(
        (tokens, cotangent, query_weight, key_weight, value_weight, out_weight, up_weight, down_weight, step_table),
        (segments, timesteps[None, :], first_gain, first_shift, second_gain, second_shift, out_bias, down_bias,
         query_bias, value_bias, up_bias),
        n_dp == 2, sv_rows,
    )
    if n_dp != 2:
        wg, sv = lax.psum((wg, sv), "dp")
    (result, token_grad, table_grad, wq, wk, wv, wo, up, down,
     gain_1, shift_1, bq, bv, bo, gain_2, shift_2, bu, bd) = finish(
        wg, token_grad, result, sv, table_rows, step_table.shape[0], up_weight.shape[1]
    )
    return (
        result, token_grad, table_grad, gain_1, shift_1, wq, bq, wk, wv, bv, wo, bo, gain_2, shift_2, up, bu, down, bd
    )


def solution(mesh):
    rows, chars, whole = P("dp", ("seq", "mp"), None), P("dp", ("seq", "mp")), P()
    columns, split, tall = P(None, "mp"), P("mp"), P("mp", None)
    in_specs = (
        rows, chars, P("dp"), whole, whole, whole, columns, split, columns, columns, split, tall,
        whole, whole, whole, columns, split, tall, whole, rows,
    )
    out_specs = (
        rows, rows, whole, whole, whole, columns, split, columns, columns, split, tall,
        whole, whole, whole, columns, split, tall, whole,
    )
    return jax.shard_map(
        functools.partial(local, mesh.shape["dp"]),
        mesh=mesh,
        in_specs=in_specs,
        out_specs=out_specs,
        check_vma=False,
    )
```

```python
import functools
import math

import jax
import jax.numpy as jnp
from jax import lax
from jax.experimental import pallas as pl
from jax.experimental.pallas import tpu as pltpu
from jax.sharding import PartitionSpec as P

MESH = pl.DeviceIdType.MESH
BF, F32 = jnp.bfloat16, jnp.float32
NN = (((1,), (0,)), ((), ()))
NT = (((1,), (1,)), ((), ()))
TN = (((0,), (0,)), ((), ()))
HEAD_DIM = 64
BLOCK = 128
PAIR = 2 * HEAD_DIM
MASKED = -1e30
GELU_A = 0.044715
GELU_C = math.sqrt(2.0 / math.pi)
OUT_AT, PAIR_AT, PAIR_ROWS, WG_ROWS = 4096, (4608, 5376), 768, 6144
SV_TABLE = 16
RECEIVES, SENDS, KEEPS = 132, 48, 30
SPANS_AT, ROWS_AT = 128, 144
PEERS = ("y", "zl", "diag")
PARTS = {
    "a": (
        ("a0", 0, 768, (("zl",), ("x", "y",), ("zh",),)),
        ("a1", 768, 768, (("x",), ("y",), ("zl", "zh",),)),
    ),
    "b": (
        ("b0", 1536, 768, (("x",), ("y",), ("zl", "zh",),)),
        ("b1", 2304, 768, (("x", "y",), ("zl", "zh",),)),
    ),
    "c": (
        ("c0", 3072, 768, (("x",), ("zl", "zh",), ("y",),)),
        ("c1", 3840, 768, (("y",), ("x",), ("zl",), ("zh",),)),
    ),
    "p": (
        ("p0", 4608, 768, (("x",), ("y",), ("zl", "zh",),)),
    ),
    "q": (
        ("q0", 5376, 768, (("x", "y",), ("zl", "zh",),)),
    ),
}
SCRIPT = (
    (),
    ("a0", "a1", "b0", "b1",),
    (),
    (),
    ("a0", "a1", "c0", "c1",),
    (),
    ("b0",),
    (),
    ("a1",),
    (),
    ("b1",),
    (),
    ("a0", "a1", "c1", "b0", "p0", "a0", "b1", "c0",),
    ("a1", "c1",),
    (),
    ("b0",),
    ("a0",),
    ("p0", "b1", "a1",),
    ("c1",),
    ("a0",),
    (),
    ("c0", "p0",),
    ("b0", "q0", "c1",),
    ("a0", "b1", "c0",),
    ("p0", "a1", "c1",),
    ("t0", "b0",),
    (
        "p0", "c1", "q0", "s", "c0", "t1", "p0", "b0", "t0", "c1", "q0", "s", "c0", "t1", "q0",
        "p0", "t0", "s", "c0", "t1", "c1", "t0", "q0",
    ),
)


def dot(a, b, dims):
    return lax.dot_general(a, b, dims, preferred_element_type=F32)


def bit(v, n):
    return lax.rem(lax.div(v, n), 2)


def flip(v, n):
    return v + n - 2 * n * bit(v, n)


def here():
    return lax.axis_index("dp"), lax.axis_index("seq"), lax.axis_index("mp")


def neighbour(name):
    dp, seq, mp = here()
    dims = {"diag": ("y", "zl")}.get(name, name if isinstance(name, tuple) else (name,))
    for dim in dims:
        if dim == "core":
            mp = 1 - mp
        elif dim == "x":
            dp = 1 - dp
        else:
            seq = flip(seq, {"y": 1, "zl": 2, "zh": 4}[dim])
    return (dp, seq, mp)


def side(name):
    dp, seq, mp = here()
    return {"x": dp, "y": bit(seq, 1), "zl": bit(seq, 2), "zh": bit(seq, 4), "core": mp}[name]


def relations(stage):
    return [tuple(dim for i, dim in enumerate(stage) if k >> i & 1) for k in range(1, 1 << len(stage))]


def rank(stage, differs=()):
    place = 0
    for dim in stage:
        b = side(dim)
        place = 2 * place + (1 - b if dim in differs else b)
    return place


def greet(names):
    barrier = pltpu.get_barrier_semaphore()
    for name in names:
        pl.semaphore_signal(barrier, inc=1, device_id=neighbour(name), device_id_type=MESH)
    pl.semaphore_wait(barrier, len(names))


class Wire:
    def __init__(self, send_sem, recv_sem):
        self.send_sem, self.recv_sem = send_sem, recv_sem
        self.count, self.slots = 0, 0
        self.leaving = {}

    def slot(self):
        self.slots += 1
        return self.slots - 1

    def send(self, src, dst, name, slot=None):
        if slot is None:
            slot = self.slot()
        if slot in self.leaving:
            self.leaving.pop(slot).wait_send()
        copy = pltpu.make_async_remote_copy(
            src_ref=src,
            dst_ref=dst,
            send_sem=self.send_sem.at[slot],
            recv_sem=self.recv_sem.at[self.count],
            device_id=neighbour(name),
            device_id_type=MESH,
        )
        copy.start()
        self.count += 1
        assert self.count <= RECEIVES and slot < SENDS
        self.leaving[slot] = copy
        return copy

    def finish(self):
        for copy in self.leaving.values():
            copy.wait_send()
        self.leaving = {}
        self.slots = 0


def any_spec(n):
    return [pl.BlockSpec(memory_space=pl.ANY)] * n


def vmem_spec(n):
    return [pl.BlockSpec(memory_space=pltpu.VMEM)] * n


def normalise(value):
    centred = value - jnp.mean(value, axis=-1, keepdims=True)
    rstd = lax.rsqrt(jnp.mean(centred * centred, axis=-1, keepdims=True) + 1e-5)
    return centred * rstd, rstd


def normalise_back(grad_hat, hat, rstd):
    return rstd * (
        grad_hat
        - jnp.mean(grad_hat, axis=-1, keepdims=True)
        - hat * jnp.mean(grad_hat * hat, axis=-1, keepdims=True)
    )


def column_sum(value):
    return jnp.sum(value, axis=0, keepdims=True)


class Chains:
    def __init__(self):
        self.running = {}
        self.place = 0

    def add(self, name, chain):
        next(chain)
        self.running[name] = chain

    def advance(self, name):
        if name in self.running and next(self.running[name], "ended") == "ended":
            del self.running[name]

    def tick(self):
        for name in SCRIPT[self.place]:
            self.advance(name)
        self.place += 1

    def drain(self):
        assert self.place == len(SCRIPT) - 1
        self.tick()
        while self.running:
            for name in tuple(self.running):
                self.advance(name)


def layer_kernel(
    has_x,
    tokens, cot, wq_h, wk_h, wv_h, wo_h, up_h, down_h, table_h,
    segments, timesteps, gain_1, shift_1, gain_2, shift_2, out_bias_1, down_bias_1, query_bias_1, value_bias_1, up_bias_1,
    wg_h, sv_out, tg_out, res_out,
    xrow, xcross, table, cot2, wq, wk, wv, wo, up, down, bias,
    normed, normed_t, k_ref, v_ref, hot, s_buf, att, att_t, lse, q_ref, dkv, dq_ref, t_buf, part_top, part_sum,
    wg, acc, core_buf, step_buf, wg_out, t_out, t_core, t_acc, t_step, result2, sv_buf, sv_acc,
    send_sem, recv_sem, local_sem,
):
    dp, seq, mp = here()
    g = lax.div(seq, 4)
    pseq = flip(seq, 4)
    own, par = 2 * seq + mp, 2 * pseq + mp
    y, zl = bit(seq, 1), bit(seq, 2)
    d = normed.shape[1]
    length = normed.shape[0]
    pairs = d // PAIR
    step = 512
    steps = length // step
    nb = step // BLOCK
    ff = up.shape[1]
    half = ff // 2
    nq = 2 * BLOCK
    wire = Wire(send_sem, recv_sem)
    chains = Chains()
    kept = []

    def keep(src, dst):
        copy = pltpu.make_async_copy(src, dst, local_sem.at[len(kept)])
        copy.start()
        kept.append(copy)
        return copy

    def columns(ref):
        w = ref.shape[1] // 2
        return ref.at[:, pl.ds(pl.multiple_of(mp * w, w), w)]

    def rows(ref):
        w = ref.shape[0] // 2
        return ref.at[pl.ds(pl.multiple_of(mp * w, w), w)]

    def arrive(copies):
        for copy in copies:
            copy.wait_recv()

    chars = pl.ds(0, BLOCK)
    cross_kept = keep(tokens.at[1 - g], xcross.at[chars])
    own_kept = keep(tokens.at[g], xrow.at[own, chars])
    early_kept = [keep(table_h, table), keep(wk_h, columns(wk)), keep(wv_h, columns(wv)), keep(wq_h, columns(wq))]
    spans = segments[...].astype(F32)
    first_row = jnp.where(g == 0, spans[0:1, :], spans[1:2, :])
    second_row = jnp.where(g == 0, spans[1:2, :], spans[0:1, :])
    blank = jnp.zeros((ROWS_AT - SPANS_AT, d - BLOCK), F32)

    def span_rows(row):
        return jnp.concatenate([jnp.broadcast_to(row, (ROWS_AT - SPANS_AT, BLOCK)), blank], axis=1).astype(BF)

    xcross[SPANS_AT:, :] = span_rows(second_row)
    xrow[own, SPANS_AT:, :] = span_rows(first_row)

    def line(ref):
        return ref[...].astype(F32).reshape(1, ref.shape[0])

    bias[mp] = jnp.concatenate(
        [jnp.concatenate([line(query_bias_1), line(value_bias_1)], axis=1)]
        + [line(up_bias_1)[:, i * d : (i + 1) * d] for i in range(half // d)]
        + [jnp.zeros((8 - 1 - half // d, d), F32)],
        axis=0,
    )
    greet(("core", "y", "zl", "diag", "zh", ("zl", "zh")) + (("x", ("x", "y")) if has_x else ()))

    upper, lower = pl.ds(0, BLOCK // 2), pl.ds(BLOCK // 2, ROWS_AT - BLOCK // 2)
    cross_kept.wait()
    crossing = [wire.send(xcross.at[part], xrow.at[own, part], "zh") for part in (upper, lower)]
    own_kept.wait()
    first = {name: wire.send(xrow.at[own], xrow.at[own], name) for name in PEERS}
    own_mate = wire.send(xrow.at[own], xrow.at[own], "core")
    early = [
        wire.send(wk_h, columns(wk), "core"),
        wire.send(wv_h, columns(wv), "core"),
        wire.send(wq_h, columns(wq), "core"),
        wire.send(bias.at[mp], bias.at[mp], "core"),
    ]
    late_kept = [
        keep(src, dst)
        for src, dst in ((wo_h, rows(wo)), (up_h, columns(up)), (down_h, rows(down)), (cot.at[g], cot2.at[0]))
    ]
    for copy in early_kept:
        copy.wait()

    t_buf[...] = jnp.zeros_like(t_buf)

    lane = lax.broadcasted_iota(jnp.int32, timesteps.shape, 1)
    moment = jnp.sum(jnp.where(lane == g, timesteps[...], 0).astype(F32), axis=1, keepdims=True)
    ids = lax.broadcasted_iota(jnp.int32, (8, table.shape[0]), 1).astype(F32)
    row_embed = dot(jnp.where(ids == moment, 1.0, 0.0).astype(BF), table[...], NN)[0:1, :]
    gain, shift = line(gain_1), line(shift_1)

    def hidden_of(block):
        return block.astype(F32) + row_embed

    def seg_column(b):
        return jnp.transpose(xrow[b, SPANS_AT:, 0:BLOCK].astype(F32))[:, 0:1]

    arrive(early)
    query_bias = jnp.concatenate([bias[0, 0:1, :256], bias[1, 0:1, :256]], axis=1)
    value_bias = jnp.concatenate([bias[0, 0:1, 256:], bias[1, 0:1, 256:]], axis=1)

    def project(s):
        n = 2 * BLOCK
        at = pl.ds(pl.multiple_of(s * n, n), n)
        hat, _ = normalise(hidden_of(xrow[pl.ds(2 * s, 2), 0:BLOCK, :].reshape(n, d)))
        low = (hat * gain + shift).astype(BF)
        normed[at, :] = low
        normed_t[:, at] = jnp.transpose(low)
        k_ref[at, :] = dot(low, wk[...], NN).astype(BF)
        v_ref[at, :] = (dot(low, wv[...], NN) + value_bias).astype(BF)
        spans = jnp.concatenate([seg_column(2 * s + i) for i in range(2)], axis=0)
        lanes = lax.broadcasted_iota(jnp.int32, (n, BLOCK), 1).astype(F32)
        hot[at, :] = jnp.where(spans == lanes, 1.0, 0.0).astype(BF)

    def beyond(base, name):
        return {"y": flip(base, 1), "zl": flip(base, 2), "diag": flip(flip(base, 1), 2)}[name]

    def to_mate(s):
        block = xrow.at[2 * s + mp]
        return wire.send(block, block, "core")

    own_mate.wait_recv()
    project(seq)
    first["y"].wait_recv()
    mates = {"y": to_mate(beyond(seq, "y"))}
    second = {name: [] for name in PEERS}
    for copy, part in zip(crossing, (upper, lower)):
        copy.wait_recv()
        for name in PEERS:
            second[name].append(wire.send(xrow.at[par, part], xrow.at[par, part], name))
    par_mate = to_mate(pseq)
    mates["y"].wait_recv()
    project(beyond(seq, "y"))
    for name in ("zl", "diag"):
        first[name].wait_recv()
        mates[name] = to_mate(beyond(seq, name))
    late = [
        wire.send(src, dst, "core")
        for src, dst in ((wo_h, rows(wo)), (up_h, columns(up)), (down_h, rows(down)))
    ]
    late.append(wire.send(cot.at[1 - g], cot2.at[1], "zh"))
    par_mate.wait_recv()
    project(pseq)

    def query_rows(ref):
        return jnp.concatenate(
            [ref[pl.ds(pl.multiple_of(b * BLOCK, BLOCK), BLOCK), :] for b in (own, par)], axis=0
        )

    scale = 1.0 / math.sqrt(HEAD_DIM)
    query_low = (dot(query_rows(normed), wq[...], NN) + query_bias).astype(BF)
    q_ref[...] = (query_low.astype(F32) * scale).astype(BF)
    for name in ("zl", "diag"):
        mates[name].wait_recv()
        project(beyond(seq, name))

    spans_q = jnp.concatenate([seg_column(own), seg_column(par)], axis=0)
    lanes_q = lax.broadcasted_iota(jnp.int32, (nq, BLOCK), 1).astype(F32)
    other = jnp.where(spans_q == lanes_q, 0.0, MASKED).astype(BF)
    live = jnp.where(spans_q > 0.0, 1.0, 0.0)
    other2 = jnp.concatenate([other, other], axis=0)
    first_head = lax.broadcasted_iota(jnp.int32, (nq, PAIR), 1) < HEAD_DIM
    first_head_t = lax.broadcasted_iota(jnp.int32, (PAIR, nq), 0) < HEAD_DIM

    def split_heads(value):
        wide = value.astype(F32)
        return jnp.concatenate(
            [jnp.where(first_head, wide, 0.0), jnp.where(first_head, 0.0, wide)], axis=0
        ).astype(BF)

    def join_heads_t(value):
        return jnp.where(first_head_t, value[:, :nq], value[:, nq:])

    def lanes_of(p):
        return pl.ds(p * PAIR if isinstance(p, int) else pl.multiple_of(p * PAIR, PAIR), PAIR)

    def chunk(c):
        return pl.ds(c * step, step)

    def attend(p, places):
        at = lanes_of(p)
        query = jnp.concatenate([split_heads(q_ref[:, at]), other2], axis=1)
        top = jnp.full((8, 2 * nq), -3e38, F32)
        keys_at = [pl.ds(pl.multiple_of(s * nq, nq), nq) for s in places]
        for i, here_at in enumerate(keys_at):
            keys = jnp.concatenate([k_ref[here_at, at], hot[here_at, :]], axis=1)
            scores = dot(keys, query, NT)
            s_buf[pl.ds(i * nq, nq), :] = scores
            top = jnp.maximum(top, jnp.max(scores.reshape(nq // 8, 8, 2 * nq), axis=0))
        top = jnp.max(top, axis=0, keepdims=True)
        total = jnp.zeros((8, 2 * nq), F32)
        summed = jnp.zeros((PAIR, 2 * nq), F32)
        for i, here_at in enumerate(keys_at):
            weights = jnp.exp(s_buf[pl.ds(i * nq, nq), :] - top)
            total = total + jnp.sum(weights.reshape(nq // 8, 8, 2 * nq), axis=0)
            summed = summed + dot(v_ref[here_at, at], weights.astype(BF), TN)
        return top, jnp.sum(total, axis=0, keepdims=True), summed

    near = [seq] + [beyond(seq, name) for name in PEERS] + [pseq]
    def near_pair(p, carry):
        top, total, summed = attend(p, near)
        part_top[p, 0:1, :] = top
        part_top[p, 8:9, :] = total
        part_sum[p] = summed
        return carry

    lax.fori_loop(0, pairs // 2, near_pair, 0)
    for name in PEERS:
        arrive(second[name])
        mates[name] = to_mate(beyond(pseq, name))
    lax.fori_loop(pairs // 2, pairs, near_pair, 0)
    for name in PEERS:
        mates[name].wait_recv()
        project(beyond(pseq, name))
    far = [beyond(pseq, name) for name in PEERS]
    def far_pair(p, carry):
        top, total, summed = attend(p, far)
        top_near = part_top[p, 0:1, :]
        top_all = jnp.maximum(top, top_near)
        weight, weight_near = jnp.exp(top - top_all), jnp.exp(top_near - top_all)
        total = total * weight + part_top[p, 8:9, :] * weight_near
        summed = summed * weight + part_sum[p] * weight_near
        joined = join_heads_t(summed / total)
        att_t[p] = joined
        att[:, lanes_of(p)] = jnp.transpose(joined)
        lse[p] = jnp.broadcast_to(top_all + jnp.log(total), (8, 2 * nq))
        return carry

    lax.fori_loop(0, pairs, far_pair, 0)

    for copy in late_kept:
        copy.wait()
    arrive(late)
    wire.finish()

    def stages_of(order):
        stages = [tuple(dim for dim in stage if has_x or dim != "x") for stage in order]
        return [stage for stage in stages if stage]

    def add_rows(out, out_at, terms, n):
        size = next(s for s in (256, 192, 128, 96, 64, 48, 32, 16) if n % s == 0)

        def one(i, carry):
            def at(base):
                return pl.ds(pl.multiple_of(base + i * size, size), size)

            values = [ref[at(base), :] for ref, base in terms]
            if len(values) == 2:
                out[at(out_at), :] = values[0] + values[1]
            else:
                out[at(out_at), :] = sum(value.astype(F32) for value in values).astype(BF)
            return carry

        lax.fori_loop(0, n // size, one, 0)

    def weights_chain(low, size, order):
        stages = stages_of(order)
        whole = pl.ds(low, size)
        used = low
        slots = [wire.slot() for _ in range(max(len(relations(stage)) for stage in stages))]
        copy = wire.send(wg.at[1 - mp, whole], core_buf.at[whole], "core", slots[0])
        yield
        copy.wait_recv()
        add_rows(acc, low, [(wg.at[mp], low), (core_buf, low)], size)
        for i, stage in enumerate(stages):
            size = size >> len(stage)
            terms, copies = [], []
            for slot, differs in zip(slots, relations(stage)):
                there = pl.ds(pl.multiple_of(low + rank(stage, differs) * size, size), size)
                copies.append(wire.send(acc.at[there], step_buf.at[pl.ds(used, size)], differs, slot))
                terms.append((step_buf, used))
                used += size
            yield
            arrive(copies)
            low = low + rank(stage) * size
            add_rows(wg_out if i == len(stages) - 1 else acc, low, [(acc, low)] + terms, size)
        for stage in reversed(stages):
            at = pl.ds(pl.multiple_of(low, size), size)
            copies = [wire.send(wg_out.at[at], wg_out.at[at], differs, slot) for slot, differs in zip(slots, relations(stage))]
            yield
            arrive(copies)
            low = low - rank(stage) * size
            size = size << len(stage)
        keep(wg_out.at[whole], wg_h.at[whole])

    def start_weights(wave):
        for name, low, size, order in PARTS[wave]:
            chains.add(name, weights_chain(low, size, order))

    finished = len(kept)
    mixed = (att[...] * live).astype(BF)
    hidden_q = hidden_of(jnp.concatenate([xrow[own, 0:BLOCK, :], xrow[par, 0:BLOCK, :]], axis=0))
    residual = hidden_q + dot(mixed, wo[...], NN) + line(out_bias_1)
    gain2, shift2 = line(gain_2), line(shift_2)
    hat2, rstd2 = normalise(residual)
    normed2 = (hat2 * gain2 + shift2).astype(BF)
    cotangent = jnp.concatenate([cot2[0], cot2[1]], axis=0)
    unit_result = residual + line(down_bias_1)
    grad_normed2 = jnp.zeros((nq, d), F32)
    sv = sv_acc.at[0]
    for r in range(half // step):
        for m in range(2):
            j = (m * half + r * step) // step
            units = pl.ds(j * step, step)
            inner = dot(normed2, up[:, units], NN) + bias[m, 1 + r : 2 + r, :]
            square = inner * inner
            bent = jnp.tanh(GELU_C * inner * (1.0 + GELU_A * square))
            activated = (0.5 * inner * (1.0 + bent)).astype(BF)
            unit_result = unit_result + dot(activated, down[units, :], NN)
            slope = 0.5 * (1.0 + bent) + 0.5 * inner * (1.0 - bent * bent) * (
                GELU_C * (1.0 + 3.0 * GELU_A * square)
            )
            grad_inner = (dot(cotangent, down[units, :], NT) * slope).astype(BF)
            grad_normed2 = grad_normed2 + dot(grad_inner, up[:, units], NT)
            down_grad = dot(activated, cotangent, TN).astype(BF)
            up_grad = dot(normed2, grad_inner, TN).astype(BF)
            for b in range(2):
                at = slice(b * 256, (b + 1) * 256)
                wg[m, pl.ds(2048 * r + b * 512, 512), :] = up_grad[:, at]
                wg[m, pl.ds(2048 * r + 1024 + b * 512, 512), :] = down_grad[:, at]
            sv[6 + j : 7 + j, :] = column_sum(grad_inner.astype(F32))
            if r == 1 and m == 0:
                chains.tick()
        start_weights("ab"[r])
        if r == 1:
            chains.tick()
    out = unit_result.astype(BF)
    result2[0] = out[:BLOCK]
    result2[1] = out[BLOCK:]
    result_back = wire.send(result2.at[1], res_out.at[g], "zh")
    res_out[g] = out[:BLOCK]
    chains.tick()
    cot_f = cotangent.astype(F32)
    grad_residual = cot_f + normalise_back(grad_normed2 * gain2, hat2, rstd2)
    sv[2:3, :] = column_sum(grad_normed2 * hat2)
    sv[3:4, :] = column_sum(grad_normed2)
    sv[4:5, :] = column_sum(grad_residual)
    sv[5:6, :] = column_sum(cot_f)
    branch_grad = grad_residual.astype(BF)
    out_grad = dot(mixed, branch_grad, TN).astype(BF)
    for m in range(2):
        for b in range(2):
            wg[m, pl.ds(OUT_AT + b * 256, 256), :] = out_grad[m * 256 : (m + 1) * 256, b * 256 : (b + 1) * 256]
    start_weights("c")
    chains.tick()
    att[...] = dot(branch_grad, wo[...], NT).astype(BF).astype(F32) * live

    def back(p):
        at = lanes_of(p)
        query = split_heads(q_ref[:, at])
        query_wide = jnp.concatenate([query, other2], axis=1)
        heads = att[:, at]
        grads = split_heads(heads)
        product = jnp.transpose(heads) * att_t[p]
        delta = jnp.concatenate([column_sum(product[:HEAD_DIM]), column_sum(product[HEAD_DIM:])], axis=1)
        log_total = lse[p][0:1, :]
        query_grad = jnp.zeros((PAIR, 2 * nq), F32)
        for c in range(steps):
            keys = k_ref[chunk(c), at]
            scores = dot(jnp.concatenate([keys, hot[chunk(c), :]], axis=1), query_wide, NT)
            probs = jnp.exp(scores - log_total)
            grad_probs = dot(v_ref[chunk(c), at], grads, NT)
            grad_scores = (probs * (grad_probs - delta)).astype(BF)
            dkv[p, chunk(c), 0:PAIR] = dot(grad_scores, query, NN).astype(BF)
            dkv[p, chunk(c), PAIR:] = dot(probs.astype(BF), grads, NN).astype(BF)
            query_grad = query_grad + dot(keys, grad_scores, TN)
            chains.tick()
        joined = join_heads_t(query_grad) * scale
        dq_ref[:, at] = jnp.transpose(joined).astype(BF)

    normed_q = query_rows(normed)
    for n in range(2):
        for m in range(2):
            back(2 * m + n)
        for m in range(2):
            p = 2 * m + n
            pair_grad = dot(normed_t[...], dkv[p], NN)
            wg[m, pl.ds(PAIR_AT[n], d), :] = pair_grad.astype(BF)
            pair_grad = dot(normed_q, dq_ref[:, lanes_of(p)], TN).astype(BF)
            wg[m, pl.ds(PAIR_AT[n] + d, d // 2), 0:PAIR] = pair_grad[: d // 2]
            wg[m, pl.ds(PAIR_AT[n] + d, d // 2), PAIR:] = pair_grad[d // 2 :]
        start_weights("pq"[n])
        chains.tick()

    def tokens_back(grad_normed, block):
        hat, rstd = normalise(hidden_of(block))
        return (
            normalise_back(grad_normed * gain, hat, rstd),
            column_sum(grad_normed * hat),
            column_sum(grad_normed),
        )

    query_grad = dq_ref[...]
    token_grad, gain_sum, shift_sum = tokens_back(
        dot(query_grad, wq[...], NT), jnp.concatenate([xrow[own, 0:BLOCK, :], xrow[par, 0:BLOCK, :]], axis=0)
    )
    token_grad = token_grad + grad_residual
    t_buf[own] = token_grad[:BLOCK]
    t_buf[par] = token_grad[BLOCK:]
    token_sum = column_sum(token_grad)
    value_sums = [jnp.zeros((1, PAIR), F32) for _ in range(pairs)]

    def tokens_chain(hi, one, leaves):
        slot = wire.slot()
        copy = wire.send(t_out.at[hi, :, :, 1 - mp], t_core.at[hi], "core", slot)
        yield
        copy.wait_recv()
        for b in range(2):
            for c in range(2):
                t_acc[hi, b, c] = t_out[hi, b, c, mp] + t_core[hi, b, c]
        if one == "y":
            copy = wire.send(t_acc.at[hi, :, 1 - y], t_step.at[hi, 0:2], "y", slot)
        else:
            copy = wire.send(t_acc.at[hi, 1 - zl], t_step.at[hi, 0:2], "zl", slot)
        yield
        copy.wait_recv()
        if one == "y":
            for i in range(2):
                t_acc[hi, i, y] += t_step[hi, i]
            copy = wire.send(t_acc.at[hi, 1 - zl, y], t_step.at[hi, 2], "zl", slot)
        else:
            for i in range(2):
                t_acc[hi, zl, i] += t_step[hi, i]
            copy = wire.send(t_acc.at[hi, zl, 1 - y], t_step.at[hi, 2], "y", slot)
        yield
        copy.wait_recv()
        t_acc[hi, zl, y] += t_step[hi, 2]
        if leaves:
            copy = wire.send(t_acc.at[hi, zl, y], tg_out.at[g], "zh", slot)
            yield
            copy.wait_recv()
        else:
            tg_out[g] = t_acc[hi, zl, y]

    for n, (hi, one) in enumerate(((1 - g, "zl"), (g, "y"))):
        for c in range(2):
            place = 2 * hi + c
            at = pl.ds(pl.multiple_of(place * step, step), step)
            grad_normed = jnp.zeros((step, d), F32)
            for p in range(pairs):
                pair_grad = dkv[p, at, :]
                both = jnp.concatenate([wk[:, lanes_of(p)], wv[:, lanes_of(p)]], axis=1)
                grad_normed = grad_normed + dot(pair_grad, both, NT)
                value_sums[p] = value_sums[p] + column_sum(pair_grad[:, PAIR:].astype(F32))
            blocks_at = pl.ds(place * nb, nb)
            token_grad, a, b = tokens_back(grad_normed, xrow[blocks_at, 0:BLOCK, :].reshape(step, d))
            gain_sum, shift_sum, token_sum = gain_sum + a, shift_sum + b, token_sum + column_sum(token_grad)
            token_grad = t_buf[blocks_at] + token_grad.reshape(nb, BLOCK, d)
            for i in range(nb):
                t_out[hi, c, i // 2, i % 2] = token_grad[i].astype(BF)
            chains.tick()
        chains.add(("t0", "t1")[n], tokens_chain(hi, one, n == 0))
    value_sum = jnp.concatenate(value_sums, axis=1)

    sv[0:1, :] = gain_sum
    sv[1:2, :] = shift_sum
    sv[10:11, :] = column_sum(query_grad.astype(F32))
    sv[11:12, :] = value_sum
    sv[12:16, :] = jnp.zeros((4, d), F32)
    slot_lane = lax.broadcasted_iota(jnp.int32, (1, d), 1)
    speaks = jnp.logical_and(lax.rem(seq, 4) == 0, mp == 0)
    my_slot = 2 * dp + g
    sv[12:13, :] = jnp.where(slot_lane == jnp.where(speaks, my_slot, -1), moment, 0.0)
    slot = lax.broadcasted_iota(jnp.int32, (sv.shape[0] - SV_TABLE, d), 0) == my_slot
    sv[SV_TABLE:, :] = jnp.where(slot, token_sum, 0.0)

    def vectors_chain():
        slots = [wire.slot() for _ in range(3)]
        stages = [("core",)] + stages_of((("x", "y"), ("zl", "zh")))
        for i, stage in enumerate(stages):
            copies = [
                wire.send(sv_acc.at[i], sv_buf.at[i, k], differs, slots[k])
                for k, differs in enumerate(relations(stage))
            ]
            yield
            arrive(copies)
            total = sv_acc[i] + sv_buf[i, 0]
            if len(copies) == 3:
                total = total + (sv_buf[i, 1] + sv_buf[i, 2])
            sv_acc[i + 1] = total
        sv_out[...] = sv_acc[len(stages)]
        result_back.wait_recv()

    chains.add("s", vectors_chain())
    chains.drain()
    wire.finish()
    for copy in kept[finished:]:
        copy.wait()


def layer(big, small, has_x, sv_rows):
    shape = jax.ShapeDtypeStruct
    tokens, up, table = big[0], big[6], big[8]
    d = tokens.shape[2]
    blocks = 2 * lax.axis_size("seq")
    length = blocks * BLOCK
    nq = 2 * BLOCK
    pairs = d // PAIR
    ff = 2 * up.shape[1]
    block = (BLOCK, d)
    vmem = pltpu.VMEM
    return pl.pallas_call(
        functools.partial(layer_kernel, has_x),
        out_shape=(
            shape((WG_ROWS, 256), BF),
            shape((sv_rows, d), F32),
            shape(tokens.shape, BF),
            shape(tokens.shape, BF),
        ),
        in_specs=any_spec(len(big)) + vmem_spec(len(small)),
        out_specs=tuple(any_spec(1) + vmem_spec(3)),
        scratch_shapes=[
            vmem((blocks, ROWS_AT, d), BF),
            vmem((ROWS_AT, d), BF),
            vmem(table.shape, BF),
            vmem((2,) + block, BF),
            vmem((d, d), BF),
            vmem((d, d), BF),
            vmem((d, d), BF),
            vmem((d, d), BF),
            vmem((d, ff), BF),
            vmem((ff, d), BF),
            vmem((2, 8, d), F32),
            vmem((length, d), BF),
            vmem((d, length), BF),
            vmem((length, d), BF),
            vmem((length, d), BF),
            vmem((length, BLOCK), BF),
            vmem((5 * nq, 2 * nq), F32),
            vmem((nq, d), F32),
            vmem((pairs, PAIR, nq), F32),
            vmem((pairs, 8, 2 * nq), F32),
            vmem((nq, d), BF),
            vmem((pairs, length, 2 * PAIR), BF),
            vmem((nq, d), BF),
            vmem((blocks,) + block, F32),
            vmem((pairs, 16, 2 * nq), F32),
            vmem((pairs, PAIR, 2 * nq), F32),
            vmem((2, WG_ROWS, 256), BF),
            vmem((WG_ROWS, 256), BF),
            vmem((WG_ROWS, 256), BF),
            vmem((WG_ROWS, 256), BF),
            vmem((WG_ROWS, 256), BF),
            vmem((2, 2, 2, 2) + block, BF),
            vmem((2, 2, 2) + block, BF),
            vmem((2, 2, 2) + block, BF),
            vmem((2, 3) + block, BF),
            vmem((2,) + block, BF),
            vmem((3, 3, sv_rows, d), F32),
            vmem((4, sv_rows, d), F32),
            pltpu.SemaphoreType.DMA((SENDS,)),
            pltpu.SemaphoreType.DMA((RECEIVES,)),
            pltpu.SemaphoreType.DMA((KEEPS,)),
        ],
        compiler_params=pltpu.CompilerParams(
            collective_id=0, has_side_effects=True, vmem_limit_bytes=62 << 20
        ),
        name="layer",
    )(*big, *small)


def finish_kernel(
    table_rows, wg, tg, res, sv,
    res_o, tg_o, table_o, wq_o, wk_o, wv_o, wo_o, up_o, down_o,
    gain_1, shift_1, query_bias, value_bias, out_bias, gain_2, shift_2, up_bias, down_bias,
    wg_v, tg_v, res_v, tg_f, table_v, wq_v, wk_v, wv_v, wo_v, up_v, down_v,
    in_sem, out_sem,
):
    mp = lax.axis_index("mp")
    leaving = []
    rows = 1024
    parts = WG_ROWS // rows

    def fetch(src, dst, n):
        copy = pltpu.make_async_copy(src, dst, in_sem.at[n])
        copy.start()
        return copy

    def leave(src, dst):
        copy = pltpu.make_async_copy(src, dst, out_sem.at[len(leaving)])
        copy.start()
        leaving.append(copy)

    coming = [fetch(wg.at[pl.ds(i * rows, rows)], wg_v.at[pl.ds(i * rows, rows)], i) for i in range(parts)]
    coming_tg, coming_res = fetch(tg, tg_v, parts), fetch(res, res_v, parts + 1)
    ids = sv[12:13, 0:128]
    spread = jnp.where(lax.broadcasted_iota(jnp.int32, (table_v.shape[0], 128), 0).astype(F32) == ids, 1.0, 0.0)
    sums = jnp.concatenate([sv[SV_TABLE:, :], jnp.zeros((128 - (sv.shape[0] - SV_TABLE), sv.shape[1]), F32)], axis=0)
    table_v[...] = lax.dot_general(spread, sums, NN, precision=lax.Precision.HIGHEST, preferred_element_type=F32)
    leave(table_v, table_o)

    def flat(ref, value):
        ref[...] = value.reshape(ref.shape)

    for ref, r in ((gain_1, 0), (shift_1, 1), (gain_2, 2), (shift_2, 3), (out_bias, 4), (down_bias, 5)):
        flat(ref, sv[r : r + 1, :])
    for ref, r in ((query_bias, 10), (value_bias, 11)):
        flat(ref, jnp.where(mp == 0, sv[r : r + 1, 0:256], sv[r : r + 1, 256:512]))
    flat(up_bias, jnp.where(mp == 0, jnp.concatenate([sv[6:7, :], sv[7:8, :]], axis=1), jnp.concatenate([sv[8:9, :], sv[9:10, :]], axis=1)))

    def take(at, n):
        return wg_v[at : at + n, :].astype(F32)

    for i in range(parts):
        coming[i].wait()
        if i in (0, 2):
            for b in range(2):
                up_v[:, i * 256 + b * 256 : i * 256 + (b + 1) * 256] = take(i * rows + b * 512, 512)
            leave(up_v.at[:, pl.ds(i * 256, 512)], up_o.at[:, pl.ds(i * 256, 512)])
        elif i in (1, 3):
            at = pl.ds(i // 2 * 512, 512)
            for b in range(2):
                down_v[at, b * 256 : (b + 1) * 256] = take(i * rows + b * 512, 512)
            leave(down_v.at[at], down_o.at[at])
        elif i == 4:
            for b in range(2):
                wo_v[:, b * 256 : (b + 1) * 256] = take(OUT_AT + b * 256, 256)
            leave(wo_v, wo_o)
        else:
            for n, at in enumerate(PAIR_AT):
                lanes = slice(n * PAIR, (n + 1) * PAIR)
                both, query = take(at, 512), take(at + 512, 256)
                wk_v[:, lanes] = both[:, :PAIR]
                wv_v[:, lanes] = both[:, PAIR:]
                wq_v[0:256, lanes] = query[:, :PAIR]
                wq_v[256:512, lanes] = query[:, PAIR:]
            leave(wk_v, wk_o)
            leave(wv_v, wv_o)
            leave(wq_v, wq_o)
    coming_res.wait()
    leave(res_v, res_o)
    coming_tg.wait()
    tg_f[...] = tg_v[...].astype(F32)
    leave(tg_f, tg_o)
    for copy in leaving:
        copy.wait()


def finish(wg, tg, res, sv, table_rows, steps, units):
    shape = jax.ShapeDtypeStruct
    d = sv.shape[1]
    big = [
        shape(res.shape, BF), shape(tg.shape, F32), shape((steps, d), F32),
        shape((d, d // 2), F32), shape((d, d // 2), F32), shape((d, d // 2), F32), shape((d // 2, d), F32),
        shape((d, units), F32), shape((units, d), F32),
    ]
    small = [shape((n,), F32) for n in (d, d, d // 2, d // 2, d, d, d, units, d)]
    vmem = pltpu.VMEM
    return pl.pallas_call(
        functools.partial(finish_kernel, table_rows),
        out_shape=tuple(big + small),
        in_specs=any_spec(3) + vmem_spec(1),
        out_specs=tuple(any_spec(len(big)) + vmem_spec(len(small))),
        scratch_shapes=[vmem(wg.shape, BF), vmem(tg.shape, BF), vmem(res.shape, BF), vmem(tg.shape, F32)]
        + [vmem(item.shape, F32) for item in big[2:]]
        + [pltpu.SemaphoreType.DMA((8,)), pltpu.SemaphoreType.DMA((12,))],
        compiler_params=pltpu.CompilerParams(vmem_limit_bytes=62 << 20),
        name="finish",
    )(wg, tg, res, sv)


def local(
    n_dp, tokens, segments, timesteps, step_table, first_gain, first_shift, query_weight, query_bias,
    key_weight, value_weight, value_bias, out_weight, out_bias, second_gain, second_shift,
    up_weight, up_bias, down_weight, down_bias, cotangent,
):
    table_rows = tokens.shape[0] * n_dp
    sv_rows = SV_TABLE + -(-table_rows // 8) * 8
    wg, sv, token_grad, result = layer(
        (tokens, cotangent, query_weight, key_weight, value_weight, out_weight, up_weight, down_weight, step_table),
        (segments, timesteps[None, :], first_gain, first_shift, second_gain, second_shift, out_bias, down_bias,
         query_bias, value_bias, up_bias),
        n_dp == 2, sv_rows,
    )
    if n_dp != 2:
        wg, sv = lax.psum((wg, sv), "dp")
    (result, token_grad, table_grad, wq, wk, wv, wo, up, down,
     gain_1, shift_1, bq, bv, bo, gain_2, shift_2, bu, bd) = finish(
        wg, token_grad, result, sv, table_rows, step_table.shape[0], up_weight.shape[1]
    )
    return (
        result, token_grad, table_grad, gain_1, shift_1, wq, bq, wk, wv, bv, wo, bo, gain_2, shift_2, up, bu, down, bd
    )


def solution(mesh):
    rows, chars, whole = P("dp", ("seq", "mp"), None), P("dp", ("seq", "mp")), P()
    columns, split, tall = P(None, "mp"), P("mp"), P("mp", None)
    in_specs = (
        rows, chars, P("dp"), whole, whole, whole, columns, split, columns, columns, split, tall,
        whole, whole, whole, columns, split, tall, whole, rows,
    )
    out_specs = (
        rows, rows, whole, whole, whole, columns, split, columns, columns, split, tall,
        whole, whole, whole, columns, split, tall, whole,
    )
    return jax.shard_map(
        functools.partial(local, mesh.shape["dp"]),
        mesh=mesh,
        in_specs=in_specs,
        out_specs=out_specs,
        check_vma=False,
    )
```

```python
import functools
import math

import jax
import jax.numpy as jnp
from jax import lax
from jax.experimental import pallas as pl
from jax.experimental.pallas import tpu as pltpu
from jax.sharding import PartitionSpec as P

MESH = pl.DeviceIdType.MESH
BF, F32 = jnp.bfloat16, jnp.float32
NN = (((1,), (0,)), ((), ()))
NT = (((1,), (1,)), ((), ()))
TN = (((0,), (0,)), ((), ()))
HEAD_DIM = 64
BLOCK = 128
PAIR = 2 * HEAD_DIM
MASKED = -1e30
GELU_A = 0.044715
GELU_C = math.sqrt(2.0 / math.pi)
OUT_AT, PAIR_AT, PAIR_ROWS, WG_ROWS = 4096, (4608, 5376), 768, 6144
SV_TABLE = 16
RECEIVES, SENDS, KEEPS = 146, 44, 22
SPAN_ROWS = 16
PEERS = ("y", "zl", "diag")
PARTS = {
    "a": (
        ("a0", 0, 768, (("x",), ("y",), ("zl", "zh",),)),
        ("a1", 768, 768, (("zl",), ("x", "y",), ("zh",),)),
    ),
    "b": (
        ("b0", 1536, 768, (("x",), ("zl",), ("y",), ("zh",),)),
        ("b1", 2304, 768, (("zl",), ("x", "y",), ("zh",),)),
    ),
    "c": (
        ("c0", 3072, 768, (("x", "y",), ("zl", "zh",),)),
        ("c1", 3840, 768, (("x",), ("zl",), ("y",), ("zh",),)),
    ),
    "p": (
        ("p0", 4608, 768, (("y",), ("x",), ("zl", "zh",),)),
    ),
    "q": (
        ("q0", 5376, 768, (("x", "y",), ("zl", "zh",),)),
    ),
}
SCRIPT = (
    (),
    ("a0", "a1", "b0", "b1",),
    (),
    (),
    ("a0", "a1", "c0", "c1",),
    ("a0", "b1", "b0", "a1",),
    (),
    (),
    ("a0",),
    ("b0", "a1", "c0",),
    (),
    ("a0", "b0",),
    ("a1", "c1",),
    ("p0", "a0", "b1", "c0", "b0",),
    ("a1", "c1",),
    ("b1",),
    (),
    (),
    ("c0", "p0", "a0", "b0",),
    ("c1",),
    (),
    ("a1", "b1",),
    ("q0", "c0", "c1", "b0",),
    ("p0",),
    ("c1",),
    ("b1", "t0", "b0",),
    (
        "p0", "q0", "s", "c1", "t1", "b1", "b0", "p0", "t0", "q0", "s", "c1", "p0", "t0", "q0",
        "t1", "c1", "s", "p0", "t0", "t1", "q0",
    ),
)


def dot(a, b, dims):
    return lax.dot_general(a, b, dims, preferred_element_type=F32)


def bit(v, n):
    return lax.rem(lax.div(v, n), 2)


def flip(v, n):
    return v + n - 2 * n * bit(v, n)


def here():
    return lax.axis_index("dp"), lax.axis_index("seq"), lax.axis_index("mp")


def neighbour(name):
    dp, seq, mp = here()
    dims = {"diag": ("y", "zl")}.get(name, name if isinstance(name, tuple) else (name,))
    for dim in dims:
        if dim == "core":
            mp = 1 - mp
        elif dim == "x":
            dp = 1 - dp
        else:
            seq = flip(seq, {"y": 1, "zl": 2, "zh": 4}[dim])
    return (dp, seq, mp)


def side(name):
    dp, seq, mp = here()
    return {"x": dp, "y": bit(seq, 1), "zl": bit(seq, 2), "zh": bit(seq, 4), "core": mp}[name]


def relations(stage):
    return [tuple(dim for i, dim in enumerate(stage) if k >> i & 1) for k in range(1, 1 << len(stage))]


def rank(stage, differs=()):
    place = 0
    for dim in stage:
        b = side(dim)
        place = 2 * place + (1 - b if dim in differs else b)
    return place


def greet(names):
    barrier = pltpu.get_barrier_semaphore()
    for name in names:
        pl.semaphore_signal(barrier, inc=1, device_id=neighbour(name), device_id_type=MESH)
    pl.semaphore_wait(barrier, len(names))


class Wire:
    def __init__(self, send_sem, recv_sem):
        self.send_sem, self.recv_sem = send_sem, recv_sem
        self.count, self.slots = 0, 0
        self.leaving = {}

    def slot(self):
        self.slots += 1
        return self.slots - 1

    def send(self, src, dst, name, slot=None):
        if slot is None:
            slot = self.slot()
        if slot in self.leaving:
            self.leaving.pop(slot).wait_send()
        copy = pltpu.make_async_remote_copy(
            src_ref=src,
            dst_ref=dst,
            send_sem=self.send_sem.at[slot],
            recv_sem=self.recv_sem.at[self.count],
            device_id=neighbour(name),
            device_id_type=MESH,
        )
        copy.start()
        self.count += 1
        assert self.count <= RECEIVES and slot < SENDS
        self.leaving[slot] = copy
        return copy

    def finish(self):
        for copy in self.leaving.values():
            copy.wait_send()
        self.leaving = {}
        self.slots = 0


def any_spec(n):
    return [pl.BlockSpec(memory_space=pl.ANY)] * n


def vmem_spec(n):
    return [pl.BlockSpec(memory_space=pltpu.VMEM)] * n


def normalise(value):
    centred = value - jnp.mean(value, axis=-1, keepdims=True)
    rstd = lax.rsqrt(jnp.mean(centred * centred, axis=-1, keepdims=True) + 1e-5)
    return centred * rstd, rstd


def normalise_back(grad_hat, hat, rstd):
    return rstd * (
        grad_hat
        - jnp.mean(grad_hat, axis=-1, keepdims=True)
        - hat * jnp.mean(grad_hat * hat, axis=-1, keepdims=True)
    )


def column_sum(value):
    return jnp.sum(value, axis=0, keepdims=True)


class Chains:
    def __init__(self):
        self.running = {}
        self.place = 0

    def add(self, name, chain):
        next(chain)
        self.running[name] = chain

    def advance(self, name):
        if name in self.running and next(self.running[name], "ended") == "ended":
            del self.running[name]

    def tick(self):
        for name in SCRIPT[self.place]:
            self.advance(name)
        self.place += 1

    def drain(self):
        assert self.place == len(SCRIPT) - 1
        self.tick()
        while self.running:
            for name in tuple(self.running):
                self.advance(name)


def layer_kernel(
    has_x,
    tokens, cot, wq_h, wk_h, wv_h, wo_h, up_h, down_h, table_h,
    segments, timesteps, gain_1, shift_1, gain_2, shift_2, out_bias_1, down_bias_1, query_bias_1, value_bias_1, up_bias_1,
    wg_h, sv_out, tg_out, res_out,
    xrow, span, xcross, span_cross, table, cot2, wq, wk, wv, wo, up, down, bias,
    normed, normed_t, k_ref, v_ref, hot, s_buf, att, att_t, lse, q_ref, dkv, dq_ref, t_buf, part_top, part_sum,
    wg, acc, core_buf, step_buf, wg_out, t_out, t_core, t_acc, t_step, result2, sv_buf, sv_acc,
    send_sem, recv_sem, local_sem,
):
    dp, seq, mp = here()
    g = lax.div(seq, 4)
    pseq = flip(seq, 4)
    own, par = 2 * seq + mp, 2 * pseq + mp
    y, zl = bit(seq, 1), bit(seq, 2)
    d = normed.shape[1]
    length = normed.shape[0]
    pairs = d // PAIR
    step = 512
    steps = length // step
    nb = step // BLOCK
    ff = up.shape[1]
    half = ff // 2
    nq = 2 * BLOCK
    wire = Wire(send_sem, recv_sem)
    chains = Chains()
    kept = []

    def keep(src, dst):
        copy = pltpu.make_async_copy(src, dst, local_sem.at[len(kept)])
        copy.start()
        kept.append(copy)
        return copy

    def columns(ref):
        w = ref.shape[1] // 2
        return ref.at[:, pl.ds(pl.multiple_of(mp * w, w), w)]

    def rows(ref):
        w = ref.shape[0] // 2
        return ref.at[pl.ds(pl.multiple_of(mp * w, w), w)]

    def arrive(copies):
        for copy in copies:
            copy.wait_recv()

    cross_kept = keep(tokens.at[1 - g], xcross)
    own_kept = keep(tokens.at[g], xrow.at[own])
    early_kept = [keep(table_h, table), keep(wk_h, columns(wk)), keep(wv_h, columns(wv)), keep(wq_h, columns(wq))]
    spans = segments[...].astype(F32)
    first_row = jnp.where(g == 0, spans[0:1, :], spans[1:2, :])
    second_row = jnp.where(g == 0, spans[1:2, :], spans[0:1, :])
    span_cross[...] = jnp.broadcast_to(second_row, (SPAN_ROWS, BLOCK)).astype(BF)
    span[own] = jnp.broadcast_to(first_row, (SPAN_ROWS, BLOCK)).astype(BF)

    def line(ref):
        return ref[...].astype(F32).reshape(1, ref.shape[0])

    bias[mp] = jnp.concatenate(
        [jnp.concatenate([line(query_bias_1), line(value_bias_1)], axis=1)]
        + [line(up_bias_1)[:, i * d : (i + 1) * d] for i in range(half // d)]
        + [jnp.zeros((8 - 1 - half // d, d), F32)],
        axis=0,
    )
    greet(("core", "y", "zl", "diag", "zh", ("zl", "zh")) + (("x", ("x", "y")) if has_x else ()))

    def pass_on(block, name):
        return [
            wire.send(span.at[block], span.at[block], name),
            wire.send(xrow.at[block], xrow.at[block], name),
        ]

    halves = pl.ds(0, BLOCK // 2), pl.ds(BLOCK // 2, BLOCK // 2)
    crossing_span = wire.send(span_cross, span.at[own], "zh")
    cross_kept.wait()
    crossing = [wire.send(xcross.at[part], xrow.at[own, part], "zh") for part in halves]
    own_kept.wait()
    first = {name: pass_on(own, name) for name in PEERS}
    own_mate = pass_on(own, "core")
    early = [
        wire.send(wk_h, columns(wk), "core"),
        wire.send(wv_h, columns(wv), "core"),
        wire.send(wq_h, columns(wq), "core"),
        wire.send(bias.at[mp], bias.at[mp], "core"),
    ]
    late_kept = [
        keep(src, dst)
        for src, dst in ((wo_h, rows(wo)), (up_h, columns(up)), (down_h, rows(down)), (cot.at[g], cot2.at[0]))
    ]
    for copy in early_kept:
        copy.wait()

    t_buf[...] = jnp.zeros_like(t_buf)

    lane = lax.broadcasted_iota(jnp.int32, timesteps.shape, 1)
    moment = jnp.sum(jnp.where(lane == g, timesteps[...], 0).astype(F32), axis=1, keepdims=True)
    ids = lax.broadcasted_iota(jnp.int32, (8, table.shape[0]), 1).astype(F32)
    row_embed = dot(jnp.where(ids == moment, 1.0, 0.0).astype(BF), table[...], NN)[0:1, :]
    gain, shift = line(gain_1), line(shift_1)

    def hidden_of(block):
        return block.astype(F32) + row_embed

    def seg_column(b):
        return jnp.transpose(span[b].astype(F32))[:, 0:1]

    arrive(early)
    query_bias = jnp.concatenate([bias[0, 0:1, :256], bias[1, 0:1, :256]], axis=1)
    value_bias = jnp.concatenate([bias[0, 0:1, 256:], bias[1, 0:1, 256:]], axis=1)

    def project(s):
        n = 2 * BLOCK
        at = pl.ds(pl.multiple_of(s * n, n), n)
        hat, _ = normalise(hidden_of(xrow[pl.ds(2 * s, 2)].reshape(n, d)))
        low = (hat * gain + shift).astype(BF)
        normed[at, :] = low
        normed_t[:, at] = jnp.transpose(low)
        k_ref[at, :] = dot(low, wk[...], NN).astype(BF)
        v_ref[at, :] = (dot(low, wv[...], NN) + value_bias).astype(BF)
        spans = jnp.concatenate([seg_column(2 * s + i) for i in range(2)], axis=0)
        lanes = lax.broadcasted_iota(jnp.int32, (n, BLOCK), 1).astype(F32)
        hot[at, :] = jnp.where(spans == lanes, 1.0, 0.0).astype(BF)

    def beyond(base, name):
        return {"y": flip(base, 1), "zl": flip(base, 2), "diag": flip(flip(base, 1), 2)}[name]

    def to_mate(s):
        return pass_on(2 * s + mp, "core")

    arrive(own_mate)
    project(seq)
    arrive(first["y"])
    mates = {"y": to_mate(beyond(seq, "y"))}
    crossing_span.wait_recv()
    second = {name: [wire.send(span.at[par], span.at[par], name)] for name in PEERS}
    for copy, part in zip(crossing, halves):
        copy.wait_recv()
        for name in PEERS:
            second[name].append(wire.send(xrow.at[par, part], xrow.at[par, part], name))
    par_mate = to_mate(pseq)
    arrive(mates["y"])
    project(beyond(seq, "y"))
    for name in ("zl", "diag"):
        arrive(first[name])
        mates[name] = to_mate(beyond(seq, name))
    late = [
        wire.send(src, dst, "core")
        for src, dst in ((wo_h, rows(wo)), (up_h, columns(up)), (down_h, rows(down)))
    ]
    late.append(wire.send(cot.at[1 - g], cot2.at[1], "zh"))
    arrive(par_mate)
    project(pseq)

    def query_rows(ref):
        return jnp.concatenate(
            [ref[pl.ds(pl.multiple_of(b * BLOCK, BLOCK), BLOCK), :] for b in (own, par)], axis=0
        )

    scale = 1.0 / math.sqrt(HEAD_DIM)
    query_low = (dot(query_rows(normed), wq[...], NN) + query_bias).astype(BF)
    q_ref[...] = (query_low.astype(F32) * scale).astype(BF)
    for name in ("zl", "diag"):
        arrive(mates[name])
        project(beyond(seq, name))

    spans_q = jnp.concatenate([seg_column(own), seg_column(par)], axis=0)
    lanes_q = lax.broadcasted_iota(jnp.int32, (nq, BLOCK), 1).astype(F32)
    other = jnp.where(spans_q == lanes_q, 0.0, MASKED).astype(BF)
    live = jnp.where(spans_q > 0.0, 1.0, 0.0)
    other2 = jnp.concatenate([other, other], axis=0)
    first_head = lax.broadcasted_iota(jnp.int32, (nq, PAIR), 1) < HEAD_DIM
    first_head_t = lax.broadcasted_iota(jnp.int32, (PAIR, nq), 0) < HEAD_DIM

    def split_heads(value):
        wide = value.astype(F32)
        return jnp.concatenate(
            [jnp.where(first_head, wide, 0.0), jnp.where(first_head, 0.0, wide)], axis=0
        ).astype(BF)

    def join_heads_t(value):
        return jnp.where(first_head_t, value[:, :nq], value[:, nq:])

    def lanes_of(p):
        return pl.ds(p * PAIR if isinstance(p, int) else pl.multiple_of(p * PAIR, PAIR), PAIR)

    def chunk(c):
        return pl.ds(c * step, step)

    def attend(p, places):
        at = lanes_of(p)
        query = jnp.concatenate([split_heads(q_ref[:, at]), other2], axis=1)
        top = jnp.full((8, 2 * nq), -3e38, F32)
        keys_at = [pl.ds(pl.multiple_of(s * nq, nq), nq) for s in places]
        for i, here_at in enumerate(keys_at):
            keys = jnp.concatenate([k_ref[here_at, at], hot[here_at, :]], axis=1)
            scores = dot(keys, query, NT)
            s_buf[pl.ds(i * nq, nq), :] = scores
            top = jnp.maximum(top, jnp.max(scores.reshape(nq // 8, 8, 2 * nq), axis=0))
        top = jnp.max(top, axis=0, keepdims=True)
        total = jnp.zeros((8, 2 * nq), F32)
        summed = jnp.zeros((PAIR, 2 * nq), F32)
        for i, here_at in enumerate(keys_at):
            weights = jnp.exp(s_buf[pl.ds(i * nq, nq), :] - top)
            total = total + jnp.sum(weights.reshape(nq // 8, 8, 2 * nq), axis=0)
            summed = summed + dot(v_ref[here_at, at], weights.astype(BF), TN)
        return top, jnp.sum(total, axis=0, keepdims=True), summed

    near = [seq] + [beyond(seq, name) for name in PEERS] + [pseq]
    def near_pair(p, carry):
        top, total, summed = attend(p, near)
        part_top[p, 0:1, :] = top
        part_top[p, 8:9, :] = total
        part_sum[p] = summed
        return carry

    lax.fori_loop(0, pairs // 2, near_pair, 0)
    for name in PEERS:
        arrive(second[name])
        mates[name] = to_mate(beyond(pseq, name))
    lax.fori_loop(pairs // 2, pairs, near_pair, 0)
    for name in PEERS:
        arrive(mates[name])
        project(beyond(pseq, name))
    far = [beyond(pseq, name) for name in PEERS]
    def far_pair(p, carry):
        top, total, summed = attend(p, far)
        top_near = part_top[p, 0:1, :]
        top_all = jnp.maximum(top, top_near)
        weight, weight_near = jnp.exp(top - top_all), jnp.exp(top_near - top_all)
        total = total * weight + part_top[p, 8:9, :] * weight_near
        summed = summed * weight + part_sum[p] * weight_near
        joined = join_heads_t(summed / total)
        att_t[p] = joined
        att[:, lanes_of(p)] = jnp.transpose(joined)
        lse[p] = jnp.broadcast_to(top_all + jnp.log(total), (8, 2 * nq))
        return carry

    lax.fori_loop(0, pairs, far_pair, 0)

    for copy in late_kept:
        copy.wait()
    arrive(late)
    wire.finish()

    def stages_of(order):
        stages = [tuple(dim for dim in stage if has_x or dim != "x") for stage in order]
        return [stage for stage in stages if stage]

    def add_rows(out, out_at, terms, n):
        size = next(s for s in (256, 192, 128, 96, 64, 48, 32, 16) if n % s == 0)

        def one(i, carry):
            def at(base):
                return pl.ds(pl.multiple_of(base + i * size, size), size)

            values = [ref[at(base), :] for ref, base in terms]
            if len(values) == 2:
                out[at(out_at), :] = values[0] + values[1]
            else:
                out[at(out_at), :] = sum(value.astype(F32) for value in values).astype(BF)
            return carry

        lax.fori_loop(0, n // size, one, 0)

    def weights_chain(low, size, order):
        stages = stages_of(order)
        whole = pl.ds(low, size)
        used = low
        slots = [wire.slot() for _ in range(max(len(relations(stage)) for stage in stages))]
        copy = wire.send(wg.at[1 - mp, whole], core_buf.at[whole], "core", slots[0])
        yield
        copy.wait_recv()
        add_rows(acc, low, [(wg.at[mp], low), (core_buf, low)], size)
        for i, stage in enumerate(stages):
            size = size >> len(stage)
            terms, copies = [], []
            for slot, differs in zip(slots, relations(stage)):
                there = pl.ds(pl.multiple_of(low + rank(stage, differs) * size, size), size)
                copies.append(wire.send(acc.at[there], step_buf.at[pl.ds(used, size)], differs, slot))
                terms.append((step_buf, used))
                used += size
            yield
            arrive(copies)
            low = low + rank(stage) * size
            add_rows(wg_out if i == len(stages) - 1 else acc, low, [(acc, low)] + terms, size)
        for stage in reversed(stages):
            at = pl.ds(pl.multiple_of(low, size), size)
            copies = [wire.send(wg_out.at[at], wg_out.at[at], differs, slot) for slot, differs in zip(slots, relations(stage))]
            yield
            arrive(copies)
            low = low - rank(stage) * size
            size = size << len(stage)
        keep(wg_out.at[whole], wg_h.at[whole])

    def start_weights(wave):
        for name, low, size, order in PARTS[wave]:
            chains.add(name, weights_chain(low, size, order))

    finished = len(kept)
    mixed = (att[...] * live).astype(BF)
    hidden_q = hidden_of(jnp.concatenate([xrow[own], xrow[par]], axis=0))
    residual = hidden_q + dot(mixed, wo[...], NN) + line(out_bias_1)
    gain2, shift2 = line(gain_2), line(shift_2)
    hat2, rstd2 = normalise(residual)
    normed2 = (hat2 * gain2 + shift2).astype(BF)
    cotangent = jnp.concatenate([cot2[0], cot2[1]], axis=0)
    unit_result = residual + line(down_bias_1)
    grad_normed2 = jnp.zeros((nq, d), F32)
    sv = sv_acc.at[0]
    for r in range(half // step):
        for k in range(2):
            m = mp if k else 1 - mp
            j = m * (half // step) + r
            units = pl.ds(pl.multiple_of(j * step, step), step)
            inner = dot(normed2, up[:, units], NN) + bias[m, pl.ds(1 + r, 1), :]
            square = inner * inner
            bent = jnp.tanh(GELU_C * inner * (1.0 + GELU_A * square))
            activated = (0.5 * inner * (1.0 + bent)).astype(BF)
            unit_result = unit_result + dot(activated, down[units, :], NN)
            slope = 0.5 * (1.0 + bent) + 0.5 * inner * (1.0 - bent * bent) * (
                GELU_C * (1.0 + 3.0 * GELU_A * square)
            )
            grad_inner = (dot(cotangent, down[units, :], NT) * slope).astype(BF)
            grad_normed2 = grad_normed2 + dot(grad_inner, up[:, units], NT)
            down_grad = dot(activated, cotangent, TN).astype(BF)
            up_grad = dot(normed2, grad_inner, TN).astype(BF)
            for b in range(2):
                at = slice(b * 256, (b + 1) * 256)
                wg[m, pl.ds(2048 * r + b * 512, 512), :] = up_grad[:, at]
                wg[m, pl.ds(2048 * r + 1024 + b * 512, 512), :] = down_grad[:, at]
            sv_acc[0, pl.ds(6 + j, 1), :] = column_sum(grad_inner.astype(F32))
            if r == 1:
                chains.tick()
            if k == 0:
                start_weights("ab"[r])
    out = unit_result.astype(BF)
    result2[0] = out[:BLOCK]
    result2[1] = out[BLOCK:]
    result_back = wire.send(result2.at[1], res_out.at[g], "zh")
    res_out[g] = out[:BLOCK]
    chains.tick()
    cot_f = cotangent.astype(F32)
    grad_residual = cot_f + normalise_back(grad_normed2 * gain2, hat2, rstd2)
    sv[2:3, :] = column_sum(grad_normed2 * hat2)
    sv[3:4, :] = column_sum(grad_normed2)
    sv[4:5, :] = column_sum(grad_residual)
    sv[5:6, :] = column_sum(cot_f)
    branch_grad = grad_residual.astype(BF)
    out_grad = dot(mixed, branch_grad, TN).astype(BF)
    for m in range(2):
        for b in range(2):
            wg[m, pl.ds(OUT_AT + b * 256, 256), :] = out_grad[m * 256 : (m + 1) * 256, b * 256 : (b + 1) * 256]
    start_weights("c")
    chains.tick()
    att[...] = dot(branch_grad, wo[...], NT).astype(BF).astype(F32) * live

    def back(p):
        at = lanes_of(p)
        query = split_heads(q_ref[:, at])
        query_wide = jnp.concatenate([query, other2], axis=1)
        heads = att[:, at]
        grads = split_heads(heads)
        product = jnp.transpose(heads) * att_t[p]
        delta = jnp.concatenate([column_sum(product[:HEAD_DIM]), column_sum(product[HEAD_DIM:])], axis=1)
        log_total = lse[p][0:1, :]
        query_grad = jnp.zeros((PAIR, 2 * nq), F32)
        for c in range(steps):
            keys = k_ref[chunk(c), at]
            scores = dot(jnp.concatenate([keys, hot[chunk(c), :]], axis=1), query_wide, NT)
            probs = jnp.exp(scores - log_total)
            grad_probs = dot(v_ref[chunk(c), at], grads, NT)
            grad_scores = (probs * (grad_probs - delta)).astype(BF)
            dkv[p, chunk(c), 0:PAIR] = dot(grad_scores, query, NN).astype(BF)
            dkv[p, chunk(c), PAIR:] = dot(probs.astype(BF), grads, NN).astype(BF)
            query_grad = query_grad + dot(keys, grad_scores, TN)
            chains.tick()
        joined = join_heads_t(query_grad) * scale
        dq_ref[:, at] = jnp.transpose(joined).astype(BF)

    normed_q = query_rows(normed)
    for n in range(2):
        for m in range(2):
            back(2 * m + n)
        for m in range(2):
            p = 2 * m + n
            pair_grad = dot(normed_t[...], dkv[p], NN)
            wg[m, pl.ds(PAIR_AT[n], d), :] = pair_grad.astype(BF)
            pair_grad = dot(normed_q, dq_ref[:, lanes_of(p)], TN).astype(BF)
            wg[m, pl.ds(PAIR_AT[n] + d, d // 2), 0:PAIR] = pair_grad[: d // 2]
            wg[m, pl.ds(PAIR_AT[n] + d, d // 2), PAIR:] = pair_grad[d // 2 :]
        start_weights("pq"[n])
        chains.tick()

    def tokens_back(grad_normed, block):
        hat, rstd = normalise(hidden_of(block))
        return (
            normalise_back(grad_normed * gain, hat, rstd),
            column_sum(grad_normed * hat),
            column_sum(grad_normed),
        )

    query_grad = dq_ref[...]
    token_grad, gain_sum, shift_sum = tokens_back(
        dot(query_grad, wq[...], NT), jnp.concatenate([xrow[own], xrow[par]], axis=0)
    )
    token_grad = token_grad + grad_residual
    t_buf[own] = token_grad[:BLOCK]
    t_buf[par] = token_grad[BLOCK:]
    token_sum = column_sum(token_grad)
    value_sums = [jnp.zeros((1, PAIR), F32) for _ in range(pairs)]

    def tokens_chain(hi, one, leaves):
        slot = wire.slot()
        copy = wire.send(t_out.at[hi, :, :, 1 - mp], t_core.at[hi], "core", slot)
        yield
        copy.wait_recv()
        for b in range(2):
            for c in range(2):
                t_acc[hi, b, c] = t_out[hi, b, c, mp] + t_core[hi, b, c]
        if one == "y":
            copy = wire.send(t_acc.at[hi, :, 1 - y], t_step.at[hi, 0:2], "y", slot)
        else:
            copy = wire.send(t_acc.at[hi, 1 - zl], t_step.at[hi, 0:2], "zl", slot)
        yield
        copy.wait_recv()
        if one == "y":
            for i in range(2):
                t_acc[hi, i, y] += t_step[hi, i]
            copy = wire.send(t_acc.at[hi, 1 - zl, y], t_step.at[hi, 2], "zl", slot)
        else:
            for i in range(2):
                t_acc[hi, zl, i] += t_step[hi, i]
            copy = wire.send(t_acc.at[hi, zl, 1 - y], t_step.at[hi, 2], "y", slot)
        yield
        copy.wait_recv()
        t_acc[hi, zl, y] += t_step[hi, 2]
        if leaves:
            copy = wire.send(t_acc.at[hi, zl, y], tg_out.at[g], "zh", slot)
            yield
            copy.wait_recv()
        else:
            tg_out[g] = t_acc[hi, zl, y]

    for n, (hi, one) in enumerate(((1 - g, "y"), (g, "y"))):
        for c in range(2):
            place = 2 * hi + c
            at = pl.ds(pl.multiple_of(place * step, step), step)
            grad_normed = jnp.zeros((step, d), F32)
            for p in range(pairs):
                pair_grad = dkv[p, at, :]
                both = jnp.concatenate([wk[:, lanes_of(p)], wv[:, lanes_of(p)]], axis=1)
                grad_normed = grad_normed + dot(pair_grad, both, NT)
                value_sums[p] = value_sums[p] + column_sum(pair_grad[:, PAIR:].astype(F32))
            blocks_at = pl.ds(place * nb, nb)
            token_grad, a, b = tokens_back(grad_normed, xrow[blocks_at].reshape(step, d))
            gain_sum, shift_sum, token_sum = gain_sum + a, shift_sum + b, token_sum + column_sum(token_grad)
            token_grad = t_buf[blocks_at] + token_grad.reshape(nb, BLOCK, d)
            for i in range(nb):
                t_out[hi, c, i // 2, i % 2] = token_grad[i].astype(BF)
            chains.tick()
        chains.add(("t0", "t1")[n], tokens_chain(hi, one, n == 0))
    value_sum = jnp.concatenate(value_sums, axis=1)

    sv[0:1, :] = gain_sum
    sv[1:2, :] = shift_sum
    sv[10:11, :] = column_sum(query_grad.astype(F32))
    sv[11:12, :] = value_sum
    sv[12:16, :] = jnp.zeros((4, d), F32)
    slot_lane = lax.broadcasted_iota(jnp.int32, (1, d), 1)
    speaks = jnp.logical_and(lax.rem(seq, 4) == 0, mp == 0)
    my_slot = 2 * dp + g
    sv[12:13, :] = jnp.where(slot_lane == jnp.where(speaks, my_slot, -1), moment, 0.0)
    slot = lax.broadcasted_iota(jnp.int32, (sv.shape[0] - SV_TABLE, d), 0) == my_slot
    sv[SV_TABLE:, :] = jnp.where(slot, token_sum, 0.0)

    def vectors_chain():
        slots = [wire.slot() for _ in range(3)]
        stages = [("core",)] + stages_of((("x", "y"), ("zl", "zh")))
        for i, stage in enumerate(stages):
            copies = [
                wire.send(sv_acc.at[i], sv_buf.at[i, k], differs, slots[k])
                for k, differs in enumerate(relations(stage))
            ]
            yield
            arrive(copies)
            total = sv_acc[i] + sv_buf[i, 0]
            if len(copies) == 3:
                total = total + (sv_buf[i, 1] + sv_buf[i, 2])
            sv_acc[i + 1] = total
        sv_out[...] = sv_acc[len(stages)]
        result_back.wait_recv()

    chains.add("s", vectors_chain())
    chains.drain()
    wire.finish()
    for copy in kept[finished:]:
        copy.wait()


def layer(big, small, has_x, sv_rows):
    shape = jax.ShapeDtypeStruct
    tokens, up, table = big[0], big[6], big[8]
    d = tokens.shape[2]
    blocks = 2 * lax.axis_size("seq")
    length = blocks * BLOCK
    nq = 2 * BLOCK
    pairs = d // PAIR
    ff = 2 * up.shape[1]
    block = (BLOCK, d)
    vmem = pltpu.VMEM
    return pl.pallas_call(
        functools.partial(layer_kernel, has_x),
        out_shape=(
            shape((WG_ROWS, 256), BF),
            shape((sv_rows, d), F32),
            shape(tokens.shape, BF),
            shape(tokens.shape, BF),
        ),
        in_specs=any_spec(len(big)) + vmem_spec(len(small)),
        out_specs=tuple(any_spec(1) + vmem_spec(3)),
        scratch_shapes=[
            vmem((blocks, BLOCK, d), BF),
            vmem((blocks, SPAN_ROWS, BLOCK), BF),
            vmem(block, BF),
            vmem((SPAN_ROWS, BLOCK), BF),
            vmem(table.shape, BF),
            vmem((2,) + block, BF),
            vmem((d, d), BF),
            vmem((d, d), BF),
            vmem((d, d), BF),
            vmem((d, d), BF),
            vmem((d, ff), BF),
            vmem((ff, d), BF),
            vmem((2, 8, d), F32),
            vmem((length, d), BF),
            vmem((d, length), BF),
            vmem((length, d), BF),
            vmem((length, d), BF),
            vmem((length, BLOCK), BF),
            vmem((5 * nq, 2 * nq), F32),
            vmem((nq, d), F32),
            vmem((pairs, PAIR, nq), F32),
            vmem((pairs, 8, 2 * nq), F32),
            vmem((nq, d), BF),
            vmem((pairs, length, 2 * PAIR), BF),
            vmem((nq, d), BF),
            vmem((blocks,) + block, F32),
            vmem((pairs, 16, 2 * nq), F32),
            vmem((pairs, PAIR, 2 * nq), F32),
            vmem((2, WG_ROWS, 256), BF),
            vmem((WG_ROWS, 256), BF),
            vmem((WG_ROWS, 256), BF),
            vmem((WG_ROWS, 256), BF),
            vmem((WG_ROWS, 256), BF),
            vmem((2, 2, 2, 2) + block, BF),
            vmem((2, 2, 2) + block, BF),
            vmem((2, 2, 2) + block, BF),
            vmem((2, 3) + block, BF),
            vmem((2,) + block, BF),
            vmem((3, 3, sv_rows, d), F32),
            vmem((4, sv_rows, d), F32),
            pltpu.SemaphoreType.DMA((SENDS,)),
            pltpu.SemaphoreType.DMA((RECEIVES,)),
            pltpu.SemaphoreType.DMA((KEEPS,)),
        ],
        compiler_params=pltpu.CompilerParams(
            collective_id=0, has_side_effects=True, vmem_limit_bytes=62 << 20
        ),
        name="layer",
    )(*big, *small)


def finish_kernel(
    table_rows, wg, tg, res, sv,
    res_o, tg_o, table_o, wq_o, wk_o, wv_o, wo_o, up_o, down_o,
    gain_1, shift_1, query_bias, value_bias, out_bias, gain_2, shift_2, up_bias, down_bias,
    wg_v, tg_v, res_v, tg_f, table_v, wq_v, wk_v, wv_v, wo_v, up_v, down_v,
    in_sem, out_sem,
):
    mp = lax.axis_index("mp")
    leaving = []
    rows = 1024
    parts = WG_ROWS // rows

    def fetch(src, dst, n):
        copy = pltpu.make_async_copy(src, dst, in_sem.at[n])
        copy.start()
        return copy

    def leave(src, dst):
        copy = pltpu.make_async_copy(src, dst, out_sem.at[len(leaving)])
        copy.start()
        leaving.append(copy)

    coming = [fetch(wg.at[pl.ds(i * rows, rows)], wg_v.at[pl.ds(i * rows, rows)], i) for i in range(parts)]
    coming_tg, coming_res = fetch(tg, tg_v, parts), fetch(res, res_v, parts + 1)
    ids = sv[12:13, 0:128]
    spread = jnp.where(lax.broadcasted_iota(jnp.int32, (table_v.shape[0], 128), 0).astype(F32) == ids, 1.0, 0.0)
    sums = jnp.concatenate([sv[SV_TABLE:, :], jnp.zeros((128 - (sv.shape[0] - SV_TABLE), sv.shape[1]), F32)], axis=0)
    spread = spread.astype(BF)
    high = sums.astype(BF)
    rest = sums - high.astype(F32)
    middle = rest.astype(BF)
    low = (rest - middle.astype(F32)).astype(BF)
    table_v[...] = dot(spread, high, NN) + (dot(spread, middle, NN) + dot(spread, low, NN))
    leave(table_v, table_o)

    def flat(ref, value):
        ref[...] = value.reshape(ref.shape)

    for ref, r in ((gain_1, 0), (shift_1, 1), (gain_2, 2), (shift_2, 3), (out_bias, 4), (down_bias, 5)):
        flat(ref, sv[r : r + 1, :])
    for ref, r in ((query_bias, 10), (value_bias, 11)):
        flat(ref, jnp.where(mp == 0, sv[r : r + 1, 0:256], sv[r : r + 1, 256:512]))
    flat(up_bias, jnp.where(mp == 0, jnp.concatenate([sv[6:7, :], sv[7:8, :]], axis=1), jnp.concatenate([sv[8:9, :], sv[9:10, :]], axis=1)))

    def take(at, n):
        return wg_v[at : at + n, :].astype(F32)

    for i in range(parts):
        coming[i].wait()
        if i in (0, 2):
            for b in range(2):
                up_v[:, i * 256 + b * 256 : i * 256 + (b + 1) * 256] = take(i * rows + b * 512, 512)
            leave(up_v.at[:, pl.ds(i * 256, 512)], up_o.at[:, pl.ds(i * 256, 512)])
        elif i in (1, 3):
            at = pl.ds(i // 2 * 512, 512)
            for b in range(2):
                down_v[at, b * 256 : (b + 1) * 256] = take(i * rows + b * 512, 512)
            leave(down_v.at[at], down_o.at[at])
        elif i == 4:
            for b in range(2):
                wo_v[:, b * 256 : (b + 1) * 256] = take(OUT_AT + b * 256, 256)
            leave(wo_v, wo_o)
        else:
            for n, at in enumerate(PAIR_AT):
                lanes = slice(n * PAIR, (n + 1) * PAIR)
                both, query = take(at, 512), take(at + 512, 256)
                wk_v[:, lanes] = both[:, :PAIR]
                wv_v[:, lanes] = both[:, PAIR:]
                wq_v[0:256, lanes] = query[:, :PAIR]
                wq_v[256:512, lanes] = query[:, PAIR:]
            leave(wk_v, wk_o)
            leave(wv_v, wv_o)
            leave(wq_v, wq_o)
    coming_res.wait()
    leave(res_v, res_o)
    coming_tg.wait()
    tg_f[...] = tg_v[...].astype(F32)
    leave(tg_f, tg_o)
    for copy in leaving:
        copy.wait()


def finish(wg, tg, res, sv, table_rows, steps, units):
    shape = jax.ShapeDtypeStruct
    d = sv.shape[1]
    big = [
        shape(res.shape, BF), shape(tg.shape, F32), shape((steps, d), F32),
        shape((d, d // 2), F32), shape((d, d // 2), F32), shape((d, d // 2), F32), shape((d // 2, d), F32),
        shape((d, units), F32), shape((units, d), F32),
    ]
    small = [shape((n,), F32) for n in (d, d, d // 2, d // 2, d, d, d, units, d)]
    vmem = pltpu.VMEM
    return pl.pallas_call(
        functools.partial(finish_kernel, table_rows),
        out_shape=tuple(big + small),
        in_specs=any_spec(3) + vmem_spec(1),
        out_specs=tuple(any_spec(len(big)) + vmem_spec(len(small))),
        scratch_shapes=[vmem(wg.shape, BF), vmem(tg.shape, BF), vmem(res.shape, BF), vmem(tg.shape, F32)]
        + [vmem(item.shape, F32) for item in big[2:]]
        + [pltpu.SemaphoreType.DMA((8,)), pltpu.SemaphoreType.DMA((12,))],
        compiler_params=pltpu.CompilerParams(vmem_limit_bytes=62 << 20),
        name="finish",
    )(wg, tg, res, sv)


def local(
    n_dp, tokens, segments, timesteps, step_table, first_gain, first_shift, query_weight, query_bias,
    key_weight, value_weight, value_bias, out_weight, out_bias, second_gain, second_shift,
    up_weight, up_bias, down_weight, down_bias, cotangent,
):
    table_rows = tokens.shape[0] * n_dp
    sv_rows = SV_TABLE + -(-table_rows // 8) * 8
    wg, sv, token_grad, result = layer(
        (tokens, cotangent, query_weight, key_weight, value_weight, out_weight, up_weight, down_weight, step_table),
        (segments, timesteps[None, :], first_gain, first_shift, second_gain, second_shift, out_bias, down_bias,
         query_bias, value_bias, up_bias),
        n_dp == 2, sv_rows,
    )
    if n_dp != 2:
        wg, sv = lax.psum((wg, sv), "dp")
    (result, token_grad, table_grad, wq, wk, wv, wo, up, down,
     gain_1, shift_1, bq, bv, bo, gain_2, shift_2, bu, bd) = finish(
        wg, token_grad, result, sv, table_rows, step_table.shape[0], up_weight.shape[1]
    )
    return (
        result, token_grad, table_grad, gain_1, shift_1, wq, bq, wk, wv, bv, wo, bo, gain_2, shift_2, up, bu, down, bd
    )


def solution(mesh):
    rows, chars, whole = P("dp", ("seq", "mp"), None), P("dp", ("seq", "mp")), P()
    columns, split, tall = P(None, "mp"), P("mp"), P("mp", None)
    in_specs = (
        rows, chars, P("dp"), whole, whole, whole, columns, split, columns, columns, split, tall,
        whole, whole, whole, columns, split, tall, whole, rows,
    )
    out_specs = (
        rows, rows, whole, whole, whole, columns, split, columns, columns, split, tall,
        whole, whole, whole, columns, split, tall, whole,
    )
    return jax.shard_map(
        functools.partial(local, mesh.shape["dp"]),
        mesh=mesh,
        in_specs=in_specs,
        out_specs=out_specs,
        check_vma=False,
    )
```

```python
import functools
import math

import jax
import jax.numpy as jnp
from jax import lax
from jax.experimental import pallas as pl
from jax.experimental.pallas import tpu as pltpu
from jax.sharding import PartitionSpec as P

MESH = pl.DeviceIdType.MESH
BF, F32 = jnp.bfloat16, jnp.float32
NN = (((1,), (0,)), ((), ()))
NT = (((1,), (1,)), ((), ()))
TN = (((0,), (0,)), ((), ()))
HEAD_DIM = 64
BLOCK = 128
PAIR = 2 * HEAD_DIM
MASKED = -1e30
GELU_A = 0.044715
GELU_C = math.sqrt(2.0 / math.pi)
OUT_AT, PAIR_AT, PAIR_ROWS, WG_ROWS = 4096, (4608, 5376), 768, 6144
SV_TABLE = 16
RECEIVES, SENDS, KEEPS = 146, 44, 22
SPAN_ROWS = 16
PEERS = ("y", "zl", "diag")
PARTS = {
    "a": (
        ("a0", 0, 768, (("x",), ("y",), ("zl", "zh",),)),
        ("a1", 768, 768, (("zl",), ("x", "y",), ("zh",),)),
    ),
    "b": (
        ("b0", 1536, 768, (("x",), ("zl",), ("y",), ("zh",),)),
        ("b1", 2304, 768, (("zl",), ("x", "y",), ("zh",),)),
    ),
    "c": (
        ("c0", 3072, 768, (("x", "y",), ("zl", "zh",),)),
        ("c1", 3840, 768, (("x",), ("zl",), ("y",), ("zh",),)),
    ),
    "p": (
        ("p0", 4608, 768, (("y",), ("x",), ("zl", "zh",),)),
    ),
    "q": (
        ("q0", 5376, 768, (("x", "y",), ("zl", "zh",),)),
    ),
}
SCRIPT = (
    (),
    ("a0", "a1", "b0", "b1",),
    (),
    (),
    ("a0", "a1", "c0", "c1",),
    ("a0", "b1", "b0", "a1",),
    (),
    (),
    ("a0",),
    ("b0", "a1", "c0",),
    (),
    ("a0", "b0",),
    ("a1", "c1",),
    ("p0", "a0", "b1", "c0", "b0",),
    ("a1", "c1",),
    ("b1",),
    (),
    (),
    ("c0", "p0", "a0", "b0",),
    ("c1",),
    (),
    ("a1", "b1",),
    ("q0", "c0", "c1", "b0",),
    ("p0",),
    ("c1",),
    ("b1", "t0", "b0",),
    (
        "p0", "q0", "s", "c1", "t1", "b1", "b0", "p0", "t0", "q0", "s", "c1", "p0", "t0", "q0",
        "t1", "c1", "s", "p0", "t0", "t1", "q0",
    ),
)


def dot(a, b, dims):
    return lax.dot_general(a, b, dims, preferred_element_type=F32)


def bit(v, n):
    return lax.rem(lax.div(v, n), 2)


def flip(v, n):
    return v + n - 2 * n * bit(v, n)


def here():
    return lax.axis_index("dp"), lax.axis_index("seq"), lax.axis_index("mp")


def neighbour(name):
    dp, seq, mp = here()
    dims = {"diag": ("y", "zl")}.get(name, name if isinstance(name, tuple) else (name,))
    for dim in dims:
        if dim == "core":
            mp = 1 - mp
        elif dim == "x":
            dp = 1 - dp
        else:
            seq = flip(seq, {"y": 1, "zl": 2, "zh": 4}[dim])
    return (dp, seq, mp)


def side(name):
    dp, seq, mp = here()
    return {"x": dp, "y": bit(seq, 1), "zl": bit(seq, 2), "zh": bit(seq, 4), "core": mp}[name]


def relations(stage):
    return [tuple(dim for i, dim in enumerate(stage) if k >> i & 1) for k in range(1, 1 << len(stage))]


def rank(stage, differs=()):
    place = 0
    for dim in stage:
        b = side(dim)
        place = 2 * place + (1 - b if dim in differs else b)
    return place


def greet(names):
    barrier = pltpu.get_barrier_semaphore()
    for name in names:
        pl.semaphore_signal(barrier, inc=1, device_id=neighbour(name), device_id_type=MESH)
    pl.semaphore_wait(barrier, len(names))


class Wire:
    def __init__(self, send_sem, recv_sem):
        self.send_sem, self.recv_sem = send_sem, recv_sem
        self.count, self.slots = 0, 0
        self.leaving = {}

    def slot(self):
        self.slots += 1
        return self.slots - 1

    def send(self, src, dst, name, slot=None):
        if slot is None:
            slot = self.slot()
        if slot in self.leaving:
            self.leaving.pop(slot).wait_send()
        copy = pltpu.make_async_remote_copy(
            src_ref=src,
            dst_ref=dst,
            send_sem=self.send_sem.at[slot],
            recv_sem=self.recv_sem.at[self.count],
            device_id=neighbour(name),
            device_id_type=MESH,
        )
        copy.start()
        self.count += 1
        assert self.count <= RECEIVES and slot < SENDS
        self.leaving[slot] = copy
        return copy

    def finish(self):
        for copy in self.leaving.values():
            copy.wait_send()
        self.leaving = {}
        self.slots = 0


def any_spec(n):
    return [pl.BlockSpec(memory_space=pl.ANY)] * n


def vmem_spec(n):
    return [pl.BlockSpec(memory_space=pltpu.VMEM)] * n


def normalise(value):
    centred = value - jnp.mean(value, axis=-1, keepdims=True)
    rstd = lax.rsqrt(jnp.mean(centred * centred, axis=-1, keepdims=True) + 1e-5)
    return centred * rstd, rstd


def normalise_back(grad_hat, hat, rstd):
    return rstd * (
        grad_hat
        - jnp.mean(grad_hat, axis=-1, keepdims=True)
        - hat * jnp.mean(grad_hat * hat, axis=-1, keepdims=True)
    )


def column_sum(value):
    return jnp.sum(value, axis=0, keepdims=True)


class Chains:
    def __init__(self):
        self.running = {}
        self.place = 0

    def add(self, name, chain):
        next(chain)
        self.running[name] = chain

    def advance(self, name):
        if name in self.running and next(self.running[name], "ended") == "ended":
            del self.running[name]

    def tick(self):
        for name in SCRIPT[self.place]:
            self.advance(name)
        self.place += 1

    def drain(self):
        assert self.place == len(SCRIPT) - 1
        self.tick()
        while self.running:
            for name in tuple(self.running):
                self.advance(name)


def layer_kernel(
    has_x,
    tokens, cot, wq_h, wk_h, wv_h, wo_h, up_h, down_h, table_h,
    segments, timesteps, gain_1, shift_1, gain_2, shift_2, out_bias_1, down_bias_1, query_bias_1, value_bias_1, up_bias_1,
    wg_h, sv_out, tg_out, res_out,
    xrow, span, xcross, span_cross, table, cot2, wq, wk, wv, wo, up, down, bias,
    normed, normed_t, k_ref, v_ref, hot, s_buf, att, att_t, lse, q_ref, dkv, dq_ref, t_buf, part_top, part_sum,
    wg, acc, core_buf, step_buf, wg_out, t_out, t_core, t_acc, t_step, result2, sv_buf, sv_acc,
    send_sem, recv_sem, local_sem,
):
    dp, seq, mp = here()
    g = lax.div(seq, 4)
    pseq = flip(seq, 4)
    own, par = 2 * seq + mp, 2 * pseq + mp
    y, zl = bit(seq, 1), bit(seq, 2)
    d = normed.shape[1]
    length = normed.shape[0]
    pairs = d // PAIR
    step = 512
    steps = length // step
    nb = step // BLOCK
    ff = up.shape[1]
    half = ff // 2
    nq = 2 * BLOCK
    wire = Wire(send_sem, recv_sem)
    chains = Chains()
    kept = []

    def keep(src, dst):
        copy = pltpu.make_async_copy(src, dst, local_sem.at[len(kept)])
        copy.start()
        kept.append(copy)
        return copy

    def columns(ref):
        w = ref.shape[1] // 2
        return ref.at[:, pl.ds(pl.multiple_of(mp * w, w), w)]

    def rows(ref):
        w = ref.shape[0] // 2
        return ref.at[pl.ds(pl.multiple_of(mp * w, w), w)]

    def arrive(copies):
        for copy in copies:
            copy.wait_recv()

    cross_kept = keep(tokens.at[1 - g], xcross)
    own_kept = keep(tokens.at[g], xrow.at[own])
    early_kept = [keep(table_h, table), keep(wk_h, columns(wk)), keep(wv_h, columns(wv)), keep(wq_h, columns(wq))]
    spans = segments[...].astype(F32)
    first_row = jnp.where(g == 0, spans[0:1, :], spans[1:2, :])
    second_row = jnp.where(g == 0, spans[1:2, :], spans[0:1, :])
    span_cross[...] = jnp.broadcast_to(second_row, (SPAN_ROWS, BLOCK)).astype(BF)
    span[own] = jnp.broadcast_to(first_row, (SPAN_ROWS, BLOCK)).astype(BF)

    def line(ref):
        return ref[...].astype(F32).reshape(1, ref.shape[0])

    bias[mp] = jnp.concatenate(
        [jnp.concatenate([line(query_bias_1), line(value_bias_1)], axis=1)]
        + [line(up_bias_1)[:, i * d : (i + 1) * d] for i in range(half // d)]
        + [jnp.zeros((8 - 1 - half // d, d), F32)],
        axis=0,
    )
    greet(("core", "y", "zl", "diag", "zh", ("zl", "zh")) + (("x", ("x", "y")) if has_x else ()))

    def pass_on(block, name):
        return [
            wire.send(span.at[block], span.at[block], name),
            wire.send(xrow.at[block], xrow.at[block], name),
        ]

    halves = pl.ds(0, BLOCK // 2), pl.ds(BLOCK // 2, BLOCK // 2)
    crossing_span = wire.send(span_cross, span.at[own], "zh")
    cross_kept.wait()
    crossing = [wire.send(xcross.at[part], xrow.at[own, part], "zh") for part in halves]
    own_kept.wait()
    first = {name: pass_on(own, name) for name in PEERS}
    own_mate = pass_on(own, "core")
    early = [
        wire.send(wk_h, columns(wk), "core"),
        wire.send(wv_h, columns(wv), "core"),
        wire.send(wq_h, columns(wq), "core"),
        wire.send(bias.at[mp], bias.at[mp], "core"),
    ]
    late_kept = [
        keep(src, dst)
        for src, dst in ((wo_h, rows(wo)), (up_h, columns(up)), (down_h, rows(down)), (cot.at[g], cot2.at[0]))
    ]
    for copy in early_kept:
        copy.wait()

    t_buf[...] = jnp.zeros_like(t_buf)

    lane = lax.broadcasted_iota(jnp.int32, timesteps.shape, 1)
    moment = jnp.sum(jnp.where(lane == g, timesteps[...], 0).astype(F32), axis=1, keepdims=True)
    ids = lax.broadcasted_iota(jnp.int32, (8, table.shape[0]), 1).astype(F32)
    row_embed = dot(jnp.where(ids == moment, 1.0, 0.0).astype(BF), table[...], NN)[0:1, :]
    gain, shift = line(gain_1), line(shift_1)

    def hidden_of(block):
        return block.astype(F32) + row_embed

    def seg_column(b):
        return jnp.transpose(span[b].astype(F32))[:, 0:1]

    arrive(early)
    query_bias = jnp.concatenate([bias[0, 0:1, :256], bias[1, 0:1, :256]], axis=1)
    value_bias = jnp.concatenate([bias[0, 0:1, 256:], bias[1, 0:1, 256:]], axis=1)

    def project(s):
        n = 2 * BLOCK
        at = pl.ds(pl.multiple_of(s * n, n), n)
        hat, _ = normalise(hidden_of(xrow[pl.ds(2 * s, 2)].reshape(n, d)))
        low = (hat * gain + shift).astype(BF)
        normed[at, :] = low
        normed_t[:, at] = jnp.transpose(low)
        k_ref[at, :] = dot(low, wk[...], NN).astype(BF)
        v_ref[at, :] = (dot(low, wv[...], NN) + value_bias).astype(BF)
        spans = jnp.concatenate([seg_column(2 * s + i) for i in range(2)], axis=0)
        lanes = lax.broadcasted_iota(jnp.int32, (n, BLOCK), 1).astype(F32)
        hot[at, :] = jnp.where(spans == lanes, 1.0, 0.0).astype(BF)

    def beyond(base, name):
        return {"y": flip(base, 1), "zl": flip(base, 2), "diag": flip(flip(base, 1), 2)}[name]

    def to_mate(s):
        return pass_on(2 * s + mp, "core")

    arrive(own_mate)
    project(seq)
    arrive(first["y"])
    mates = {"y": to_mate(beyond(seq, "y"))}
    crossing_span.wait_recv()
    second = {name: [wire.send(span.at[par], span.at[par], name)] for name in PEERS}
    for copy, part in zip(crossing, halves):
        copy.wait_recv()
        for name in PEERS:
            second[name].append(wire.send(xrow.at[par, part], xrow.at[par, part], name))
    par_mate = to_mate(pseq)
    arrive(mates["y"])
    project(beyond(seq, "y"))
    for name in ("zl", "diag"):
        arrive(first[name])
        mates[name] = to_mate(beyond(seq, name))
    late = [
        wire.send(src, dst, "core")
        for src, dst in ((wo_h, rows(wo)), (up_h, columns(up)), (down_h, rows(down)))
    ]
    late.append(wire.send(cot.at[1 - g], cot2.at[1], "zh"))
    arrive(par_mate)
    project(pseq)

    def query_rows(ref):
        return jnp.concatenate(
            [ref[pl.ds(pl.multiple_of(b * BLOCK, BLOCK), BLOCK), :] for b in (own, par)], axis=0
        )

    scale = 1.0 / math.sqrt(HEAD_DIM)
    query_low = (dot(query_rows(normed), wq[...], NN) + query_bias).astype(BF)
    q_ref[...] = (query_low.astype(F32) * scale).astype(BF)
    for name in ("zl", "diag"):
        arrive(mates[name])
        project(beyond(seq, name))

    spans_q = jnp.concatenate([seg_column(own), seg_column(par)], axis=0)
    lanes_q = lax.broadcasted_iota(jnp.int32, (nq, BLOCK), 1).astype(F32)
    other = jnp.where(spans_q == lanes_q, 0.0, MASKED).astype(BF)
    live = jnp.where(spans_q > 0.0, 1.0, 0.0)
    other2 = jnp.concatenate([other, other], axis=0)
    first_head = lax.broadcasted_iota(jnp.int32, (nq, PAIR), 1) < HEAD_DIM
    first_head_t = lax.broadcasted_iota(jnp.int32, (PAIR, nq), 0) < HEAD_DIM

    def split_heads(value):
        wide = value.astype(F32)
        return jnp.concatenate(
            [jnp.where(first_head, wide, 0.0), jnp.where(first_head, 0.0, wide)], axis=0
        ).astype(BF)

    def join_heads_t(value):
        return jnp.where(first_head_t, value[:, :nq], value[:, nq:])

    def lanes_of(p):
        return pl.ds(p * PAIR if isinstance(p, int) else pl.multiple_of(p * PAIR, PAIR), PAIR)

    def chunk(c):
        return pl.ds(c * step, step)

    def attend(p, places):
        at = lanes_of(p)
        query = jnp.concatenate([split_heads(q_ref[:, at]), other2], axis=1)
        top = jnp.full((8, 2 * nq), -3e38, F32)
        keys_at = [pl.ds(pl.multiple_of(s * nq, nq), nq) for s in places]
        for i, here_at in enumerate(keys_at):
            keys = jnp.concatenate([k_ref[here_at, at], hot[here_at, :]], axis=1)
            scores = dot(keys, query, NT)
            s_buf[pl.ds(i * nq, nq), :] = scores
            top = jnp.maximum(top, jnp.max(scores.reshape(nq // 8, 8, 2 * nq), axis=0))
        top = jnp.max(top, axis=0, keepdims=True)
        total = jnp.zeros((8, 2 * nq), F32)
        summed = jnp.zeros((PAIR, 2 * nq), F32)
        for i, here_at in enumerate(keys_at):
            weights = jnp.exp(s_buf[pl.ds(i * nq, nq), :] - top)
            total = total + jnp.sum(weights.reshape(nq // 8, 8, 2 * nq), axis=0)
            summed = summed + dot(v_ref[here_at, at], weights.astype(BF), TN)
        return top, jnp.sum(total, axis=0, keepdims=True), summed

    near = [seq] + [beyond(seq, name) for name in PEERS] + [pseq]
    def near_pair(p, carry):
        top, total, summed = attend(p, near)
        part_top[p, 0:1, :] = top
        part_top[p, 8:9, :] = total
        part_sum[p] = summed
        return carry

    for n, name in enumerate(PEERS):
        lax.fori_loop((0, 2, 3)[n], (2, 3, pairs)[n], near_pair, 0)
        arrive(second[name])
        mates[name] = to_mate(beyond(pseq, name))
    for name in PEERS:
        arrive(mates[name])
        project(beyond(pseq, name))
    far = [beyond(pseq, name) for name in PEERS]
    def far_pair(p, carry):
        top, total, summed = attend(p, far)
        top_near = part_top[p, 0:1, :]
        top_all = jnp.maximum(top, top_near)
        weight, weight_near = jnp.exp(top - top_all), jnp.exp(top_near - top_all)
        total = total * weight + part_top[p, 8:9, :] * weight_near
        summed = summed * weight + part_sum[p] * weight_near
        joined = join_heads_t(summed / total)
        att_t[p] = joined
        att[:, lanes_of(p)] = jnp.transpose(joined)
        lse[p] = jnp.broadcast_to(top_all + jnp.log(total), (8, 2 * nq))
        return carry

    lax.fori_loop(0, pairs, far_pair, 0)

    for copy in late_kept:
        copy.wait()
    arrive(late)
    wire.finish()

    def stages_of(order):
        stages = [tuple(dim for dim in stage if has_x or dim != "x") for stage in order]
        return [stage for stage in stages if stage]

    def add_rows(out, out_at, terms, n):
        size = next(s for s in (256, 192, 128, 96, 64, 48, 32, 16) if n % s == 0)

        def one(i, carry):
            def at(base):
                return pl.ds(pl.multiple_of(base + i * size, size), size)

            values = [ref[at(base), :] for ref, base in terms]
            if len(values) == 2:
                out[at(out_at), :] = values[0] + values[1]
            else:
                out[at(out_at), :] = sum(value.astype(F32) for value in values).astype(BF)
            return carry

        lax.fori_loop(0, n // size, one, 0)

    def weights_chain(low, size, order):
        stages = stages_of(order)
        whole = pl.ds(low, size)
        used = low
        slots = [wire.slot() for _ in range(max(len(relations(stage)) for stage in stages))]
        copy = wire.send(wg.at[1 - mp, whole], core_buf.at[whole], "core", slots[0])
        yield
        copy.wait_recv()
        add_rows(acc, low, [(wg.at[mp], low), (core_buf, low)], size)
        for i, stage in enumerate(stages):
            size = size >> len(stage)
            terms, copies = [], []
            for slot, differs in zip(slots, relations(stage)):
                there = pl.ds(pl.multiple_of(low + rank(stage, differs) * size, size), size)
                copies.append(wire.send(acc.at[there], step_buf.at[pl.ds(used, size)], differs, slot))
                terms.append((step_buf, used))
                used += size
            yield
            arrive(copies)
            low = low + rank(stage) * size
            add_rows(wg_out if i == len(stages) - 1 else acc, low, [(acc, low)] + terms, size)
        for stage in reversed(stages):
            at = pl.ds(pl.multiple_of(low, size), size)
            copies = [wire.send(wg_out.at[at], wg_out.at[at], differs, slot) for slot, differs in zip(slots, relations(stage))]
            yield
            arrive(copies)
            low = low - rank(stage) * size
            size = size << len(stage)
        keep(wg_out.at[whole], wg_h.at[whole])

    def start_weights(wave):
        for name, low, size, order in PARTS[wave]:
            chains.add(name, weights_chain(low, size, order))

    finished = len(kept)
    mixed = (att[...] * live).astype(BF)
    hidden_q = hidden_of(jnp.concatenate([xrow[own], xrow[par]], axis=0))
    residual = hidden_q + dot(mixed, wo[...], NN) + line(out_bias_1)
    gain2, shift2 = line(gain_2), line(shift_2)
    hat2, rstd2 = normalise(residual)
    normed2 = (hat2 * gain2 + shift2).astype(BF)
    cotangent = jnp.concatenate([cot2[0], cot2[1]], axis=0)
    unit_result = residual + line(down_bias_1)
    grad_normed2 = jnp.zeros((nq, d), F32)
    sv = sv_acc.at[0]
    for r in range(half // step):
        for k in range(2):
            m = mp if k else 1 - mp
            j = m * (half // step) + r
            units = pl.ds(pl.multiple_of(j * step, step), step)
            inner = dot(normed2, up[:, units], NN) + bias[m, pl.ds(1 + r, 1), :]
            square = inner * inner
            bent = jnp.tanh(GELU_C * inner * (1.0 + GELU_A * square))
            activated = (0.5 * inner * (1.0 + bent)).astype(BF)
            unit_result = unit_result + dot(activated, down[units, :], NN)
            slope = 0.5 * (1.0 + bent) + 0.5 * inner * (1.0 - bent * bent) * (
                GELU_C * (1.0 + 3.0 * GELU_A * square)
            )
            grad_inner = (dot(cotangent, down[units, :], NT) * slope).astype(BF)
            grad_normed2 = grad_normed2 + dot(grad_inner, up[:, units], NT)
            down_grad = dot(activated, cotangent, TN).astype(BF)
            up_grad = dot(normed2, grad_inner, TN).astype(BF)
            for b in range(2):
                at = slice(b * 256, (b + 1) * 256)
                wg[m, pl.ds(2048 * r + b * 512, 512), :] = up_grad[:, at]
                wg[m, pl.ds(2048 * r + 1024 + b * 512, 512), :] = down_grad[:, at]
            sv_acc[0, pl.ds(6 + j, 1), :] = column_sum(grad_inner.astype(F32))
            if r == 1:
                chains.tick()
            if k == 0:
                start_weights("ab"[r])
    out = unit_result.astype(BF)
    result2[0] = out[:BLOCK]
    result2[1] = out[BLOCK:]
    result_back = wire.send(result2.at[1], res_out.at[g], "zh")
    res_out[g] = out[:BLOCK]
    chains.tick()
    cot_f = cotangent.astype(F32)
    grad_residual = cot_f + normalise_back(grad_normed2 * gain2, hat2, rstd2)
    sv[2:3, :] = column_sum(grad_normed2 * hat2)
    sv[3:4, :] = column_sum(grad_normed2)
    sv[4:5, :] = column_sum(grad_residual)
    sv[5:6, :] = column_sum(cot_f)
    branch_grad = grad_residual.astype(BF)
    out_grad = dot(mixed, branch_grad, TN).astype(BF)
    for m in range(2):
        for b in range(2):
            wg[m, pl.ds(OUT_AT + b * 256, 256), :] = out_grad[m * 256 : (m + 1) * 256, b * 256 : (b + 1) * 256]
    start_weights("c")
    chains.tick()
    att[...] = dot(branch_grad, wo[...], NT).astype(BF).astype(F32) * live

    def back(p):
        at = lanes_of(p)
        query = split_heads(q_ref[:, at])
        query_wide = jnp.concatenate([query, other2], axis=1)
        heads = att[:, at]
        grads = split_heads(heads)
        product = jnp.transpose(heads) * att_t[p]
        delta = jnp.concatenate([column_sum(product[:HEAD_DIM]), column_sum(product[HEAD_DIM:])], axis=1)
        log_total = lse[p][0:1, :]
        query_grad = jnp.zeros((PAIR, 2 * nq), F32)
        for c in range(steps):
            keys = k_ref[chunk(c), at]
            scores = dot(jnp.concatenate([keys, hot[chunk(c), :]], axis=1), query_wide, NT)
            probs = jnp.exp(scores - log_total)
            grad_probs = dot(v_ref[chunk(c), at], grads, NT)
            grad_scores = (probs * (grad_probs - delta)).astype(BF)
            dkv[p, chunk(c), 0:PAIR] = dot(grad_scores, query, NN).astype(BF)
            dkv[p, chunk(c), PAIR:] = dot(probs.astype(BF), grads, NN).astype(BF)
            query_grad = query_grad + dot(keys, grad_scores, TN)
            chains.tick()
        joined = join_heads_t(query_grad) * scale
        dq_ref[:, at] = jnp.transpose(joined).astype(BF)

    normed_q = query_rows(normed)
    for n in range(2):
        for m in range(2):
            back(2 * m + n)
        for m in range(2):
            p = 2 * m + n
            pair_grad = dot(normed_t[...], dkv[p], NN)
            wg[m, pl.ds(PAIR_AT[n], d), :] = pair_grad.astype(BF)
            pair_grad = dot(normed_q, dq_ref[:, lanes_of(p)], TN).astype(BF)
            wg[m, pl.ds(PAIR_AT[n] + d, d // 2), 0:PAIR] = pair_grad[: d // 2]
            wg[m, pl.ds(PAIR_AT[n] + d, d // 2), PAIR:] = pair_grad[d // 2 :]
        start_weights("pq"[n])
        chains.tick()

    def tokens_back(grad_normed, block):
        hat, rstd = normalise(hidden_of(block))
        return (
            normalise_back(grad_normed * gain, hat, rstd),
            column_sum(grad_normed * hat),
            column_sum(grad_normed),
        )

    query_grad = dq_ref[...]
    token_grad, gain_sum, shift_sum = tokens_back(
        dot(query_grad, wq[...], NT), jnp.concatenate([xrow[own], xrow[par]], axis=0)
    )
    token_grad = token_grad + grad_residual
    t_buf[own] = token_grad[:BLOCK]
    t_buf[par] = token_grad[BLOCK:]
    token_sum = column_sum(token_grad)
    value_sums = [jnp.zeros((1, PAIR), F32) for _ in range(pairs)]

    def tokens_chain(hi, one, leaves):
        slot = wire.slot()
        copy = wire.send(t_out.at[hi, :, :, 1 - mp], t_core.at[hi], "core", slot)
        yield
        copy.wait_recv()
        for b in range(2):
            for c in range(2):
                t_acc[hi, b, c] = t_out[hi, b, c, mp] + t_core[hi, b, c]
        if one == "y":
            copy = wire.send(t_acc.at[hi, :, 1 - y], t_step.at[hi, 0:2], "y", slot)
        else:
            copy = wire.send(t_acc.at[hi, 1 - zl], t_step.at[hi, 0:2], "zl", slot)
        yield
        copy.wait_recv()
        if one == "y":
            for i in range(2):
                t_acc[hi, i, y] += t_step[hi, i]
            copy = wire.send(t_acc.at[hi, 1 - zl, y], t_step.at[hi, 2], "zl", slot)
        else:
            for i in range(2):
                t_acc[hi, zl, i] += t_step[hi, i]
            copy = wire.send(t_acc.at[hi, zl, 1 - y], t_step.at[hi, 2], "y", slot)
        yield
        copy.wait_recv()
        t_acc[hi, zl, y] += t_step[hi, 2]
        if leaves:
            copy = wire.send(t_acc.at[hi, zl, y], tg_out.at[g], "zh", slot)
            yield
            copy.wait_recv()
        else:
            tg_out[g] = t_acc[hi, zl, y]

    for n, (hi, one) in enumerate(((1 - g, "y"), (g, "y"))):
        for c in range(2):
            place = 2 * hi + c
            at = pl.ds(pl.multiple_of(place * step, step), step)
            grad_normed = jnp.zeros((step, d), F32)
            for p in range(pairs):
                pair_grad = dkv[p, at, :]
                both = jnp.concatenate([wk[:, lanes_of(p)], wv[:, lanes_of(p)]], axis=1)
                grad_normed = grad_normed + dot(pair_grad, both, NT)
                value_sums[p] = value_sums[p] + column_sum(pair_grad[:, PAIR:].astype(F32))
            blocks_at = pl.ds(place * nb, nb)
            token_grad, a, b = tokens_back(grad_normed, xrow[blocks_at].reshape(step, d))
            gain_sum, shift_sum, token_sum = gain_sum + a, shift_sum + b, token_sum + column_sum(token_grad)
            token_grad = t_buf[blocks_at] + token_grad.reshape(nb, BLOCK, d)
            for i in range(nb):
                t_out[hi, c, i // 2, i % 2] = token_grad[i].astype(BF)
            chains.tick()
        chains.add(("t0", "t1")[n], tokens_chain(hi, one, n == 0))
    value_sum = jnp.concatenate(value_sums, axis=1)

    sv[0:1, :] = gain_sum
    sv[1:2, :] = shift_sum
    sv[10:11, :] = column_sum(query_grad.astype(F32))
    sv[11:12, :] = value_sum
    sv[12:16, :] = jnp.zeros((4, d), F32)
    slot_lane = lax.broadcasted_iota(jnp.int32, (1, d), 1)
    speaks = jnp.logical_and(lax.rem(seq, 4) == 0, mp == 0)
    my_slot = 2 * dp + g
    sv[12:13, :] = jnp.where(slot_lane == jnp.where(speaks, my_slot, -1), moment, 0.0)
    slot = lax.broadcasted_iota(jnp.int32, (sv.shape[0] - SV_TABLE, d), 0) == my_slot
    sv[SV_TABLE:, :] = jnp.where(slot, token_sum, 0.0)

    def vectors_chain():
        slots = [wire.slot() for _ in range(3)]
        stages = [("core",)] + stages_of((("x", "y"), ("zl", "zh")))
        for i, stage in enumerate(stages):
            copies = [
                wire.send(sv_acc.at[i], sv_buf.at[i, k], differs, slots[k])
                for k, differs in enumerate(relations(stage))
            ]
            yield
            arrive(copies)
            total = sv_acc[i] + sv_buf[i, 0]
            if len(copies) == 3:
                total = total + (sv_buf[i, 1] + sv_buf[i, 2])
            sv_acc[i + 1] = total
        sv_out[...] = sv_acc[len(stages)]
        result_back.wait_recv()

    chains.add("s", vectors_chain())
    chains.drain()
    wire.finish()
    for copy in kept[finished:]:
        copy.wait()


def layer(big, small, has_x, sv_rows):
    shape = jax.ShapeDtypeStruct
    tokens, up, table = big[0], big[6], big[8]
    d = tokens.shape[2]
    blocks = 2 * lax.axis_size("seq")
    length = blocks * BLOCK
    nq = 2 * BLOCK
    pairs = d // PAIR
    ff = 2 * up.shape[1]
    block = (BLOCK, d)
    vmem = pltpu.VMEM
    return pl.pallas_call(
        functools.partial(layer_kernel, has_x),
        out_shape=(
            shape((WG_ROWS, 256), BF),
            shape((sv_rows, d), F32),
            shape(tokens.shape, BF),
            shape(tokens.shape, BF),
        ),
        in_specs=any_spec(len(big)) + vmem_spec(len(small)),
        out_specs=tuple(any_spec(1) + vmem_spec(3)),
        scratch_shapes=[
            vmem((blocks, BLOCK, d), BF),
            vmem((blocks, SPAN_ROWS, BLOCK), BF),
            vmem(block, BF),
            vmem((SPAN_ROWS, BLOCK), BF),
            vmem(table.shape, BF),
            vmem((2,) + block, BF),
            vmem((d, d), BF),
            vmem((d, d), BF),
            vmem((d, d), BF),
            vmem((d, d), BF),
            vmem((d, ff), BF),
            vmem((ff, d), BF),
            vmem((2, 8, d), F32),
            vmem((length, d), BF),
            vmem((d, length), BF),
            vmem((length, d), BF),
            vmem((length, d), BF),
            vmem((length, BLOCK), BF),
            vmem((5 * nq, 2 * nq), F32),
            vmem((nq, d), F32),
            vmem((pairs, PAIR, nq), F32),
            vmem((pairs, 8, 2 * nq), F32),
            vmem((nq, d), BF),
            vmem((pairs, length, 2 * PAIR), BF),
            vmem((nq, d), BF),
            vmem((blocks,) + block, F32),
            vmem((pairs, 16, 2 * nq), F32),
            vmem((pairs, PAIR, 2 * nq), F32),
            vmem((2, WG_ROWS, 256), BF),
            vmem((WG_ROWS, 256), BF),
            vmem((WG_ROWS, 256), BF),
            vmem((WG_ROWS, 256), BF),
            vmem((WG_ROWS, 256), BF),
            vmem((2, 2, 2, 2) + block, BF),
            vmem((2, 2, 2) + block, BF),
            vmem((2, 2, 2) + block, BF),
            vmem((2, 3) + block, BF),
            vmem((2,) + block, BF),
            vmem((3, 3, sv_rows, d), F32),
            vmem((4, sv_rows, d), F32),
            pltpu.SemaphoreType.DMA((SENDS,)),
            pltpu.SemaphoreType.DMA((RECEIVES,)),
            pltpu.SemaphoreType.DMA((KEEPS,)),
        ],
        compiler_params=pltpu.CompilerParams(
            collective_id=0, has_side_effects=True, vmem_limit_bytes=62 << 20
        ),
        name="layer",
    )(*big, *small)


def finish_kernel(
    table_rows, wg, tg, res, sv,
    res_o, tg_o, table_o, wq_o, wk_o, wv_o, wo_o, up_o, down_o,
    gain_1, shift_1, query_bias, value_bias, out_bias, gain_2, shift_2, up_bias, down_bias,
    wg_v, tg_v, res_v, tg_f, table_v, wq_v, wk_v, wv_v, wo_v, up_v, down_v,
    in_sem, out_sem,
):
    mp = lax.axis_index("mp")
    leaving = []
    rows = 1024
    parts = WG_ROWS // rows

    def fetch(src, dst, n):
        copy = pltpu.make_async_copy(src, dst, in_sem.at[n])
        copy.start()
        return copy

    def leave(src, dst):
        copy = pltpu.make_async_copy(src, dst, out_sem.at[len(leaving)])
        copy.start()
        leaving.append(copy)

    coming_tg, coming_res = fetch(tg, tg_v, parts), fetch(res, res_v, parts + 1)
    coming = [fetch(wg.at[pl.ds(i * rows, rows)], wg_v.at[pl.ds(i * rows, rows)], i) for i in range(parts)]
    ids = sv[12:13, 0:128]
    spread = jnp.where(lax.broadcasted_iota(jnp.int32, (table_v.shape[0], 128), 0).astype(F32) == ids, 1.0, 0.0)
    sums = jnp.concatenate([sv[SV_TABLE:, :], jnp.zeros((128 - (sv.shape[0] - SV_TABLE), sv.shape[1]), F32)], axis=0)
    spread = spread.astype(BF)
    high = sums.astype(BF)
    rest = sums - high.astype(F32)
    middle = rest.astype(BF)
    low = (rest - middle.astype(F32)).astype(BF)
    table_v[...] = dot(spread, high, NN) + (dot(spread, middle, NN) + dot(spread, low, NN))
    leave(table_v, table_o)

    def flat(ref, value):
        ref[...] = value.reshape(ref.shape)

    for ref, r in ((gain_1, 0), (shift_1, 1), (gain_2, 2), (shift_2, 3), (out_bias, 4), (down_bias, 5)):
        flat(ref, sv[r : r + 1, :])
    for ref, r in ((query_bias, 10), (value_bias, 11)):
        flat(ref, jnp.where(mp == 0, sv[r : r + 1, 0:256], sv[r : r + 1, 256:512]))
    flat(up_bias, jnp.where(mp == 0, jnp.concatenate([sv[6:7, :], sv[7:8, :]], axis=1), jnp.concatenate([sv[8:9, :], sv[9:10, :]], axis=1)))

    def take(at, n):
        return wg_v[at : at + n, :].astype(F32)

    coming_res.wait()
    leave(res_v, res_o)
    coming_tg.wait()
    tg_f[...] = tg_v[...].astype(F32)
    leave(tg_f, tg_o)
    for i in range(parts):
        coming[i].wait()
        if i in (0, 2):
            for b in range(2):
                up_v[:, i * 256 + b * 256 : i * 256 + (b + 1) * 256] = take(i * rows + b * 512, 512)
            leave(up_v.at[:, pl.ds(i * 256, 512)], up_o.at[:, pl.ds(i * 256, 512)])
        elif i in (1, 3):
            at = pl.ds(i // 2 * 512, 512)
            for b in range(2):
                down_v[at, b * 256 : (b + 1) * 256] = take(i * rows + b * 512, 512)
            leave(down_v.at[at], down_o.at[at])
        elif i == 4:
            for b in range(2):
                wo_v[:, b * 256 : (b + 1) * 256] = take(OUT_AT + b * 256, 256)
            leave(wo_v, wo_o)
        else:
            for n, at in enumerate(PAIR_AT):
                lanes = slice(n * PAIR, (n + 1) * PAIR)
                both, query = take(at, 512), take(at + 512, 256)
                wk_v[:, lanes] = both[:, :PAIR]
                wv_v[:, lanes] = both[:, PAIR:]
                wq_v[0:256, lanes] = query[:, :PAIR]
                wq_v[256:512, lanes] = query[:, PAIR:]
            leave(wk_v, wk_o)
            leave(wv_v, wv_o)
            leave(wq_v, wq_o)
    for copy in leaving:
        copy.wait()


def finish(wg, tg, res, sv, table_rows, steps, units):
    shape = jax.ShapeDtypeStruct
    d = sv.shape[1]
    big = [
        shape(res.shape, BF), shape(tg.shape, F32), shape((steps, d), F32),
        shape((d, d // 2), F32), shape((d, d // 2), F32), shape((d, d // 2), F32), shape((d // 2, d), F32),
        shape((d, units), F32), shape((units, d), F32),
    ]
    small = [shape((n,), F32) for n in (d, d, d // 2, d // 2, d, d, d, units, d)]
    vmem = pltpu.VMEM
    return pl.pallas_call(
        functools.partial(finish_kernel, table_rows),
        out_shape=tuple(big + small),
        in_specs=any_spec(3) + vmem_spec(1),
        out_specs=tuple(any_spec(len(big)) + vmem_spec(len(small))),
        scratch_shapes=[vmem(wg.shape, BF), vmem(tg.shape, BF), vmem(res.shape, BF), vmem(tg.shape, F32)]
        + [vmem(item.shape, F32) for item in big[2:]]
        + [pltpu.SemaphoreType.DMA((8,)), pltpu.SemaphoreType.DMA((12,))],
        compiler_params=pltpu.CompilerParams(vmem_limit_bytes=62 << 20),
        name="finish",
    )(wg, tg, res, sv)


def local(
    n_dp, tokens, segments, timesteps, step_table, first_gain, first_shift, query_weight, query_bias,
    key_weight, value_weight, value_bias, out_weight, out_bias, second_gain, second_shift,
    up_weight, up_bias, down_weight, down_bias, cotangent,
):
    table_rows = tokens.shape[0] * n_dp
    sv_rows = SV_TABLE + -(-table_rows // 8) * 8
    wg, sv, token_grad, result = layer(
        (tokens, cotangent, query_weight, key_weight, value_weight, out_weight, up_weight, down_weight, step_table),
        (segments, timesteps[None, :], first_gain, first_shift, second_gain, second_shift, out_bias, down_bias,
         query_bias, value_bias, up_bias),
        n_dp == 2, sv_rows,
    )
    if n_dp != 2:
        wg, sv = lax.psum((wg, sv), "dp")
    (result, token_grad, table_grad, wq, wk, wv, wo, up, down,
     gain_1, shift_1, bq, bv, bo, gain_2, shift_2, bu, bd) = finish(
        wg, token_grad, result, sv, table_rows, step_table.shape[0], up_weight.shape[1]
    )
    return (
        result, token_grad, table_grad, gain_1, shift_1, wq, bq, wk, wv, bv, wo, bo, gain_2, shift_2, up, bu, down, bd
    )


def solution(mesh):
    rows, chars, whole = P("dp", ("seq", "mp"), None), P("dp", ("seq", "mp")), P()
    columns, split, tall = P(None, "mp"), P("mp"), P("mp", None)
    in_specs = (
        rows, chars, P("dp"), whole, whole, whole, columns, split, columns, columns, split, tall,
        whole, whole, whole, columns, split, tall, whole, rows,
    )
    out_specs = (
        rows, rows, whole, whole, whole, columns, split, columns, columns, split, tall,
        whole, whole, whole, columns, split, tall, whole,
    )
    return jax.shard_map(
        functools.partial(local, mesh.shape["dp"]),
        mesh=mesh,
        in_specs=in_specs,
        out_specs=out_specs,
        check_vma=False,
    )
```
